32 devices in a mesh: seq: 8 (over z, x), dp: 4 (over y, core).
Axes of the slice: x: 2, y: 2, z: 4, core: 2. Of those that a mesh axis runs over, the one named last changes fastest.
Arguments:
- tokens: bfloat16 [4, 2048, 2048], P('dp', 'seq'), may hold values from -6 to 6
- output_gradient: bfloat16 [4, 2048, 2048], P('dp', 'seq'), may hold values from -6 to 6
- sequence_adapter_index: int32 [4], P('dp'), may hold values from 0 to 7
- time_projection_weights: bfloat16 [4, 2048, 2048], P(None, None, ('seq', 'dp')), may hold values from -0.125 to 0.125
- branch_first_weights: bfloat16 [2048, 448], P(('seq', 'dp')), may hold values from -0.125 to 0.125
- branch_second_weights: bfloat16 [448, 2048], P(None, ('seq', 'dp')), may hold values from -0.375 to 0.375
- vectors: bfloat16 [18, 2048], P(None, ('seq', 'dp')), may hold values from -7.5 to 1.5
- channel_key_weight: bfloat16 [2048, 8192], P(None, ('seq', 'dp')), may hold values from -0.125 to 0.125
- channel_value_weight: bfloat16 [8192, 2048], P(('seq', 'dp')), may hold values from -0.0625 to 0.0625
- model_adapter_rows: bfloat16 [8, 160, 2048], P(None, None, ('seq', 'dp')), may hold values from -0.125 to 0.125
- hidden_adapter_rows: bfloat16 [8, 32, 8192], P(None, None, ('seq', 'dp')), may hold values from -0.0625 to 0.0625
Outputs:
- out: bfloat16 [4, 2048, 2048], P('dp', 'seq')
- grad_tokens: float32 [4, 2048, 2048], P('dp', 'seq')
- grad_adapter_model: float32 [8, 160, 2048], P(None, None, ('seq', 'dp'))
- grad_adapter_hidden: float32 [8, 32, 8192], P(None, None, ('seq', 'dp'))
The draws below stay inside these ranges and needn't reach their ends.
All inputs are finite; a program needn't handle non-finite values.
Results may differ from the reference program's by a relative error of at most 0.012.
The reference program's roundings to bfloat16 on the way count: a program that leaves them out, or rounds other values in their place, can miss the bound.
Values may be sent and summed in bfloat16 or wider, within the bound.
A program may use at most 640 MiB of HBM per device.

```python
import jax
import jax.numpy as jnp
import numpy as np
from jax import lax

MODEL_WIDTH = 2048
ATTENTION_COUNT = 32
ATTENTION_DIM = 64
FF = 8192
DECAY_INNER = 96
RATE_INNER = 96
GATE_INNER = 256
RANK = 16
ADAPTERS = 8
NVEC = 18
LEN = 2048
SEQS = 4
BRANCH_INNER_ALL = 448


row_kinds_table = np.array([0, 1, 2, 2, 2, 2, 2, 2, 3, 4, 0, 0, 4, 0, 1, 0, 1, 2])


def draw_vectors(key, part):
    key_one, key_two, key_three = jax.random.split(key, 3)
    uniform_raw = jax.random.uniform(key_one, (NVEC, MODEL_WIDTH), jnp.float32)
    signed = 2.0 * uniform_raw - 1.0
    head_level = jax.random.uniform(key_two, (ATTENTION_COUNT, 1), jnp.float32)
    jitter = jax.random.uniform(key_three, (ATTENTION_COUNT, ATTENTION_DIM), jnp.float32) - 0.5
    decay_row = (-7.0 + 5.0 * head_level + jitter).reshape(1, MODEL_WIDTH)
    row_kind = jnp.asarray(row_kinds_table)[:, None]
    values = jnp.where(row_kind == 0, 1.0 + 0.5 * signed, jnp.where(row_kind == 1, 0.5 * signed, jnp.where(row_kind == 2, uniform_raw, jnp.where(row_kind == 3, decay_row, signed))))
    return values.astype(jnp.bfloat16)


def place_ends(values, own_key, least, top_value):
    longest = values.shape.index(max(values.shape))
    spots = []
    for shift in (0, 1):
        where = [jax.random.randint(jax.random.fold_in(own_key, axis), (), 0, length) for axis, length in enumerate(values.shape)]
        where[longest] = (where[longest] + shift) % values.shape[longest]
        spots.append(tuple(where))
    return values.at[spots[0]].set(least).at[spots[1]].set(top_value)


def steps_of(own_key, dims, cuts, least, top_value):
    factor_of, own = 1.0, jax.random.fold_in(own_key, 6)
    for axis_at, blocks in cuts:
        heights = jnp.exp(jax.random.uniform(jax.random.fold_in(own, axis_at), (blocks,), jnp.float32, least / len(cuts), top_value / len(cuts)))
        factor_of = factor_of * jnp.repeat(heights, dims[axis_at] // blocks).reshape([-1 if axis == axis_at else 1 for axis in range(len(dims))])
    return factor_of


def bell_draw(rng, dims, width, reach, cuts=(), kind=jnp.bfloat16):
    entries = jax.random.normal(rng, dims, jnp.float32) * width
    if len(cuts) > 0:
        entries = steps_of(rng, dims, cuts, -0.22, 0.18) * entries
    return jnp.clip(entries, min=-reach, max=reach).astype(kind)


def setup_inputs(seed: int = 0) -> dict:
    arg_keys = jax.random.split(jax.random.key(seed), 12)
    return {
        "tokens": bell_draw(arg_keys[0], (SEQS, LEN, MODEL_WIDTH), 1.0, 6.0, ((0, 4), (1, 8))),
        "output_gradient": bell_draw(arg_keys[1], (SEQS, LEN, MODEL_WIDTH), 1.0, 6.0, ((0, 4), (1, 8))),
        "sequence_adapter_index": place_ends(jax.random.randint(arg_keys[2], (SEQS,), 0, ADAPTERS), jax.random.fold_in(arg_keys[2], 1), 0, ADAPTERS - 1).astype(jnp.int32),
        "time_projection_weights": bell_draw(arg_keys[3], (4, MODEL_WIDTH, MODEL_WIDTH), MODEL_WIDTH ** -0.5, 0.125, ((2, 32),)),
        "branch_first_weights": bell_draw(arg_keys[4], (MODEL_WIDTH, BRANCH_INNER_ALL), MODEL_WIDTH ** -0.5, 0.125, ((0, 32),)),
        "branch_second_weights": bell_draw(arg_keys[5], (BRANCH_INNER_ALL, MODEL_WIDTH), GATE_INNER ** -0.5, 0.375, ((1, 32),)),
        "vectors": draw_vectors(jax.random.fold_in(arg_keys[11], 71), 0),
        "channel_key_weight": bell_draw(arg_keys[7], (MODEL_WIDTH, FF), MODEL_WIDTH ** -0.5, 0.125, ((1, 32),)),
        "channel_value_weight": bell_draw(arg_keys[8], (FF, MODEL_WIDTH), FF ** -0.5, 0.0625, ((0, 32),)),
        "model_adapter_rows": bell_draw(arg_keys[9], (ADAPTERS, 10 * RANK, MODEL_WIDTH), MODEL_WIDTH ** -0.5, 0.125, ((2, 32),)),
        "hidden_adapter_rows": bell_draw(arg_keys[10], (ADAPTERS, 2 * RANK, FF), FF ** -0.5, 0.0625, ((2, 32),)),
    }


PRECISE = lax.Precision.HIGHEST
ADAPT_SCALE = 4.0
NORM_EPS = 1e-05
GROUP_EPS = 0.00064
UNIT_EPS = 1e-06

@jax.custom_vjp
def low(v):
    return lax.optimization_barrier(v.astype(jnp.bfloat16)).astype(jnp.float32)

@jax.custom_vjp
def low_back(v):
    return v

def low_keep(v):
    return (low(v), None)

def low_pass(kept, grad):
    return (grad,)

def back_keep(v):
    return (v, None)

def back_low(kept, grad):
    return (low(grad),)
low.defvjp(low_keep, low_pass)
low_back.defvjp(back_keep, back_low)

def matrix_product(left, right):
    return jnp.dot(left, right, precision=PRECISE, preferred_element_type=jnp.float32)

def layer_norm(values, gain_row, shift_row):
    centre = values - lax.optimization_barrier(jnp.mean(values, axis=-1, keepdims=True))
    spread = lax.optimization_barrier(jnp.mean(centre * centre, axis=-1, keepdims=True))
    return centre * lax.rsqrt(spread + NORM_EPS) * gain_row + shift_row

def previous(values):
    return jnp.concatenate([jnp.zeros_like(values[:1]), values[:-1]], axis=0)

def adapted(inputs, weight, down_rows, up_rows):
    hidden = low(low_back(matrix_product(inputs, down_rows.T)))
    return low_back(matrix_product(inputs, weight) + ADAPT_SCALE * matrix_product(hidden, up_rows))

def split_attention_blocks(values):
    return values.reshape(values.shape[0], ATTENTION_COUNT, ATTENTION_DIM)

def recurrence(acceptance_entries, decays, unit_key, context_rate, adjusted_lookup_entries, values):
    stream_extent = acceptance_entries.shape[0]
    block_len = 64 if stream_extent % 64 == 0 else stream_extent

    def one_token(carried, inputs):
        recv_t, decay_t, unit_t, rate_t, key_t, value_t = inputs
        pulled = jnp.einsum('hvk,hk->hv', carried, -unit_t, precision=PRECISE)
        carried = carried * decay_t[:, None, :] + pulled[:, :, None] * (unit_t * rate_t)[:, None, :] + value_t[:, :, None] * key_t[:, None, :]
        return (carried, jnp.einsum('hvk,hk->hv', carried, recv_t, precision=PRECISE))

    def one_block(carried, inputs):
        return lax.scan(one_token, carried, inputs)
    stacked = tuple((member.reshape(stream_extent // block_len, block_len, ATTENTION_COUNT, ATTENTION_DIM) for member in (acceptance_entries, decays, unit_key, context_rate, adjusted_lookup_entries, values)))
    initial = jnp.zeros((ATTENTION_COUNT, ATTENTION_DIM, ATTENTION_DIM), jnp.float32)
    _, outputs = lax.scan(jax.checkpoint(one_block), initial, stacked)
    return outputs.reshape(stream_extent, ATTENTION_COUNT, ATTENTION_DIM)

def layer_forward_pass(tokens, model_adapter_delta, hidden_adapter_delta, select_adapter, weight_matrices, branch_down_project, branch_up_project, stacked_parameter_lines, channel_key, channel_value):
    chosen = model_adapter_delta[select_adapter]
    chosen_hidden = hidden_adapter_delta[select_adapter]
    stream_extent = tokens.shape[0]
    normed = layer_norm(tokens, stacked_parameter_lines[0], stacked_parameter_lines[1])
    change = previous(normed) - normed
    mix_r, decay_mix_weight, mix_k, mix_v, rate_mix_weight, gate_mix_weight = (low(normed + change * stacked_parameter_lines[2 + number]) for number in range(6))
    acceptance_entries = adapted(mix_r, weight_matrices[0], chosen[0:RANK], chosen[5 * RANK:6 * RANK])
    unscaled_keys = adapted(mix_k, weight_matrices[1], chosen[RANK:2 * RANK], chosen[6 * RANK:7 * RANK])
    raw_payload_entries = adapted(mix_v, weight_matrices[2], chosen[2 * RANK:3 * RANK], chosen[7 * RANK:8 * RANK])
    rate_first_matrix = DECAY_INNER
    gate_first_matrix = DECAY_INNER + RATE_INNER
    decay_preactivation = low_back(matrix_product(decay_mix_weight, branch_down_project[:, :rate_first_matrix]))
    decay_branch = low_back(matrix_product(low(jnp.tanh(decay_preactivation)), branch_up_project[:rate_first_matrix]))
    rate_preactivation = low(low_back(matrix_product(rate_mix_weight, branch_down_project[:, rate_first_matrix:gate_first_matrix])))
    rate_branch = low_back(matrix_product(rate_preactivation, branch_up_project[rate_first_matrix:gate_first_matrix]))
    gate_preactivation = low_back(matrix_product(gate_mix_weight, branch_down_project[:, gate_first_matrix:]))
    sigmoid_filter_entries = low_back(matrix_product(low(jax.nn.sigmoid(gate_preactivation)), branch_up_project[gate_first_matrix:]))
    logarithm_rate = -jax.nn.softplus(-(stacked_parameter_lines[8] + decay_branch)) - 0.5
    decays = jnp.exp(-jnp.exp(logarithm_rate))
    context_rate = jax.nn.sigmoid(stacked_parameter_lines[9] + rate_branch)
    unit_key = split_attention_blocks(unscaled_keys * stacked_parameter_lines[10])
    unit_key = unit_key * lax.rsqrt(lax.optimization_barrier(jnp.sum(unit_key * unit_key, axis=-1, keepdims=True)) + UNIT_EPS)
    adjusted_lookup_entries = unscaled_keys * (1.0 + (context_rate - 1.0) * stacked_parameter_lines[11])
    mixed_out = recurrence(split_attention_blocks(acceptance_entries), split_attention_blocks(decays), unit_key, split_attention_blocks(context_rate), split_attention_blocks(adjusted_lookup_entries), split_attention_blocks(raw_payload_entries))
    centre = mixed_out - lax.optimization_barrier(jnp.mean(mixed_out, axis=-1, keepdims=True))
    spread = lax.optimization_barrier(jnp.mean(centre * centre, axis=-1, keepdims=True))
    groupwise_standardized = centre * lax.rsqrt(spread + GROUP_EPS) * stacked_parameter_lines[13].reshape(ATTENTION_COUNT, ATTENTION_DIM) + stacked_parameter_lines[14].reshape(ATTENTION_COUNT, ATTENTION_DIM)
    diagonal_reward_addend = lax.optimization_barrier(jnp.sum(split_attention_blocks(acceptance_entries) * split_attention_blocks(adjusted_lookup_entries) * stacked_parameter_lines[12].reshape(ATTENTION_COUNT, ATTENTION_DIM), axis=-1, keepdims=True)) * split_attention_blocks(raw_payload_entries)
    filtered_result_entries = low((groupwise_standardized + diagonal_reward_addend).reshape(stream_extent, ATTENTION_COUNT * ATTENTION_DIM) * sigmoid_filter_entries)
    attended = adapted(filtered_result_entries, weight_matrices[3], chosen[3 * RANK:4 * RANK], chosen[8 * RANK:9 * RANK])
    middle = tokens + attended
    normed_two = layer_norm(middle, stacked_parameter_lines[15], stacked_parameter_lines[16])
    chan_mix = low(normed_two + (previous(normed_two) - normed_two) * stacked_parameter_lines[17])
    pre_act = adapted(chan_mix, channel_key, chosen[4 * RANK:5 * RANK], chosen_hidden[RANK:2 * RANK])
    squared = low(jnp.square(jax.nn.relu(pre_act)))
    chan_out = adapted(squared, channel_value, chosen_hidden[0:RANK], chosen[9 * RANK:10 * RANK])
    return middle + chan_out

def reference(tokens, output_gradient, sequence_adapter_index, time_projection_weights, branch_first_weights, branch_second_weights, vectors, channel_key_weight, channel_value_weight, model_adapter_rows, hidden_adapter_rows):
    weight_matrices = time_projection_weights.astype(jnp.float32)
    branch_down_project = branch_first_weights.astype(jnp.float32)
    branch_up_project = branch_second_weights.astype(jnp.float32)
    stacked_parameter_lines = vectors.astype(jnp.float32)
    channel_key = channel_key_weight.astype(jnp.float32)
    channel_value = channel_value_weight.astype(jnp.float32)
    model_adapter_delta = model_adapter_rows.astype(jnp.float32)
    hidden_adapter_delta = hidden_adapter_rows.astype(jnp.float32)

    def per_sequence(totals, inputs):
        seq_tokens, seq_grad, sequence_select = inputs

        def forward_of(token_values, model_values, hidden_values):
            return layer_forward_pass(token_values, model_values, hidden_values, sequence_select.astype(jnp.int32), weight_matrices, branch_down_project, branch_up_project, stacked_parameter_lines, channel_key, channel_value)
        result, pull_back = jax.vjp(forward_of, seq_tokens.astype(jnp.float32), model_adapter_delta, hidden_adapter_delta)
        grad_x, grad_model, grad_hidden = pull_back(seq_grad.astype(jnp.float32))
        return ((totals[0] + grad_model, totals[1] + grad_hidden), (result.astype(jnp.bfloat16), grad_x))
    initial = (jnp.zeros_like(model_adapter_delta), jnp.zeros_like(hidden_adapter_delta))
    (sum_model, sum_hidden), (results, grads) = lax.scan(per_sequence, initial, (tokens, output_gradient, sequence_adapter_index))
    return (results, grads, sum_model, sum_hidden)
```

```python
import functools
import math

import jax
import jax.numpy as jnp
from jax import lax
from jax.experimental import pallas as pl
from jax.experimental.pallas import tpu as pltpu
from jax.sharding import PartitionSpec as P

F32, BF = jnp.float32, jnp.bfloat16
MESH = pl.DeviceIdType.MESH
D = 64
C = 64
PW = 2 * D
DECAY_INNER, RATE_INNER, RANK = 96, 96, 16
SCALE = 4.0
NORM_EPS, GROUP_EPS, UNIT_EPS = 1e-05, 0.00064, 1e-06
DECAY_SCALE = math.exp(-0.5)
PRECISE = lax.Precision.HIGHEST
DIMS = {
    "nn": (((1,), (0,)), ((), ())),
    "nt": (((1,), (1,)), ((), ())),
    "tn": (((0,), (0,)), ((), ())),
}


def split(x):
    hi = x.astype(BF)
    return hi, (x - hi.astype(F32)).astype(BF)


def dot1(a, b, m="nn"):
    return lax.dot_general(a.astype(BF), b.astype(BF), DIMS[m], preferred_element_type=F32)


def dot3(a, b, m="nn"):
    ah, al = split(a)
    bh, bl = split(b)
    ka, kb = (0 if m == "tn" else 1), (1 if m == "nt" else 0)
    n = b.shape[1 - kb]
    aa = jnp.concatenate([ah, al], axis=ka)
    bb = jnp.concatenate([jnp.concatenate([bh, bl], axis=1 - kb)] * 2, axis=kb)
    r = lax.dot_general(aa, bb, DIMS[m], preferred_element_type=F32)
    return r[:, :n] + r[:, n:]


def iota(shape, axis):
    return lax.broadcasted_iota(jnp.int32, shape, axis)


def stack2(x):
    lane = iota(x.shape, 1)
    zero = jnp.zeros_like(x)
    return jnp.concatenate([jnp.where(lane < D, x, zero), jnp.where(lane < D, zero, x)], axis=0)


def pack2(x):
    h = x.shape[0] // 2
    return x[:h] + x[h:]


def head_ones():
    r, c = iota((2 * PW, PW), 0) % PW, iota((2 * PW, PW), 1)
    return jnp.where((r // D) == (c // D), 1.0, 0.0).astype(BF)


def headsum(x, ones):
    h, l = split(x)
    return lax.dot_general(
        jnp.concatenate([h, l], axis=1), ones, DIMS["nn"], preferred_element_type=F32
    )


def triangle(upper):
    r, c = iota((C, C), 0), iota((C, C), 1)
    return jnp.where((r <= c) if upper else (r >= c), 1.0, 0.0).astype(BF)


def cums(x, tri):
    h, l = split(x)
    m = (x - h.astype(F32) - l.astype(F32)).astype(BF)
    n = x.shape[1]
    r = lax.dot_general(
        tri, jnp.concatenate([h, l, m], axis=1), DIMS["nn"], preferred_element_type=F32
    )
    return r[:, :n] + r[:, n : 2 * n] + r[:, 2 * n :]


def prelude(kr, wl, al, w0, a0, k_k, k_a, ones):
    s = jax.nn.sigmoid(w0 + wl)
    a = jax.nn.sigmoid(a0 + al)
    kx = kr * k_k
    rn = lax.rsqrt(headsum(kx * kx, ones) + UNIT_EPS)
    return s, -DECAY_SCALE * s, a, rn, kx * rn, kr * (1.0 + (a - 1.0) * k_a)


def grid_ids():
    r, c = iota((PW, PW), 0), iota((PW, PW), 1)
    return r, c, (r // D) == (c // D)


def inverse(a):
    r, c, _ = grid_ids()
    x = jnp.where(r == c, 1.0, 0.0)
    b = 1
    while b < C:
        level = ((r // (2 * b)) == (c // (2 * b))) & ((r // b) % 2 == 1) & ((c // b) % 2 == 0)
        am = jnp.where(level, a, 0.0)
        x = x + am if b == 1 else x + dot3(dot3(x, am), x)
        b *= 2
    return x


def factors(logw, tri):
    run = cums(logw, tri)
    return jnp.exp(run - logw), jnp.exp(run), jnp.exp(-run), jnp.exp(run[C - 1 : C])


def forward_chunk(r, p, q, k, v, logw, tri):
    eb, el, en, last = factors(logw, tri)
    p2, r2, q2, k2, v2 = (
        stack2(p * eb), stack2(r * el), stack2(q * en), stack2(k * en), stack2(v)
    )
    rows, cols, same = grid_ids()
    zero = jnp.zeros((PW, PW), F32)
    strict, incl = (rows > cols) & same, (rows >= cols) & same
    aa = dot3(jnp.concatenate([p2, r2], 0), jnp.concatenate([q2, k2], 0), "nt")
    apq, apk = jnp.where(strict, aa[:PW, :PW], zero), jnp.where(strict, aa[:PW, PW:], zero)
    arq, ark = jnp.where(incl, aa[PW:, :PW], zero), jnp.where(incl, aa[PW:, PW:], zero)
    x = inverse(apq)
    ww = dot3(x, jnp.concatenate([p2, dot3(apk, v2)], 1))
    left = jnp.concatenate(
        [
            jnp.concatenate([arq, ark], 1),
            jnp.concatenate([(q2 * last).T, (k2 * last).T], 1),
        ],
        0,
    )
    right = jnp.concatenate([ww, jnp.concatenate([zero, v2], 1)], 0)
    big = dot3(left, right)
    move = big[PW:, :PW] + jnp.where(rows == cols, jnp.broadcast_to(last, (PW, PW)), zero)
    return (
        pack2(r2 + big[:PW, :PW]),
        pack2(big[:PW, PW:]),
        move,
        big[PW:, PW:],
        pack2(ww[:, :PW]),
        pack2(ww[:, PW:]),
        x,
    )


def backward_chunk(r, p, q, k, v, logw, tri, tri_up, x, u, z0, h, g):
    eb, el, en, last = factors(logw, tri)
    pe, re, qe, ke = p * eb, r * el, q * en, k * en
    qh, kh = qe * last, ke * last
    g2 = stack2(g)
    rows, cols, same = grid_ids()
    zero = jnp.zeros((PW, PW), F32)
    strict, incl = (rows < cols) & same, (rows <= cols) & same
    qk = jnp.concatenate([stack2(qe), stack2(ke)], 0)
    pr = jnp.concatenate([stack2(pe), stack2(re)], 0)
    at = dot3(qk, pr, "nt")
    arq, apk, ark = (
        jnp.where(incl, at[:PW, PW:], zero),
        jnp.where(strict, at[PW:, :PW], zero),
        jnp.where(incl, at[PW:, PW:], zero),
    )
    qkh = dot3(jnp.concatenate([qh, kh], 0), h)
    du = dot3(arq, g2) + stack2(qkh[:C])
    dm = dot3(x, du, "tn")
    dg = jnp.concatenate([dm, g2], 0)
    dv = pack2(dot3(jnp.concatenate([apk, ark], 1), dg)) + qkh[C:]
    dat = dot3(jnp.concatenate([stack2(u), stack2(v)], 0), dg, "nt")
    both = jnp.concatenate([jnp.concatenate([strict, incl], 1)] * 2, 0)
    dat = jnp.where(both, dat, jnp.zeros_like(dat))
    dpr = dot3(dat, qk, "tn")
    sp = dot3(jnp.concatenate([pack2(dm), g], 0), z0, "nt")
    dp, dr = pack2(dpr[:PW]) + sp[:C], pack2(dpr[PW:]) + sp[C:]
    dqk = dot3(dat, pr)
    sq = dot3(jnp.concatenate([u, v], 0), h, "nt")
    dqh, dkh = sq[:C], sq[C:]
    dq, dk = pack2(dqk[:PW]) + dqh * last, pack2(dqk[PW:]) + dkh * last
    tail = jnp.sum(qh * dqh + kh * dkh, axis=0, keepdims=True)
    tail = tail + last * jnp.sum((z0 * h).T, axis=0, keepdims=True)
    gb = pe * dp
    gl = re * dr - qe * dq - ke * dk
    dlogw = cums(gl + gb, tri_up) - gb + tail
    return dr * el, dp * eb, dq * en, dk * en, dv, dlogw


def rec_local(nc, rr, kr, vr, wl, al, vec, reff, oloc, w1, w2, xs, mv, mt, piece):
    ones, tri = head_ones(), triangle(False)
    row = lambda i: vec[i : i + 1, :]
    _, logw, a, _, kk, km = prelude(
        kr[...], wl[...], al[...], row(8), row(9), row(10), row(11), ones
    )
    r, v = rr[...], vr[...]
    q = kk * a
    moves, adds = [], []
    for c in range(nc):
        s = slice(c * C, (c + 1) * C)
        e, o, m, n, y1, y2, x = forward_chunk(r[s], -kk[s], q[s], km[s], v[s], logw[s], tri)
        reff[s, :], oloc[s, :], w1[s, :], w2[s, :] = e, o, y1, y2
        xs[s, :] = pack2(x)
        mp = pack2(m)
        mv[0, s, :], mv[1, s, :], mt[s, :] = mp, pack2(n), pack2(m.T)
        moves.append(mp)
        adds.append(n)
    total = None
    for c in range(nc):
        if c == 0:
            tm, tn = stack2(moves[0]), adds[0]
        else:
            t = dot3(moves[c], jnp.concatenate([tm, tn], 1))
            tm, tn = stack2(t[:, :PW]), stack2(t[:, PW:]) + adds[c]
    piece[0], piece[1], piece[2] = pack2(tm), pack2(tn), pack2(tm.T)


def norm_parts(o, ones):
    centre = o - headsum(o, ones) * (1.0 / D)
    rstd = lax.rsqrt(headsum(centre * centre, ones) * (1.0 / D) + GROUP_EPS)
    return centre * rstd, rstd


def rec_out(nc, zin, rr, kr, vr, al, gg, vec, reff, oloc, w1, w2, mv, z_out, o_out, u_out, zs):
    ones = head_ones()
    row = lambda i: vec[i : i + 1, :]
    state = zin[...]
    for c in range(nc):
        s = slice(c * C, (c + 1) * C)
        zs[s, :] = state
        big = stack2(state)
        t = dot3(jnp.concatenate([reff[s, :], w1[s, :], mv[0, s, :]], 0), big)
        o_out[s, :] = t[:C] + oloc[s, :]
        u_out[s, :] = t[C : 2 * C] + w2[s, :]
        state = t[2 * C :] + mv[1, s, :]
    a = jax.nn.sigmoid(row(9) + al[...])
    km = kr[...] * (1.0 + (a - 1.0) * row(11))
    hat, _ = norm_parts(o_out[...], ones)
    y = hat * row(13) + row(14) + headsum(rr[...] * km * row(12), ones) * vr[...]
    z_out[...] = (y * gg[...]).astype(BF)


def back_local(nc, dz, gg, o, rr, kr, vr, al, vec, reff, mt, do, dgg, es, piece):
    ones = head_ones()
    row = lambda i: vec[i : i + 1, :]
    a = jax.nn.sigmoid(row(9) + al[...])
    km = kr[...] * (1.0 + (a - 1.0) * row(11))
    hat, rstd = norm_parts(o[...], ones)
    y = hat * row(13) + row(14) + headsum(rr[...] * km * row(12), ones) * vr[...]
    dgg[...] = (dz[...] * y).astype(BF)
    dhat = dz[...] * gg[...] * row(13)
    d_o = rstd * (
        dhat
        - headsum(dhat, ones) * (1.0 / D)
        - hat * (headsum(dhat * hat, ones) * (1.0 / D))
    )
    do[...] = d_o
    _, _, same = grid_ids()
    state = None
    for c in reversed(range(nc)):
        s = slice(c * C, (c + 1) * C)
        e = pack2(jnp.where(same, dot3(reff[s, :], d_o[s], "tn"), 0.0))
        es[s, :] = e
        state = e if state is None else e + dot3(mt[s, :], stack2(state))
    piece[...] = state


def rec_back(
    nc, hin, dz, gg, do, rr, kr, vr, wl, al, vec, xs, us, zs, mt, es, drr, dkr, dvr, dwl, dal
):
    ones, tri, tri_up = head_ones(), triangle(False), triangle(True)
    row = lambda i: vec[i : i + 1, :]
    h = hin[...]
    for c in reversed(range(nc)):
        s = slice(c * C, (c + 1) * C)
        r, v, k = rr[s, :], vr[s, :], kr[s, :]
        sg, logw, a, rn, kk, km = prelude(
            k, wl[s, :], al[s, :], row(8), row(9), row(10), row(11), ones
        )
        big = stack2(h)
        dr, dp, dq, dk, dv, dlogw = backward_chunk(
            r, -kk, kk * a, km, v, logw, tri, tri_up,
            stack2(xs[s, :]), us[s, :], stack2(zs[s, :]), big, do[s, :],
        )
        if c:
            h = dot3(mt[s, :], big) + es[s, :]
        dy = dz[s, :] * gg[s, :]
        dv = dv + headsum(r * km * row(12), ones) * dy
        ds = headsum(dy * v, ones) * row(12)
        dr = dr + ds * km
        dkm = dk + ds * r
        dkk = dq * a - dp
        da = dq * kk + dkm * k * row(11)
        dk = dkm * (1.0 + (a - 1.0) * row(11)) + row(10) * rn * (dkk - kk * headsum(dkk * kk, ones))
        drr[s, :], dkr[s, :], dvr[s, :] = dr.astype(BF), dk.astype(BF), dv.astype(BF)
        dwl[s, :] = (dlogw * (-DECAY_SCALE) * sg * (1.0 - sg)).astype(BF)
        dal[s, :] = (da * a * (1.0 - a)).astype(BF)


def over_pairs(body, pairs, ins, outs, name):
    def spec(shape):
        lead = tuple(shape[:-1])
        return pl.BlockSpec(lead + (PW,), lambda i, n=len(lead): (0,) * n + (i,))

    return pl.pallas_call(
        body,
        grid=(pairs,),
        in_specs=[spec(x.shape) for x in ins],
        out_specs=[spec(x.shape) for x in outs],
        out_shape=outs,
        compiler_params=pltpu.CompilerParams(vmem_limit_bytes=48 * 1024 * 1024),
        name=name,
    )(*ins)


def pass_kernel(n, groups, back, move, add, out, here, send, send_sem, recv_sem):
    s, d = lax.axis_index("seq"), lax.axis_index("dp")
    if back:
        first, final, nxt, prv = s == n - 1, s == 0, s - 1, s + 1
    else:
        first, final, nxt, prv = s == 0, s == n - 1, s + 1, s - 1
    barrier = pltpu.get_barrier_semaphore()

    @pl.when(jnp.logical_not(first))
    def _():
        pl.semaphore_signal(barrier, inc=1, device_id=(prv, d), device_id_type=MESH)

    @pl.when(jnp.logical_not(final))
    def _():
        pl.semaphore_wait(barrier, 1)

    def copy(g, to):
        return pltpu.make_async_remote_copy(
            src_ref=send.at[g],
            dst_ref=here.at[g],
            send_sem=send_sem.at[g],
            recv_sem=recv_sem.at[g],
            device_id=(to, d),
            device_id_type=MESH,
        )

    per = out.shape[1] // (groups * PW)
    for g in range(groups):

        @pl.when(first)
        def _():
            here[g] = jnp.zeros(here.shape[1:], F32)

        @pl.when(jnp.logical_not(first))
        def _():
            copy(g, prv).wait_recv()

        out[:, g * per * PW : (g + 1) * per * PW] = here[g]

        @pl.when(jnp.logical_not(final))
        def _():
            for i in range(per):
                at = (g * per + i) * PW
                state = stack2(here[g, :, i * PW : (i + 1) * PW])
                send[g, :, i * PW : (i + 1) * PW] = (
                    dot3(move[:, at : at + PW], state) + add[:, at : at + PW]
                )
            copy(g, nxt).start()

    @pl.when(jnp.logical_not(final))
    def _():
        for g in range(groups):
            copy(g, nxt).wait_send()


def pass_states(n, move, add, back):
    rows, width = move.shape
    groups = 4 if width % (4 * PW) == 0 else 1
    return pl.pallas_call(
        functools.partial(pass_kernel, n, groups, back),
        out_shape=jax.ShapeDtypeStruct((rows, width), F32),
        in_specs=[pl.BlockSpec(memory_space=pltpu.VMEM)] * 2,
        out_specs=pl.BlockSpec(memory_space=pltpu.VMEM),
        scratch_shapes=[
            pltpu.VMEM((groups, rows, width // groups), F32),
            pltpu.VMEM((groups, rows, width // groups), F32),
            pltpu.SemaphoreType.DMA((groups,)),
            pltpu.SemaphoreType.DMA((groups,)),
        ],
        compiler_params=pltpu.CompilerParams(
            collective_id=1 if back else 0, has_side_effects=True
        ),
        name="pass_back" if back else "pass_on",
    )(move, add)


def shifted(block, axis, distance):
    devices = range(lax.axis_size(axis))
    route = [(i - distance, i) for i in devices if i - distance in devices]
    return lax.ppermute(block, axis, route)


def layer_norm(values, gain, shift):
    centre = values - jnp.mean(values, axis=-1, keepdims=True)
    spread = jnp.mean(centre * centre, axis=-1, keepdims=True)
    return centre * lax.rsqrt(spread + NORM_EPS) * gain + shift


def mm(a, b):
    return lax.dot_general(a, b, DIMS["nn"], preferred_element_type=F32)


def mm_nt(a, b):
    return lax.dot_general(a, b, DIMS["nt"], preferred_element_type=F32)


def mm_tn(a, b):
    return lax.dot_general(a, b, DIMS["tn"], preferred_element_type=F32)


def adapted(x, weight, down, up):
    hidden = mm_nt(x, down).astype(BF)
    return mm(x, weight) + SCALE * mm(hidden, up), hidden


def adapted_back(gradient, x, weight, down, up, hidden):
    low = gradient.astype(BF)
    grad_up = SCALE * mm_tn(hidden, low)
    grad_hidden = (SCALE * mm_nt(low, up)).astype(BF)
    return mm_nt(low, weight) + mm(grad_hidden, down), mm_tn(grad_hidden, x), grad_up


def previous(values, edge):
    return jnp.concatenate([edge, values[:-1]], axis=0)


def following(values, edge):
    return jnp.concatenate([values[1:], edge], axis=0)


def body(tokens, output_gradient, index, proj, first, second, vectors, ckey, cvalue, model_rows, hidden_rows):
    axes = ("seq", "dp")
    n_seq = lax.axis_size("seq")
    tokens, output_gradient = tokens[0], output_gradient[0]
    length, width = tokens.shape
    pairs, nc = width // PW, length // C
    lo, hi = DECAY_INNER, DECAY_INNER + RATE_INNER
    vec = lax.all_gather(vectors, axes, axis=1, tiled=True).astype(F32)
    second_all = lax.all_gather(second, axes, axis=1, tiled=True)
    first_all = lax.all_gather(first, axes, axis=0, tiled=True)
    model_all = lax.all_gather(model_rows, axes, axis=2, tiled=True)
    mats = lax.all_gather(proj, axes, axis=2, tiled=True)
    hidden_all = lax.all_gather(hidden_rows, axes, axis=2, tiled=True)
    key_all = lax.all_gather(ckey, axes, axis=1, tiled=True)
    value_all = lax.all_gather(cvalue, axes, axis=0, tiled=True)
    pick = index[0] == jnp.arange(model_all.shape[0], dtype=jnp.int32)
    chosen = jnp.einsum("a,arx->rx", pick.astype(BF), model_all, preferred_element_type=F32).astype(BF)
    chosen_hidden = jnp.einsum("a,arx->rx", pick.astype(BF), hidden_all, preferred_element_type=F32).astype(BF)
    down = lambda i: chosen[i * RANK : (i + 1) * RANK]
    up = lambda i: chosen[(5 + i) * RANK : (6 + i) * RANK]

    wide = tokens.astype(F32)
    normed, norm_pull = jax.vjp(lambda t: layer_norm(t, vec[0:1], vec[1:2]), wide)
    change = previous(normed, shifted(normed[-1:], "seq", 1)) - normed
    mix = [(normed + change * vec[2 + i : 3 + i]).astype(BF) for i in range(6)]
    m_r, m_w, m_k, m_v, m_a, m_g = mix
    rr, h_r = adapted(m_r, mats[0], down(0), up(0))
    kr, h_k = adapted(m_k, mats[1], down(1), up(1))
    vr, h_v = adapted(m_v, mats[2], down(2), up(2))
    act_w = jnp.tanh(mm(m_w, first_all[:, :lo]))
    wl = mm(act_w.astype(BF), second_all[:lo])
    pre_a = mm(m_a, first_all[:, lo:hi]).astype(BF)
    al = mm(pre_a, second_all[lo:hi])
    act_g = jax.nn.sigmoid(mm(m_g, first_all[:, hi:]))
    gg = mm(act_g.astype(BF), second_all[hi:])

    full = jax.ShapeDtypeStruct((length, width), F32)
    low = jax.ShapeDtypeStruct((length, width), BF)
    small = jax.ShapeDtypeStruct((D, width), F32)
    reff, oloc, w1, w2, xs, mv, mt, piece = over_pairs(
        functools.partial(rec_local, nc), pairs, (rr, kr, vr, wl, al, vec),
        [full] * 5 + [jax.ShapeDtypeStruct((2, length, width), F32), full, jax.ShapeDtypeStruct((3, D, width), F32)],
        "rec_local",
    )
    zin = pass_states(n_seq, piece[0], piece[1], False)
    gated, o, us, zs = over_pairs(
        functools.partial(rec_out, nc), pairs,
        (zin, rr, kr, vr, al, gg, vec, reff, oloc, w1, w2, mv),
        [low, full, full, full], "rec_out",
    )
    attended, h_o = adapted(gated, mats[3], down(3), up(3))
    middle = wide + attended
    normed2, norm2_pull = jax.vjp(lambda t: layer_norm(t, vec[15:16], vec[16:17]), middle)
    mu = vec[17:18]
    m_c = (normed2 + (previous(normed2, shifted(normed2[-1:], "seq", 1)) - normed2) * mu).astype(BF)
    pre, h_c = adapted(m_c, key_all, down(4), chosen_hidden[RANK:])
    active = jnp.maximum(pre, 0.0)
    squared = (active * active).astype(BF)
    chan, h_f = adapted(squared, value_all, chosen_hidden[:RANK], up(4))
    result = (middle + chan).astype(BF)

    cot = output_gradient.astype(F32)
    d_sq, down_f, up_f = adapted_back(cot, squared, value_all, chosen_hidden[:RANK], up(4), h_f)
    d_mc, down_c, up_c = adapted_back(d_sq * 2.0 * active, m_c, key_all, down(4), chosen_hidden[RANK:], h_c)
    moved = d_mc * mu
    d_n2 = d_mc - moved + following(moved, shifted(moved[:1], "seq", -1))
    d_mid = norm2_pull(d_n2)[0] + cot
    d_gated, down_o, up_o = adapted_back(d_mid, gated, mats[3], down(3), up(3), h_o)
    do, dgg, es, eloc = over_pairs(
        functools.partial(back_local, nc), pairs,
        (d_gated, gg, o, rr, kr, vr, al, vec, reff, mt), [full, low, full, small], "back_local",
    )
    hin = pass_states(n_seq, piece[2], eloc, True)
    drr, dkr, dvr, dwl, dal = over_pairs(
        functools.partial(rec_back, nc), pairs,
        (hin, d_gated, gg, do, rr, kr, vr, wl, al, vec, xs, us, zs, mt, es), [low] * 5, "rec_back",
    )
    d_tg = (mm_nt(dgg, second_all[hi:]) * act_g * (1.0 - act_g)).astype(BF)
    d_ta = mm_nt(dal, second_all[lo:hi]).astype(BF)
    d_tw = (mm_nt(dwl, second_all[:lo]) * (1.0 - act_w * act_w)).astype(BF)
    d_mr, down_r, up_r = adapted_back(drr, m_r, mats[0], down(0), up(0), h_r)
    d_mk, down_k, up_k = adapted_back(dkr, m_k, mats[1], down(1), up(1), h_k)
    d_mv, down_v, up_v = adapted_back(dvr, m_v, mats[2], down(2), up(2), h_v)
    grads = [
        d_mr, mm_nt(d_tw, first_all[:, :lo]), d_mk, d_mv,
        mm_nt(d_ta, first_all[:, lo:hi]), mm_nt(d_tg, first_all[:, hi:]),
    ]
    stay = sum(g * (1.0 - vec[2 + i : 3 + i]) for i, g in enumerate(grads))
    go = sum(g * vec[2 + i : 3 + i] for i, g in enumerate(grads))
    d_n1 = stay + following(go, shifted(go[:1], "seq", -1))
    grad_tokens = norm_pull(d_n1)[0] + d_mid
    per_model = jnp.concatenate([down_r, down_k, down_v, down_o, down_c, up_r, up_k, up_v, up_o, up_f], axis=0)
    per_hidden = jnp.concatenate([down_f, up_c], axis=0)
    pick_f = pick.astype(F32)[:, None, None]
    grad_model = lax.psum_scatter(pick_f * per_model, axes, scatter_dimension=2, tiled=True)
    grad_hidden = lax.psum_scatter(pick_f * per_hidden, axes, scatter_dimension=2, tiled=True)
    return result[None], grad_tokens[None], grad_model, grad_hidden


def solution(mesh):
    cols = P(None, ("seq", "dp"))
    rows = P(("seq", "dp"), None)
    deep = P(None, None, ("seq", "dp"))
    act = P("dp", "seq", None)
    return jax.shard_map(
        body,
        mesh=mesh,
        in_specs=(act, act, P("dp"), deep, rows, cols, cols, cols, rows, deep, deep),
        out_specs=(act, act, deep, deep),
        check_vma=False,
    )
```

```python
import functools
import math

import jax
import jax.numpy as jnp
from jax import lax
from jax.experimental import pallas as pl
from jax.experimental.pallas import tpu as pltpu
from jax.sharding import PartitionSpec as P

F32, BF = jnp.float32, jnp.bfloat16
MESH = pl.DeviceIdType.MESH
D = 64
C = 64
PW = 2 * D
DECAY_INNER, RATE_INNER, GATE_INNER, RANK = 96, 96, 256, 16
SCALE = 4.0
NORM_EPS, GROUP_EPS, UNIT_EPS = 1e-05, 0.00064, 1e-06
DECAY_SCALE = math.exp(-0.5)
PRECISE = lax.Precision.HIGHEST
DIMS = {
    "nn": (((1,), (0,)), ((), ())),
    "nt": (((1,), (1,)), ((), ())),
    "tn": (((0,), (0,)), ((), ())),
}


def split(x):
    hi = x.astype(BF)
    return hi, (x - hi.astype(F32)).astype(BF)


def dot1(a, b, m="nn"):
    return lax.dot_general(a.astype(BF), b.astype(BF), DIMS[m], preferred_element_type=F32)


def dot3(a, b, m="nn"):
    ah, al = split(a)
    bh, bl = split(b)
    ka, kb = (0 if m == "tn" else 1), (1 if m == "nt" else 0)
    n = b.shape[1 - kb]
    aa = jnp.concatenate([ah, al], axis=ka)
    bb = jnp.concatenate([jnp.concatenate([bh, bl], axis=1 - kb)] * 2, axis=kb)
    r = lax.dot_general(aa, bb, DIMS[m], preferred_element_type=F32)
    return r[:, :n] + r[:, n:]


dot_inv = dot_a = dot_w = dot_b = dot_g = dot3


def iota(shape, axis):
    return lax.broadcasted_iota(jnp.int32, shape, axis)


def stack2(x):
    lane = iota(x.shape, 1)
    zero = jnp.zeros_like(x)
    return jnp.concatenate([jnp.where(lane < D, x, zero), jnp.where(lane < D, zero, x)], axis=0)


def pack2(x):
    h = x.shape[0] // 2
    return x[:h] + x[h:]


def head_ones():
    r, c = iota((2 * PW, PW), 0) % PW, iota((2 * PW, PW), 1)
    return jnp.where((r // D) == (c // D), 1.0, 0.0).astype(BF)


def headsum(x, ones):
    h, l = split(x)
    return lax.dot_general(
        jnp.concatenate([h, l], axis=1), ones, DIMS["nn"], preferred_element_type=F32
    )


def triangle(upper):
    r, c = iota((C, C), 0), iota((C, C), 1)
    return jnp.where((r <= c) if upper else (r >= c), 1.0, 0.0).astype(BF)


def cums(x, tri):
    h, l = split(x)
    m = (x - h.astype(F32) - l.astype(F32)).astype(BF)
    n = x.shape[1]
    r = lax.dot_general(
        tri, jnp.concatenate([h, l, m], axis=1), DIMS["nn"], preferred_element_type=F32
    )
    return r[:, :n] + r[:, n : 2 * n] + r[:, 2 * n :]


def prelude(kr, wl, al, w0, a0, k_k, k_a, ones):
    s = jax.nn.sigmoid(w0 + wl)
    a = jax.nn.sigmoid(a0 + al)
    kx = kr * k_k
    rn = lax.rsqrt(headsum(kx * kx, ones) + UNIT_EPS)
    return s, -DECAY_SCALE * s, a, rn, kx * rn, kr * (1.0 + (a - 1.0) * k_a)


def grid_ids():
    r, c = iota((PW, PW), 0), iota((PW, PW), 1)
    return r, c, (r // D) == (c // D)


def inverses(many):
    r, c, _ = grid_ids()
    eye = jnp.where(r == c, 1.0, 0.0)
    b = 1
    while b < C:
        level = ((r // (2 * b)) == (c // (2 * b))) & ((r // b) % 2 == 1) & ((c // b) % 2 == 0)
        parts = [jnp.where(level, a, 0.0) for a in many]
        if b == 1:
            xs = [eye + p for p in parts]
        else:
            half = [dot_inv(x, p) for x, p in zip(xs, parts)]
            xs = [x + dot_inv(h, x) for h, x in zip(half, xs)]
        b *= 2
    return xs


def factors(logw, tri):
    run = cums(logw, tri)
    return jnp.exp(run - logw), jnp.exp(run), jnp.exp(-run), jnp.exp(run[C - 1 : C])


def forward_chunks(units, tri):
    rows, cols, same = grid_ids()
    zero = jnp.zeros((PW, PW), F32)
    strict, incl = (rows > cols) & same, (rows >= cols) & same
    fs = [factors(u[5], tri) for u in units]
    p2 = [stack2(u[1] * f[0]) for u, f in zip(units, fs)]
    r2 = [stack2(u[0] * f[1]) for u, f in zip(units, fs)]
    q2 = [stack2(u[2] * f[2]) for u, f in zip(units, fs)]
    k2 = [stack2(u[3] * f[2]) for u, f in zip(units, fs)]
    v2 = [stack2(u[4]) for u in units]
    aa = [
        dot_a(jnp.concatenate([p, r], 0), jnp.concatenate([q, k], 0), "nt")
        for p, r, q, k in zip(p2, r2, q2, k2)
    ]
    apk = [jnp.where(strict, a[:PW, PW:], zero) for a in aa]
    y = [dot_w(a, v) for a, v in zip(apk, v2)]
    xs = inverses([jnp.where(strict, a[:PW, :PW], zero) for a in aa])
    ww = [dot_w(x, jnp.concatenate([p, t], 1)) for x, p, t in zip(xs, p2, y)]
    left = [
        jnp.concatenate(
            [
                jnp.concatenate(
                    [jnp.where(incl, a[PW:, :PW], zero), jnp.where(incl, a[PW:, PW:], zero)], 1
                ),
                jnp.concatenate([(q * f[3]).T, (k * f[3]).T], 1),
            ],
            0,
        )
        for a, q, k, f in zip(aa, q2, k2, fs)
    ]
    right = [
        jnp.concatenate([w, jnp.concatenate([zero, v], 1)], 0) for w, v in zip(ww, v2)
    ]
    big = [dot_b(l, r) for l, r in zip(left, right)]
    move = [
        b[PW:, :PW] + jnp.where(rows == cols, jnp.broadcast_to(f[3], (PW, PW)), zero)
        for b, f in zip(big, fs)
    ]
    return [
        (pack2(r + b[:PW, :PW]), pack2(b[:PW, PW:]), m, b[PW:, PW:], pack2(w[:, :PW]), pack2(w[:, PW:]), x)
        for r, b, m, w, x in zip(r2, big, move, ww, xs)
    ]


def backward_chunks(units, tri, tri_up):
    rows, cols, same = grid_ids()
    zero = jnp.zeros((PW, PW), F32)
    strict, incl = (rows < cols) & same, (rows <= cols) & same
    both = jnp.concatenate([jnp.concatenate([strict, incl], 1)] * 2, 0)
    fs = [factors(t[5], tri) for t in units]
    pe = [t[1] * f[0] for t, f in zip(units, fs)]
    re = [t[0] * f[1] for t, f in zip(units, fs)]
    qe = [t[2] * f[2] for t, f in zip(units, fs)]
    ke = [t[3] * f[2] for t, f in zip(units, fs)]
    g2 = [stack2(t[10]) for t in units]
    qk = [jnp.concatenate([stack2(q), stack2(k)], 0) for q, k in zip(qe, ke)]
    pr = [jnp.concatenate([stack2(p), stack2(r)], 0) for p, r in zip(pe, re)]
    at = [dot_a(a, b, "nt") for a, b in zip(qk, pr)]
    qkh = [
        dot_g(jnp.concatenate([q * f[3], k * f[3]], 0), t[9])
        for q, k, f, t in zip(qe, ke, fs, units)
    ]
    sq = [dot_g(jnp.concatenate([t[7], t[4]], 0), t[9], "nt") for t in units]
    du = [
        dot_g(jnp.where(incl, a[:PW, PW:], zero), g) + stack2(h[:C])
        for a, g, h in zip(at, g2, qkh)
    ]
    dm = [dot_g(t[6], d, "tn") for t, d in zip(units, du)]
    dg = [jnp.concatenate([d, g], 0) for d, g in zip(dm, g2)]
    dv = [
        pack2(
            dot_g(
                jnp.concatenate(
                    [jnp.where(strict, a[PW:, :PW], zero), jnp.where(incl, a[PW:, PW:], zero)], 1
                ),
                d,
            )
        )
        + h[C:]
        for a, d, h in zip(at, dg, qkh)
    ]
    dat = [
        dot_g(jnp.concatenate([stack2(t[7]), stack2(t[4])], 0), d, "nt")
        for t, d in zip(units, dg)
    ]
    dat = [jnp.where(both, d, jnp.zeros_like(d)) for d in dat]
    dpr = [dot_g(d, a, "tn") for d, a in zip(dat, qk)]
    dqk = [dot_g(d, a) for d, a in zip(dat, pr)]
    sp = [dot_g(jnp.concatenate([pack2(d), t[10]], 0), t[8], "nt") for d, t in zip(dm, units)]
    outs = []
    for i, t in enumerate(units):
        eb, el, en, last = fs[i]
        dp, dr = pack2(dpr[i][:PW]) + sp[i][:C], pack2(dpr[i][PW:]) + sp[i][C:]
        dqh, dkh = sq[i][:C], sq[i][C:]
        dq, dk = pack2(dqk[i][:PW]) + dqh * last, pack2(dqk[i][PW:]) + dkh * last
        tail = jnp.sum((qe[i] * dqh + ke[i] * dkh) * last, axis=0, keepdims=True)
        tail = tail + last * jnp.sum((t[8] * t[9]).T, axis=0, keepdims=True)
        gb = pe[i] * dp
        gl = re[i] * dr - qe[i] * dq - ke[i] * dk
        dlogw = cums(gl + gb, tri_up) - gb + tail
        outs.append((dr * el, dp * eb, dq * en, dk * en, dv[i], dlogw))
    return outs


def lanes(ref):
    return [slice(i * PW, (i + 1) * PW) for i in range(ref.shape[-1] // PW)]


def rec_local(nc, rr, kr, vr, wl, al, vec, reff, oloc, w1, w2, xs, mv, mt, piece):
    ones, tri = head_ones(), triangle(False)
    units, where = [], []
    for ln in lanes(rr):
        row = lambda i: vec[i : i + 1, ln]
        _, logw, a, _, kk, km = prelude(
            kr[:, ln], wl[:, ln], al[:, ln], row(8), row(9), row(10), row(11), ones
        )
        r, v, q = rr[:, ln], vr[:, ln], kk * a
        for c in range(nc):
            s = slice(c * C, (c + 1) * C)
            units.append((r[s], -kk[s], q[s], km[s], v[s], logw[s]))
            where.append((s, ln))
    done = forward_chunks(units, tri)
    packed = []
    for (s, ln), (e, o, m, n, y1, y2, x) in zip(where, done):
        reff[s, ln], oloc[s, ln], w1[s, ln], w2[s, ln] = e, o, y1, y2
        xs[s, ln] = pack2(x)
        mp = pack2(m)
        mv[0, s, ln], mv[1, s, ln], mt[s, ln] = mp, pack2(n), pack2(m.T)
        packed.append(mp)
    for i, ln in enumerate(lanes(rr)):
        tm, tn = stack2(packed[i * nc]), done[i * nc][3]
        for c in range(1, nc):
            t = dot3(packed[i * nc + c], jnp.concatenate([tm, tn], 1))
            tm, tn = stack2(t[:, :PW]), stack2(t[:, PW:]) + done[i * nc + c][3]
        piece[0, :, ln], piece[1, :, ln], piece[2, :, ln] = pack2(tm), pack2(tn), pack2(tm.T)


def norm_parts(o, ones):
    centre = o - headsum(o, ones) * (1.0 / D)
    rstd = lax.rsqrt(headsum(centre * centre, ones) * (1.0 / D) + GROUP_EPS)
    return centre * rstd, rstd


def rec_out(
    nc, zin, rr, kr, vr, al, gg, vec, reff, oloc, w1, w2, mv, tokens, wo, down, up, norm,
    z_out, o_out, u_out, zs, middle, normed, h_out, acc_h,
):
    step, last = pl.program_id(0), pl.num_programs(0) - 1
    ones = head_ones()
    state = [zin[:, ln] for ln in lanes(rr)]
    for c in range(nc):
        s = slice(c * C, (c + 1) * C)
        ts = [
            dot3(jnp.concatenate([mv[0, s, ln], reff[s, ln], w1[s, ln]], 0), stack2(z))
            for z, ln in zip(state, lanes(rr))
        ]
        for i, (t, ln) in enumerate(zip(ts, lanes(rr))):
            zs[s, ln] = state[i]
            o_out[s, ln] = t[C : 2 * C] + oloc[s, ln]
            u_out[s, ln] = t[2 * C :] + w2[s, ln]
            state[i] = t[:C] + mv[1, s, ln]
    for ln in lanes(rr):
        row = lambda i: vec[i : i + 1, ln]
        a = jax.nn.sigmoid(row(9) + al[:, ln])
        km = kr[:, ln] * (1.0 + (a - 1.0) * row(11))
        hat, _ = norm_parts(o_out[:, ln], ones)
        y = hat * row(13) + row(14) + headsum(rr[:, ln] * km * row(12), ones) * vr[:, ln]
        z_out[:, ln] = (y * gg[:, ln]).astype(BF)

    @pl.when(step == 0)
    def _():
        acc_h[...] = jnp.zeros_like(acc_h)
        middle[...] = tokens[...].astype(F32)

    acc_h[...] += mm_nt(z_out[...], down[...])
    middle[...] += mm_nt(z_out[...], wo[...])

    @pl.when(step == last)
    def _():
        h_out[...] = acc_h[...].astype(BF)
        x1 = middle[...] + SCALE * mm(h_out[...], up[...])
        middle[...] = x1
        centre = x1 - jnp.mean(x1, axis=-1, keepdims=True)
        rstd = lax.rsqrt(jnp.mean(centre * centre, axis=-1, keepdims=True) + NORM_EPS)
        normed[...] = centre * rstd * norm[15:16, :] + norm[16:17, :]


def back_local(
    nc, d_mc, edge, gy, middle, norm, wo, down, down_all, up, h_o, gated,
    gg, o, rr, kr, vr, al, vec, reff, mt,
    d_mid, dz, do, dgg, es, piece, g_down, g_up, low, dh,
):
    @pl.when(pl.program_id(0) == 0)
    def _():
        moved = d_mc[...] * norm[17:18, :]
        n = moved.shape[0]
        up_one = pltpu.roll(moved, n - 1, axis=0)
        up_one = jnp.where(iota(moved.shape, 0) == n - 1, edge[...], up_one)
        dn = d_mc[...] - moved + up_one
        x1 = middle[...]
        centre = x1 - jnp.mean(x1, axis=-1, keepdims=True)
        rstd = lax.rsqrt(jnp.mean(centre * centre, axis=-1, keepdims=True) + NORM_EPS)
        hat = centre * rstd
        dhat = dn * norm[15:16, :]
        d = rstd * (
            dhat
            - jnp.mean(dhat, axis=-1, keepdims=True)
            - hat * jnp.mean(dhat * hat, axis=-1, keepdims=True)
        )
        d = d + gy[...].astype(F32)
        d_mid[...] = d
        low[...] = d.astype(BF)
        dh[...] = (SCALE * mm_nt(low[...], up[...])).astype(BF)
        g_up[...] = SCALE * mm_tn(h_o[...], low[...])

    dz[...] = mm(low[...], wo[...]) + mm(dh[...], down[...])
    g_down[...] = mm_tn(dh[...], gated[...])
    ones = head_ones()
    _, _, same = grid_ids()
    for ln in lanes(rr):
        row = lambda i: vec[i : i + 1, ln]
        a = jax.nn.sigmoid(row(9) + al[:, ln])
        km = kr[:, ln] * (1.0 + (a - 1.0) * row(11))
        hat, rstd = norm_parts(o[:, ln], ones)
        y = hat * row(13) + row(14) + headsum(rr[:, ln] * km * row(12), ones) * vr[:, ln]
        dgg[:, ln] = (dz[:, ln] * y).astype(BF)
        dhat = dz[:, ln] * gg[:, ln] * row(13)
        do[:, ln] = rstd * (
            dhat
            - headsum(dhat, ones) * (1.0 / D)
            - hat * (headsum(dhat * hat, ones) * (1.0 / D))
        )
    for c in range(nc):
        s = slice(c * C, (c + 1) * C)
        for ln in lanes(rr):
            es[s, ln] = pack2(jnp.where(same, dot3(reff[s, ln], do[s, ln], "tn"), 0.0))
    state = [es[(nc - 1) * C : nc * C, ln] for ln in lanes(rr)]
    for c in reversed(range(nc - 1)):
        s = slice(c * C, (c + 1) * C)
        state = [es[s, ln] + dot3(mt[s, ln], stack2(h)) for h, ln in zip(state, lanes(rr))]
    for h, ln in zip(state, lanes(rr)):
        piece[:, ln] = h


def rec_back(
    nc, hin, dz, gg, do, rr, kr, vr, wl, al, vec, xs, us, zs, mt, es, drr, dkr, dvr, dwl, dal
):
    ones, tri, tri_up = head_ones(), triangle(False), triangle(True)
    units, where, pre = [], [], []
    hs = {}
    for ln in lanes(rr):
        h = hin[:, ln]
        for c in reversed(range(nc)):
            s = slice(c * C, (c + 1) * C)
            hs[c, ln.start] = stack2(h)
            if c:
                h = dot3(mt[s, ln], hs[c, ln.start]) + es[s, ln]
    for ln in lanes(rr):
        row = lambda i: vec[i : i + 1, ln]
        for c in range(nc):
            s = slice(c * C, (c + 1) * C)
            r, v, k = rr[s, ln], vr[s, ln], kr[s, ln]
            sg, logw, a, rn, kk, km = prelude(
                k, wl[s, ln], al[s, ln], row(8), row(9), row(10), row(11), ones
            )
            units.append(
                (r, -kk, kk * a, km, v, logw, stack2(xs[s, ln]), us[s, ln], stack2(zs[s, ln]),
                 hs[c, ln.start], do[s, ln])
            )
            where.append((s, ln))
            pre.append((sg, a, rn, kk, km))
    done = backward_chunks(units, tri, tri_up)
    for (s, ln), (sg, a, rn, kk, km), (dr, dp, dq, dk, dv, dlogw) in zip(where, pre, done):
        row = lambda i: vec[i : i + 1, ln]
        r, v, k = rr[s, ln], vr[s, ln], kr[s, ln]
        dy = dz[s, ln] * gg[s, ln]
        dv = dv + headsum(r * km * row(12), ones) * dy
        ds = headsum(dy * v, ones) * row(12)
        dr = dr + ds * km
        dkm = dk + ds * r
        dkk = dq * a - dp
        da = dq * kk + dkm * k * row(11)
        dk = dkm * (1.0 + (a - 1.0) * row(11)) + row(10) * rn * (dkk - kk * headsum(dkk * kk, ones))
        drr[s, ln], dkr[s, ln], dvr[s, ln] = dr.astype(BF), dk.astype(BF), dv.astype(BF)
        dwl[s, ln] = (dlogw * (-DECAY_SCALE) * sg * (1.0 - sg)).astype(BF)
        dal[s, ln] = (da * a * (1.0 - a)).astype(BF)


TILE = 2 * PW


def cut(shape):
    lead = tuple(shape[:-1])
    return pl.BlockSpec(lead + (TILE,), lambda i, n=len(lead): (0,) * n + (i,))


def whole(shape):
    return pl.BlockSpec(tuple(shape), lambda i, n=len(shape): (0,) * n)


def tile_rows(shape):
    return pl.BlockSpec((TILE, shape[1]), lambda i: (i, 0))


def over_tiles(body, steps, ins, outs, name, scratch=(), **params):
    made = lambda spec, shape: spec if isinstance(spec, pl.BlockSpec) else spec(shape)
    return pl.pallas_call(
        body,
        grid=(steps,),
        in_specs=[made(spec, x.shape) for spec, x in ins],
        out_specs=[made(spec, x.shape) for spec, x in outs],
        out_shape=[x for _, x in outs],
        scratch_shapes=list(scratch),
        compiler_params=pltpu.CompilerParams(vmem_limit_bytes=60 * 1024 * 1024, **params),
        name=name,
    )(*[x for _, x in ins])


def pass_kernel(n, groups, back, move, add, out, here, send, send_sem, recv_sem):
    s, d = lax.axis_index("seq"), lax.axis_index("dp")
    if back:
        first, final, nxt, prv = s == n - 1, s == 0, s - 1, s + 1
    else:
        first, final, nxt, prv = s == 0, s == n - 1, s + 1, s - 1
    barrier = pltpu.get_barrier_semaphore()

    @pl.when(jnp.logical_not(first))
    def _():
        pl.semaphore_signal(barrier, inc=1, device_id=(prv, d), device_id_type=MESH)

    @pl.when(jnp.logical_not(final))
    def _():
        pl.semaphore_wait(barrier, 1)

    def copy(g, to):
        return pltpu.make_async_remote_copy(
            src_ref=send.at[g],
            dst_ref=here.at[g],
            send_sem=send_sem.at[g],
            recv_sem=recv_sem.at[g],
            device_id=(to, d),
            device_id_type=MESH,
        )

    per = out.shape[1] // (groups * PW)
    for g in range(groups):

        @pl.when(first)
        def _():
            here[g] = jnp.zeros(here.shape[1:], F32)

        @pl.when(jnp.logical_not(first))
        def _():
            copy(g, prv).wait_recv()

        out[:, g * per * PW : (g + 1) * per * PW] = here[g]

        @pl.when(jnp.logical_not(final))
        def _():
            for i in range(per):
                at = (g * per + i) * PW
                state = stack2(here[g, :, i * PW : (i + 1) * PW])
                send[g, :, i * PW : (i + 1) * PW] = (
                    dot3(move[:, at : at + PW], state) + add[:, at : at + PW]
                )
            copy(g, nxt).start()

    @pl.when(jnp.logical_not(final))
    def _():
        for g in range(groups):
            copy(g, nxt).wait_send()


def pass_states(n, move, add, back):
    rows, width = move.shape
    groups = width // PW
    return pl.pallas_call(
        functools.partial(pass_kernel, n, groups, back),
        out_shape=jax.ShapeDtypeStruct((rows, width), F32),
        in_specs=[pl.BlockSpec(memory_space=pltpu.VMEM)] * 2,
        out_specs=pl.BlockSpec(memory_space=pltpu.VMEM),
        scratch_shapes=[
            pltpu.VMEM((groups, rows, width // groups), F32),
            pltpu.VMEM((groups, rows, width // groups), F32),
            pltpu.SemaphoreType.DMA((groups,)),
            pltpu.SemaphoreType.DMA((groups,)),
        ],
        compiler_params=pltpu.CompilerParams(
            collective_id=1 if back else 0, has_side_effects=True
        ),
        name="pass_back" if back else "pass_on",
    )(move, add)


ORDERS = ("zxy", "zyx", "xzy", "yzx")
DIRS = "xyuds"


def gather_events(order, z, x, y):
    other = {"x": lambda q: (q, 1 - x, y), "y": lambda q: (q, x, 1 - y), "z": lambda q: (q, x, y)}
    inside = lambda k: None if k == 0 else jnp.logical_and(z + k >= 0, z + k <= 3)
    if order[0] == "z":
        a, b = order[1], order[2]
        events = [(0, (z, x, y), None, None, [a, b, "u", "d", "s"])]
        for k in (1, 2, 3):
            events.append((k, (z - k, x, y), "u", z >= k, ["u", a, b, "s"]))
            events.append((k, (z + k, x, y), "d", z + k <= 3, ["d", a, b, "s"]))
        for k in range(-3, 4):
            events.append((abs(k) + 1, other[a](z + k), a, inside(k), [b, "s"]))
    else:
        a, b = order[0], order[2]
        events = [(0, (z, x, y), None, None, [a, "u", "d", b, "s"])]
        events.append((1, other[a](z), a, None, ["u", "d", b, "s"]))
        for k in (1, 2, 3):
            for late, at in ((0, other["z"]), (1, other[a])):
                events.append((k + late, at(z - k), "u", z >= k, ["u", b, "s"]))
                events.append((k + late, at(z + k), "d", z + k <= 3, ["d", b, "s"]))
    for k in range(-3, 4):
        events.append((abs(k) + 1, other[b](z + k), b, inside(k), ["s"]))
        events.append((abs(k) + 2, (z + k, 1 - x, 1 - y), b, inside(k), ["s"]))
    return events


def maybe(condition, run):
    if condition is None:
        run()
    else:
        pl.when(condition)(run)


def gather_kernel(orders, *refs):
    n = len(orders)
    shards, whole = refs[:n], refs[n : 2 * n]
    send, recv, near = refs[2 * n :]
    seq, dp = lax.axis_index("seq"), lax.axis_index("dp")
    z, x, y, c = seq // 2, seq % 2, dp // 2, dp % 2
    to = {
        "x": (z * 2 + 1 - x, dp),
        "y": (seq, (1 - y) * 2 + c),
        "u": (seq + 2, dp),
        "d": (seq - 2, dp),
        "s": (seq, y * 2 + 1 - c),
    }
    exists = {"u": z < 3, "d": z > 0}
    barrier = pltpu.get_barrier_semaphore()
    for k in DIRS:
        maybe(
            exists.get(k),
            lambda k=k: pl.semaphore_signal(barrier, inc=1, device_id=to[k], device_id_type=MESH),
        )
    pl.semaphore_wait(barrier, 3 + (z + 2) // 3 + (5 - z) // 3)

    chip = lambda b: b[0] * 4 + b[1] * 2 + b[2]

    def copy(t, own, b, k):
        slot = whole[t].at[chip(b) * 2 + c]
        return pltpu.make_async_remote_copy(
            src_ref=shards[t] if own else slot,
            dst_ref=slot,
            send_sem=send.at[DIRS.index(k), t, chip(b)],
            recv_sem=recv.at[1 if k == "s" else 0, t, chip(b)],
            device_id=to[k],
            device_id_type=MESH,
        )

    todo = [(e[0], t, i, e) for t, o in enumerate(orders) for i, e in enumerate(gather_events(o, z, x, y))]
    todo.sort(key=lambda q: q[0])
    sent, own = [], []
    for _, t, _, (_, b, came, condition, goes) in todo:
        if came is None:
            own.append(pltpu.make_async_copy(shards[t], whole[t].at[chip(b) * 2 + c], near.at[t]))
            own[-1].start()
        else:
            maybe(condition, lambda: copy(t, False, b, came).wait_recv())
        for k in goes:
            both = exists.get(k) if condition is None else condition
            if condition is not None and k in exists:
                both = jnp.logical_and(condition, exists[k])
            maybe(both, lambda: copy(t, came is None, b, k).start())
            sent.append((t, came is None, b, k, both))
    for t in range(n):
        for i in range(16):
            pltpu.make_async_remote_copy(
                src_ref=shards[t],
                dst_ref=whole[t].at[i * 2 + 1 - c],
                send_sem=send.at[4, t, i],
                recv_sem=recv.at[1, t, i],
                device_id=to["s"],
                device_id_type=MESH,
            ).wait_recv()
    for t, mine, b, k, both in sent:
        maybe(both, lambda: copy(t, mine, b, k).wait_send())
    for o in own:
        o.wait()


def gather(shards):
    n_seq, n_dp, n = lax.axis_size("seq"), lax.axis_size("dp"), len(shards)
    if (n_seq, n_dp) != (8, 4):
        return [lax.all_gather(s, ("seq", "dp"), axis=0) for s in shards]
    return pl.pallas_call(
        functools.partial(gather_kernel, [ORDERS[i % len(ORDERS)] for i in range(n)]),
        out_shape=[jax.ShapeDtypeStruct((n_seq * n_dp,) + s.shape, s.dtype) for s in shards],
        in_specs=[pl.BlockSpec(memory_space=pl.ANY)] * n,
        out_specs=[pl.BlockSpec(memory_space=pl.ANY)] * n,
        scratch_shapes=[
            pltpu.SemaphoreType.DMA((5, n, 16)),
            pltpu.SemaphoreType.DMA((2, n, 16)),
            pltpu.SemaphoreType.DMA((n,)),
        ],
        compiler_params=pltpu.CompilerParams(collective_id=2, has_side_effects=True),
        name="gather_time",
    )(*shards)


def channel_kernel(
    n2, edge, norm, gy, middle, down_c, up_f, kv, hidden,
    out, dmc, first, g_hidden, g_up_f, g_down_c, mc, ffo, h_c, dh_f, acc_f, acc_c,
):
    step, last = pl.program_id(0), pl.num_programs(0) - 1
    per, ff = kv.shape[0], kv.shape[1] // 2

    @pl.when(step == 0)
    def _():
        x = n2[...]
        before = jnp.where(iota(x.shape, 0) == 0, edge[...], pltpu.roll(x, 1, axis=0))
        mc[...] = (x + (before - x) * norm[17:18, :]).astype(BF)
        h_c[...] = mm_nt(mc[...], down_c[...]).astype(BF)
        dh_f[...] = (SCALE * mm_nt(gy[...], up_f[...])).astype(BF)
        acc_f[...] = jnp.zeros_like(acc_f)
        acc_c[...] = jnp.zeros_like(acc_c)
        ffo[...] = jnp.zeros_like(ffo)
        dmc[...] = jnp.zeros_like(dmc)

    hqs, dps = [], []
    for b in range(per):
        down_f, up_c = hidden[b, :RANK], hidden[b, RANK:]
        pre = mm_nt(mc[...], kv[b, :ff]) + SCALE * mm(h_c[...], up_c)
        dsq = mm_nt(gy[...], kv[b, ff:]) + mm(dh_f[...], down_f)
        active = jnp.maximum(pre, 0.0)
        hq = (active * active).astype(BF)
        dpre = (dsq * (2.0 * active)).astype(BF)
        g_hidden[b, :RANK] = mm_tn(dh_f[...], hq)
        g_hidden[b, RANK:] = SCALE * mm_tn(h_c[...], dpre)
        acc_f[...] += mm_nt(hq, down_f)
        acc_c[...] += mm_nt(dpre, up_c)
        hqs.append(hq)
        dps.append(dpre)
    hq, dpre = jnp.concatenate(hqs, 1), jnp.concatenate(dps, 1)
    ffo[...] += mm(hq, jnp.concatenate([kv[b, ff:] for b in range(per)], 0))
    dmc[...] += mm(dpre, jnp.concatenate([kv[b, :ff] for b in range(per)], 0))

    @pl.when(step == last)
    def _():
        h_f = acc_f[...].astype(BF)
        out[...] = (middle[...] + ffo[...] + SCALE * mm(h_f, up_f[...])).astype(BF)
        g_up_f[...] = SCALE * mm_tn(h_f, gy[...])
        dh_c = (SCALE * acc_c[...]).astype(BF)
        d = dmc[...] + mm(dh_c, down_c[...])
        dmc[...] = d
        first[...] = d[:8] * norm[17:18, :]
        g_down_c[...] = mm_tn(dh_c, mc[...])


def channel(n2, edge, norm, gy, middle, down_c, up_f, kv, hidden):
    n, both, width = kv.shape
    ff, length = both // 2, n2.shape[0]
    per = max(1, min(n, 512 // ff))
    block = lambda shape: pl.BlockSpec((per,) + tuple(shape[1:]), lambda i: (i, 0, 0))
    rank = jax.ShapeDtypeStruct((RANK, width), F32)
    return over_tiles(
        channel_kernel,
        n // per,
        [(whole, a) for a in (n2, edge, norm, gy, middle, down_c, up_f)] + [(block, kv), (block, hidden)],
        [
            (whole, jax.ShapeDtypeStruct((length, width), BF)),
            (whole, jax.ShapeDtypeStruct((length, width), F32)),
            (whole, jax.ShapeDtypeStruct((8, width), F32)),
            (block, jax.ShapeDtypeStruct((n, 2 * RANK, ff), F32)),
            (whole, rank),
            (whole, rank),
        ],
        "channel",
        [
            pltpu.VMEM((length, width), BF),
            pltpu.VMEM((length, width), F32),
            pltpu.VMEM((length, RANK), BF),
            pltpu.VMEM((length, RANK), BF),
            pltpu.VMEM((length, RANK), F32),
            pltpu.VMEM((length, RANK), F32),
        ],
    )


HALF = 512


def branch_masks(shape):
    lane = iota(shape, 1)
    lo, hi = DECAY_INNER, DECAY_INNER + RATE_INNER
    return lane < lo, (lane >= lo) & (lane < hi), (lane >= hi) & (lane < hi + GATE_INNER)


def project_kernel(
    hat, hat_prev, valid, vec, first, chosen, second, w_r, w_k, w_v, up,
    rr, kr, vr, wl, al, gg, m_r, m_k, m_v, hs, act, act_low,
):
    @pl.when(pl.program_id(0) == 0)
    def _():
        n1 = hat[...] * vec[0:1, :] + vec[1:2, :]
        change = (hat_prev[...] * vec[0:1, :] + vec[1:2, :]) * valid[...] - n1
        mixed = lambda i: (n1 + change * vec[2 + i : 3 + i, :]).astype(BF)
        m_r[...], m_k[...], m_v[...] = mixed(0), mixed(2), mixed(3)
        for i, m in enumerate((m_r, m_k, m_v)):
            hs[i] = mm_nt(m[...], chosen[i * RANK : (i + 1) * RANK, :]).astype(BF)
        t_w = mm(mixed(1), first[...])
        t_a = mm(mixed(4), first[...])
        t_g = mm(mixed(5), first[...])
        is_w, is_a, is_g = branch_masks(t_w.shape)
        zero = jnp.zeros_like(t_w)
        t_w = jnp.where(is_w, jnp.tanh(t_w), zero)
        t_a = jnp.where(is_a, t_a, zero)
        t_g = jnp.where(is_g, jax.nn.sigmoid(t_g), zero)
        act[...] = t_w + t_a + t_g
        act_low[0], act_low[1], act_low[2] = t_w.astype(BF), t_a.astype(BF), t_g.astype(BF)

    for i, (m, w, out) in enumerate(((m_r, w_r, rr), (m_k, w_k, kr), (m_v, w_v, vr))):
        out[...] = mm_nt(m[...], w[...]) + SCALE * mm(hs[i], up[(5 + i) * RANK : (6 + i) * RANK, :])
    for i, out in enumerate((wl, al, gg)):
        out[...] = mm_nt(act_low[i], second[...])


def late_kernel(drr, dkr, dvr, dwl, dal, dgg, m_r, m_k, m_v, hs, act, chosen, second, dhs, d_act, grads):
    for i, (d, m) in enumerate(((drr, m_r), (dkr, m_k), (dvr, m_v))):
        dh = (SCALE * mm_nt(d[...], chosen[(5 + i) * RANK : (6 + i) * RANK, :])).astype(BF)
        dhs[i] = dh
        down, up = mm_tn(dh, m[...]), SCALE * mm_tn(hs[i], d[...])
        wide = grads.shape[2]
        for p in range(grads.shape[0]):
            part = slice(p * wide, (p + 1) * wide)
            grads[p, i * RANK : (i + 1) * RANK, :] = down[:, part]
            grads[p, (3 + i) * RANK : (4 + i) * RANK, :] = up[:, part]
    is_w, is_a, is_g = branch_masks(act.shape)
    a = act[...]
    zero = jnp.zeros_like(a)
    d_act[0] = jnp.where(is_w, mm(dwl[...], second[...]) * (1.0 - a * a), zero).astype(BF)
    d_act[1] = jnp.where(is_a, mm(dal[...], second[...]), zero).astype(BF)
    d_act[2] = jnp.where(is_g, mm(dgg[...], second[...]) * a * (1.0 - a), zero).astype(BF)


def final_kernel(
    n, drr, dkr, dvr, w_r, w_k, w_v, dhs, down, d_act, first, vec, parts,
    stay, go, summed, here, send_sem, recv_sem,
):
    step, last = pl.program_id(0), pl.num_programs(0) - 1
    me, dp = lax.axis_index("seq"), lax.axis_index("dp")

    def copy(k):
        peer = lax.rem(me + k, n)
        return pltpu.make_async_remote_copy(
            src_ref=parts.at[peer],
            dst_ref=here.at[k - 1],
            send_sem=send_sem.at[k - 1],
            recv_sem=recv_sem.at[k - 1],
            device_id=(peer, dp),
            device_id_type=MESH,
        )

    @pl.when(step == 0)
    def _():
        barrier = pltpu.get_barrier_semaphore()
        for k in range(1, n):
            pl.semaphore_signal(
                barrier, inc=1, device_id=(lax.rem(me + k, n), dp), device_id_type=MESH
            )
        pl.semaphore_wait(barrier, n - 1)
        for k in range(1, n):
            copy(k).start()

    total, moved = None, None
    for i, (d, w, at) in enumerate(((drr, w_r, 2), (dkr, w_k, 4), (dvr, w_v, 5))):
        g = mm(d[...], w[...]) + mm(dhs[i], down[i * RANK : (i + 1) * RANK, :])
        move = g * vec[at : at + 1, :]
        total, moved = (g, move) if total is None else (total + g, moved + move)
    for i, at in enumerate((3, 6, 7)):
        g = mm_nt(d_act[i], first[...])
        total, moved = total + g, moved + g * vec[at : at + 1, :]
    stay[...] = total - moved
    go[...] = moved

    @pl.when(step == last)
    def _():
        for k in range(1, n):
            copy(k).wait()
        t = parts[me]
        for k in range(1, n):
            t = t + here[k - 1]
        summed[...] = t


def shifted(block, axis, distance):
    devices = range(lax.axis_size(axis))
    route = [(i - distance, i) for i in devices if i - distance in devices]
    return lax.ppermute(block, axis, route)


def mm(a, b):
    return lax.dot_general(a, b, DIMS["nn"], preferred_element_type=F32)


def mm_nt(a, b):
    return lax.dot_general(a, b, DIMS["nt"], preferred_element_type=F32)


def mm_tn(a, b):
    return lax.dot_general(a, b, DIMS["tn"], preferred_element_type=F32)


def body(tokens, output_gradient, index, proj, first, second, vectors, ckey, cvalue, model_rows, hidden_rows):
    axes = ("seq", "dp")
    n_seq, n_dp = lax.axis_size("seq"), lax.axis_size("dp")
    n = n_seq * n_dp
    tokens, gy = tokens[0], output_gradient[0]
    length, width = tokens.shape
    nc, tiles = length // C, width // TILE
    adapters, kinds, cols = model_rows.shape
    ff, inner, nvec = ckey.shape[1], first.shape[1], vectors.shape[0]

    kv = lax.all_gather(jnp.concatenate([ckey.T, cvalue], 0), axes, axis=0)

    index_all = lax.all_gather(index, "dp", axis=0, tiled=True)
    pick = index_all[:, None] == jnp.arange(adapters, dtype=jnp.int32)[None, :]
    few = jnp.concatenate([model_rows.reshape(adapters, -1), hidden_rows.reshape(adapters, -1)], 1)
    few = jnp.einsum("sa,ax->sx", pick.astype(BF), few, preferred_element_type=F32).astype(BF)
    pad = lambda k: jnp.zeros((cols, k), BF)
    misc = jnp.concatenate(
        [first, pad(HALF - inner), second.T, vectors.T, pad(HALF - inner - nvec)], axis=1
    )
    turned = jnp.swapaxes(proj, 1, 2)

    wide = tokens.astype(F32)
    ahead = shifted(tokens[-1:], "seq", 1).astype(F32)
    rows = jnp.concatenate([ahead, wide], 0)
    centre = rows - jnp.mean(rows, axis=-1, keepdims=True)
    rstd = lax.rsqrt(jnp.mean(centre * centre, axis=-1, keepdims=True) + NORM_EPS)
    hat = centre * rstd
    start = (jnp.arange(length)[:, None] == 0) & (lax.axis_index("seq") == 0)
    valid = jnp.where(start, 0.0, 1.0).astype(F32)
    hat_prev, hat, rstd = hat[:-1], hat[1:], rstd[1:]

    *mats, misc, few_all = gather([turned[0], turned[1], turned[2], turned[3], misc, few.reshape(-1, 128)])
    mats = [m.reshape(width, width) for m in mats]
    misc = misc.reshape(width, -1)
    vec = misc[:, HALF + inner : HALF + inner + nvec].T.astype(F32)
    own = lax.dynamic_index_in_dim(few_all.reshape(n, n_dp, -1, 128), lax.axis_index("dp"), 1, False)
    own = own.reshape(n, -1)
    chosen = own[:, : kinds * cols].reshape(n, kinds, cols).transpose(1, 0, 2).reshape(kinds, width)
    hidden = own[:, kinds * cols :].reshape(n, 2 * RANK, ff)
    down = lambda i: chosen[i * RANK : (i + 1) * RANK]
    up = lambda i: chosen[(5 + i) * RANK : (6 + i) * RANK]

    shape = jax.ShapeDtypeStruct
    full, low = shape((length, width), F32), shape((length, width), BF)
    small, rank = shape((D, width), F32), shape((RANK, width), F32)
    firsts = pl.BlockSpec((width, HALF), lambda i: (0, 0))
    seconds = pl.BlockSpec((width, HALF), lambda i: (0, 1))
    first_rows = pl.BlockSpec((TILE, HALF), lambda i: (i, 0))
    second_rows = pl.BlockSpec((TILE, HALF), lambda i: (i, 1))
    rr, kr, vr, wl, al, gg, m_r, m_k, m_v, hs, act = over_tiles(
        project_kernel, tiles,
        [
            (whole, hat), (whole, hat_prev), (whole, valid), (whole, vec), (firsts, misc), (whole, chosen),
            (second_rows, misc), (tile_rows, mats[0]), (tile_rows, mats[1]), (tile_rows, mats[2]), (cut, chosen),
        ],
        [(cut, full)] * 6
        + [(whole, low)] * 3
        + [(whole, shape((3, length, RANK), BF)), (whole, shape((length, HALF), F32))],
        "project",
        [pltpu.VMEM((3, length, HALF), BF)],
    )
    reff, oloc, w1, w2, xs, mv, mt, piece = over_tiles(
        functools.partial(rec_local, nc), tiles,
        [(cut, a) for a in (rr, kr, vr, wl, al, vec)],
        [(cut, full)] * 5 + [(cut, shape((2, length, width), F32)), (cut, full), (cut, shape((3, D, width), F32))],
        "rec_local",
    )
    zin = pass_states(n_seq, piece[0], piece[1], False)
    gated, o, us, zs, middle, n2, h_o = over_tiles(
        functools.partial(rec_out, nc), tiles,
        [(cut, a) for a in (zin, rr, kr, vr, al, gg, vec, reff, oloc, w1, w2, mv)]
        + [(whole, tokens), (cut, mats[3]), (cut, down(3)), (whole, up(3)), (whole, vec)],
        [(cut, low), (cut, full), (cut, full), (cut, full), (whole, full), (whole, full), (whole, shape((length, RANK), BF))],
        "rec_out",
        [pltpu.VMEM((length, RANK), F32)],
    )
    result, d_mc, moved, g_hidden, up_f, down_c = channel(
        n2, shifted(n2[-1:], "seq", 1), vec, gy, middle, down(4), up(4), kv, hidden
    )
    d_mid, dz, do, dgg, es, eloc, down_o, up_o = over_tiles(
        functools.partial(back_local, nc), tiles,
        [
            (whole, d_mc), (whole, shifted(moved[:1], "seq", -1)), (whole, gy), (whole, middle), (whole, vec),
            (cut, mats[3]), (cut, down(3)), (whole, down(3)), (whole, up(3)), (whole, h_o),
        ]
        + [(cut, a) for a in (gated, gg, o, rr, kr, vr, al, vec, reff, mt)],
        [(whole, full), (cut, full), (cut, full), (cut, low), (cut, full), (cut, small), (cut, rank), (whole, rank)],
        "back_local",
        [pltpu.VMEM((length, width), BF), pltpu.VMEM((length, RANK), BF)],
    )
    wide = n_dp * cols
    early = jnp.concatenate([down_o, down_c, up_o, up_f], 0)
    early = jnp.swapaxes(early.reshape(4 * RANK, n_seq, wide), 0, 1)
    early = jnp.concatenate([early, g_hidden.reshape(n_seq, -1, wide)], 1)
    early = lax.psum_scatter(early, "seq", scatter_dimension=0, tiled=True)[0]
    hin = pass_states(n_seq, piece[2], eloc, True)
    drr, dkr, dvr, dwl, dal = over_tiles(
        functools.partial(rec_back, nc), tiles,
        [(cut, a) for a in (hin, dz, gg, do, rr, kr, vr, wl, al, vec, xs, us, zs, mt, es)],
        [(cut, low)] * 5, "rec_back",
    )
    early, drr = lax.optimization_barrier((early, drr))
    dhs, d_act, late = over_tiles(
        late_kernel, 1,
        [(whole, a) for a in (drr, dkr, dvr, dwl, dal, dgg, m_r, m_k, m_v, hs, act, chosen)] + [(seconds, misc)],
        [
            (whole, shape((3, length, RANK), BF)),
            (whole, shape((3, length, HALF), BF)),
            (whole, shape((n_seq, 6 * RANK, wide), F32)),
        ],
        "late",
    )
    stay, go, late = over_tiles(
        functools.partial(final_kernel, n_seq), tiles,
        [
            (whole, drr), (whole, dkr), (whole, dvr), (cut, mats[0]), (cut, mats[1]), (cut, mats[2]),
            (whole, dhs), (cut, chosen), (whole, d_act), (first_rows, misc), (cut, vec), (whole, late),
        ],
        [(cut, full)] * 2 + [(whole, shape((6 * RANK, wide), F32))], "final",
        [
            pltpu.VMEM((n_seq - 1, 6 * RANK, wide), F32),
            pltpu.SemaphoreType.DMA((n_seq - 1,)),
            pltpu.SemaphoreType.DMA((n_seq - 1,)),
        ],
        collective_id=3, has_side_effects=True,
    )
    d_n1 = stay + jnp.concatenate([go[1:], shifted(go[:1], "seq", -1)], 0)
    dhat = d_n1 * vec[0:1]
    grad_tokens = d_mid + rstd * (
        dhat
        - jnp.mean(dhat, axis=-1, keepdims=True)
        - hat * jnp.mean(dhat * hat, axis=-1, keepdims=True)
    )

    columns = jnp.concatenate([early[: 4 * RANK], late], 0).reshape(10 * RANK, n_dp, cols)
    both = jnp.concatenate(
        [jnp.swapaxes(columns, 0, 1).reshape(n_dp, -1), early[4 * RANK :].reshape(n_dp, -1)], 1
    )
    both = lax.all_to_all(both, "dp", split_axis=0, concat_axis=0, tiled=True)
    both = jnp.einsum("sa,sx->ax", pick.astype(F32), both, precision=PRECISE)
    at = 10 * RANK * cols
    a = both[:, :at].reshape(adapters, 10 * RANK, cols)
    h = both[:, at:].reshape(adapters, 2 * RANK, ff)
    grad_model = jnp.concatenate(
        [a[:, 4 * RANK : 7 * RANK], a[:, : 2 * RANK], a[:, 7 * RANK :], a[:, 2 * RANK : 4 * RANK]], axis=1
    )
    return result[None], grad_tokens[None], grad_model, h


def solution(mesh):
    cols = P(None, ("seq", "dp"))
    rows = P(("seq", "dp"), None)
    deep = P(None, None, ("seq", "dp"))
    act = P("dp", "seq", None)
    return jax.shard_map(
        body,
        mesh=mesh,
        in_specs=(act, act, P("dp"), deep, rows, cols, cols, cols, rows, deep, deep),
        out_specs=(act, act, deep, deep),
        check_vma=False,
    )
```

```python
import functools
import math

import jax
import jax.numpy as jnp
from jax import lax
from jax.experimental import pallas as pl
from jax.experimental.pallas import tpu as pltpu
from jax.sharding import PartitionSpec as P

F32, BF = jnp.float32, jnp.bfloat16
MESH = pl.DeviceIdType.MESH
D = 64
C = 64
PW = 2 * D
DECAY_INNER, RATE_INNER, GATE_INNER, RANK = 96, 96, 256, 16
SCALE = 4.0
NORM_EPS, GROUP_EPS, UNIT_EPS = 1e-05, 0.00064, 1e-06
DECAY_SCALE = math.exp(-0.5)
PRECISE = lax.Precision.HIGHEST
DIMS = {
    "nn": (((1,), (0,)), ((), ())),
    "nt": (((1,), (1,)), ((), ())),
    "tn": (((0,), (0,)), ((), ())),
}


def split(x):
    hi = x.astype(BF)
    return hi, (x - hi.astype(F32)).astype(BF)


def dot1(a, b, m="nn"):
    return lax.dot_general(a.astype(BF), b.astype(BF), DIMS[m], preferred_element_type=F32)


def dot3(a, b, m="nn"):
    ah, al = split(a)
    bh, bl = split(b)
    ka, kb = (0 if m == "tn" else 1), (1 if m == "nt" else 0)
    n = b.shape[1 - kb]
    aa = jnp.concatenate([ah, al], axis=ka)
    bb = jnp.concatenate([jnp.concatenate([bh, bl], axis=1 - kb)] * 2, axis=kb)
    r = lax.dot_general(aa, bb, DIMS[m], preferred_element_type=F32)
    return r[:, :n] + r[:, n:]


dot_inv = dot_a = dot_w = dot_b = dot_g = dot3


def iota(shape, axis):
    return lax.broadcasted_iota(jnp.int32, shape, axis)


def stack2(x):
    lane = iota(x.shape, 1)
    zero = jnp.zeros_like(x)
    return jnp.concatenate([jnp.where(lane < D, x, zero), jnp.where(lane < D, zero, x)], axis=0)


def pack2(x):
    h = x.shape[0] // 2
    return x[:h] + x[h:]


def head_ones():
    r, c = iota((2 * PW, PW), 0) % PW, iota((2 * PW, PW), 1)
    return jnp.where((r // D) == (c // D), 1.0, 0.0).astype(BF)


def headsum(x, ones):
    h, l = split(x)
    return lax.dot_general(
        jnp.concatenate([h, l], axis=1), ones, DIMS["nn"], preferred_element_type=F32
    )


def triangle(upper):
    r, c = iota((C, C), 0), iota((C, C), 1)
    return jnp.where((r <= c) if upper else (r >= c), 1.0, 0.0).astype(BF)


def cums(x, tri):
    h, l = split(x)
    m = (x - h.astype(F32) - l.astype(F32)).astype(BF)
    n = x.shape[1]
    r = lax.dot_general(
        tri, jnp.concatenate([h, l, m], axis=1), DIMS["nn"], preferred_element_type=F32
    )
    return r[:, :n] + r[:, n : 2 * n] + r[:, 2 * n :]


def prelude(kr, wl, al, w0, a0, k_k, k_a, ones):
    s = jax.nn.sigmoid(w0 + wl)
    a = jax.nn.sigmoid(a0 + al)
    kx = kr * k_k
    rn = lax.rsqrt(headsum(kx * kx, ones) + UNIT_EPS)
    return s, -DECAY_SCALE * s, a, rn, kx * rn, kr * (1.0 + (a - 1.0) * k_a)


def grid_ids():
    r, c = iota((PW, PW), 0), iota((PW, PW), 1)
    return r, c, (r // D) == (c // D)


def inverses(many):
    r, c, _ = grid_ids()
    eye = jnp.where(r == c, 1.0, 0.0)
    b = 1
    while b < C:
        level = ((r // (2 * b)) == (c // (2 * b))) & ((r // b) % 2 == 1) & ((c // b) % 2 == 0)
        parts = [jnp.where(level, a, 0.0) for a in many]
        if b == 1:
            xs = [eye + p for p in parts]
        else:
            half = [dot_inv(x, p) for x, p in zip(xs, parts)]
            xs = [x + dot_inv(h, x) for h, x in zip(half, xs)]
        b *= 2
    return xs


def factors(logw, tri):
    run = cums(logw, tri)
    return jnp.exp(run - logw), jnp.exp(run), jnp.exp(-run), jnp.exp(run[C - 1 : C])


def forward_chunks(units, tri):
    rows, cols, same = grid_ids()
    zero = jnp.zeros((PW, PW), F32)
    strict, incl = (rows > cols) & same, (rows >= cols) & same
    fs = [factors(u[5], tri) for u in units]
    p2 = [stack2(u[1] * f[0]) for u, f in zip(units, fs)]
    r2 = [stack2(u[0] * f[1]) for u, f in zip(units, fs)]
    q2 = [stack2(u[2] * f[2]) for u, f in zip(units, fs)]
    k2 = [stack2(u[3] * f[2]) for u, f in zip(units, fs)]
    v2 = [stack2(u[4]) for u in units]
    aa = [
        dot_a(jnp.concatenate([p, r], 0), jnp.concatenate([q, k], 0), "nt")
        for p, r, q, k in zip(p2, r2, q2, k2)
    ]
    apk = [jnp.where(strict, a[:PW, PW:], zero) for a in aa]
    y = [dot_w(a, v) for a, v in zip(apk, v2)]
    xs = inverses([jnp.where(strict, a[:PW, :PW], zero) for a in aa])
    ww = [dot_w(x, jnp.concatenate([p, t], 1)) for x, p, t in zip(xs, p2, y)]
    left = [
        jnp.concatenate(
            [
                jnp.concatenate(
                    [jnp.where(incl, a[PW:, :PW], zero), jnp.where(incl, a[PW:, PW:], zero)], 1
                ),
                jnp.concatenate([(q * f[3]).T, (k * f[3]).T], 1),
            ],
            0,
        )
        for a, q, k, f in zip(aa, q2, k2, fs)
    ]
    right = [
        jnp.concatenate([w, jnp.concatenate([zero, v], 1)], 0) for w, v in zip(ww, v2)
    ]
    big = [dot_b(l, r) for l, r in zip(left, right)]
    move = [
        b[PW:, :PW] + jnp.where(rows == cols, jnp.broadcast_to(f[3], (PW, PW)), zero)
        for b, f in zip(big, fs)
    ]
    return [
        (pack2(r + b[:PW, :PW]), pack2(b[:PW, PW:]), m, b[PW:, PW:], pack2(w[:, :PW]), pack2(w[:, PW:]), x)
        for r, b, m, w, x in zip(r2, big, move, ww, xs)
    ]


def backward_chunks(units, tri, tri_up):
    rows, cols, same = grid_ids()
    zero = jnp.zeros((PW, PW), F32)
    strict, incl = (rows < cols) & same, (rows <= cols) & same
    both = jnp.concatenate([jnp.concatenate([strict, incl], 1)] * 2, 0)
    fs = [factors(t[5], tri) for t in units]
    pe = [t[1] * f[0] for t, f in zip(units, fs)]
    re = [t[0] * f[1] for t, f in zip(units, fs)]
    qe = [t[2] * f[2] for t, f in zip(units, fs)]
    ke = [t[3] * f[2] for t, f in zip(units, fs)]
    g2 = [stack2(t[10]) for t in units]
    qk = [jnp.concatenate([stack2(q), stack2(k)], 0) for q, k in zip(qe, ke)]
    pr = [jnp.concatenate([stack2(p), stack2(r)], 0) for p, r in zip(pe, re)]
    at = [dot_a(a, b, "nt") for a, b in zip(qk, pr)]
    qkh = [
        dot_g(jnp.concatenate([q * f[3], k * f[3]], 0), t[9])
        for q, k, f, t in zip(qe, ke, fs, units)
    ]
    sq = [dot_g(jnp.concatenate([t[7], t[4]], 0), t[9], "nt") for t in units]
    du = [
        dot_g(jnp.where(incl, a[:PW, PW:], zero), g) + stack2(h[:C])
        for a, g, h in zip(at, g2, qkh)
    ]
    dm = [dot_g(t[6], d, "tn") for t, d in zip(units, du)]
    dg = [jnp.concatenate([d, g], 0) for d, g in zip(dm, g2)]
    dv = [
        pack2(
            dot_g(
                jnp.concatenate(
                    [jnp.where(strict, a[PW:, :PW], zero), jnp.where(incl, a[PW:, PW:], zero)], 1
                ),
                d,
            )
        )
        + h[C:]
        for a, d, h in zip(at, dg, qkh)
    ]
    dat = [
        dot_g(jnp.concatenate([stack2(t[7]), stack2(t[4])], 0), d, "nt")
        for t, d in zip(units, dg)
    ]
    dat = [jnp.where(both, d, jnp.zeros_like(d)) for d in dat]
    dpr = [dot_g(d, a, "tn") for d, a in zip(dat, qk)]
    dqk = [dot_g(d, a) for d, a in zip(dat, pr)]
    sp = [dot_g(jnp.concatenate([pack2(d), t[10]], 0), t[8], "nt") for d, t in zip(dm, units)]
    outs = []
    for i, t in enumerate(units):
        eb, el, en, last = fs[i]
        dp, dr = pack2(dpr[i][:PW]) + sp[i][:C], pack2(dpr[i][PW:]) + sp[i][C:]
        dqh, dkh = sq[i][:C], sq[i][C:]
        dq, dk = pack2(dqk[i][:PW]) + dqh * last, pack2(dqk[i][PW:]) + dkh * last
        tail = jnp.sum((qe[i] * dqh + ke[i] * dkh) * last, axis=0, keepdims=True)
        tail = tail + last * jnp.sum((t[8] * t[9]).T, axis=0, keepdims=True)
        gb = pe[i] * dp
        gl = re[i] * dr - qe[i] * dq - ke[i] * dk
        dlogw = cums(gl + gb, tri_up) - gb + tail
        outs.append((dr * el, dp * eb, dq * en, dk * en, dv[i], dlogw))
    return outs


def lanes(ref):
    return [slice(i * PW, (i + 1) * PW) for i in range(ref.shape[-1] // PW)]


def norm_parts(o, ones):
    centre = o - headsum(o, ones) * (1.0 / D)
    rstd = lax.rsqrt(headsum(centre * centre, ones) * (1.0 / D) + GROUP_EPS)
    return centre * rstd, rstd


def hand_on(n, half, back, move, add, here, send, send_sem, recv_sem):
    step, last = pl.program_id(0), pl.num_programs(0) - 1
    s, d = lax.axis_index("seq"), lax.axis_index("dp")
    at = n - 1 - s if back else s
    first, final = at == 0, at == n - 1
    nxt, prv = (s - 1, s + 1) if back else (s + 1, s - 1)
    begins, goes = jnp.logical_not(first), jnp.logical_not(final)
    tile = step - jnp.minimum(at, half)
    now = jnp.logical_and(tile >= 0, tile < half)

    def copy(i, to):
        return pltpu.make_async_remote_copy(
            src_ref=send.at[i],
            dst_ref=here.at[i],
            send_sem=send_sem.at[i],
            recv_sem=recv_sem.at[i],
            device_id=(to, d),
            device_id_type=MESH,
        )

    @pl.when(jnp.logical_and(step == 0, begins))
    def _():
        pl.semaphore_signal(
            pltpu.get_barrier_semaphore(), inc=1, device_id=(prv, d), device_id_type=MESH
        )

    @pl.when(jnp.logical_and(step == 0, goes))
    def _():
        pl.semaphore_wait(pltpu.get_barrier_semaphore(), 1)

    @pl.when(jnp.logical_and(now, first))
    def _():
        here[tile] = jnp.zeros(here.shape[1:], F32)

    @pl.when(jnp.logical_and(now, begins))
    def _():
        copy(tile, prv).wait_recv()

    @pl.when(jnp.logical_and(now, goes))
    def _():
        for ln in lanes(here):
            send[tile, :, ln] = dot3(move[tile, :, ln], stack2(here[tile, :, ln])) + add[tile, :, ln]
        copy(tile, nxt).start()

    @pl.when(jnp.logical_and(step == last, goes))
    def _():
        for i in range(half):
            copy(i, nxt).wait_send()


def hand_scratch(steps):
    return [
        pltpu.VMEM((steps, D, TILE), F32),
        pltpu.VMEM((steps, D, TILE), F32),
        pltpu.SemaphoreType.DMA((steps,)),
        pltpu.SemaphoreType.DMA((steps,)),
    ]


def rec_forward(
    nc, n, half, rr, kr, vr, wl, al, gg, vec, tokens, wo, down, up, norm,
    reff, xs, mt, turned, z_out, o_out, u_out, zs, middle, normed, h_out,
    k_reff, k_oloc, k_w1, k_w2, k_m, k_n, move, add, acc_h, *hand,
):
    step, last = pl.program_id(0), pl.num_programs(0) - 1
    ones = head_ones()

    @pl.when(step < half)
    def _():
        tri = triangle(False)
        units, where = [], []
        for ln in lanes(rr):
            row = lambda i: vec[i : i + 1, ln]
            _, logw, a, _, kk, km = prelude(
                kr[:, ln], wl[:, ln], al[:, ln], row(8), row(9), row(10), row(11), ones
            )
            r, v, q = rr[:, ln], vr[:, ln], kk * a
            for c in range(nc):
                s = slice(c * C, (c + 1) * C)
                units.append((r[s], -kk[s], q[s], km[s], v[s], logw[s]))
                where.append((s, ln))
        done = forward_chunks(units, tri)
        packed = []
        for (s, ln), (e, o, m, z, y1, y2, x) in zip(where, done):
            reff[s, ln] = e
            k_reff[step, s, ln], k_oloc[step, s, ln] = e, o
            k_w1[step, s, ln], k_w2[step, s, ln] = y1, y2
            xs[s, ln] = pack2(x)
            mp = pack2(m)
            k_m[step, s, ln], k_n[step, s, ln], mt[s, ln] = mp, pack2(z), pack2(m.T)
            packed.append(mp)
        for i, ln in enumerate(lanes(rr)):
            tm, tn = stack2(packed[i * nc]), done[i * nc][3]
            for c in range(1, nc):
                t = dot3(packed[i * nc + c], jnp.concatenate([tm, tn], 1))
                tm, tn = stack2(t[:, :PW]), stack2(t[:, PW:]) + done[i * nc + c][3]
            move[step, :, ln], add[step, :, ln], turned[:, ln] = pack2(tm), pack2(tn), pack2(tm.T)

    hand_on(n, half, False, move, add, *hand)

    @pl.when(step >= half)
    def _():
        t = step - half
        here = hand[0]
        state = [here[t, :, ln] for ln in lanes(rr)]
        for c in range(nc):
            s = slice(c * C, (c + 1) * C)
            ts = [
                dot3(jnp.concatenate([k_m[t, s, ln], k_reff[t, s, ln], k_w1[t, s, ln]], 0), stack2(z))
                for z, ln in zip(state, lanes(rr))
            ]
            for i, (y, ln) in enumerate(zip(ts, lanes(rr))):
                zs[s, ln] = state[i]
                o_out[s, ln] = y[C : 2 * C] + k_oloc[t, s, ln]
                u_out[s, ln] = y[2 * C :] + k_w2[t, s, ln]
                state[i] = y[:C] + k_n[t, s, ln]
        for ln in lanes(rr):
            row = lambda i: vec[i : i + 1, ln]
            a = jax.nn.sigmoid(row(9) + al[:, ln])
            km = kr[:, ln] * (1.0 + (a - 1.0) * row(11))
            hat, _ = norm_parts(o_out[:, ln], ones)
            y = hat * row(13) + row(14) + headsum(rr[:, ln] * km * row(12), ones) * vr[:, ln]
            z_out[:, ln] = (y * gg[:, ln]).astype(BF)

        @pl.when(step == half)
        def _():
            acc_h[...] = jnp.zeros_like(acc_h)
            middle[...] = tokens[...].astype(F32)

        acc_h[...] += mm_nt(z_out[...], down[...])
        middle[...] += mm_nt(z_out[...], wo[...])

    @pl.when(step == last)
    def _():
        h_out[...] = acc_h[...].astype(BF)
        x1 = middle[...] + SCALE * mm(h_out[...], up[...])
        middle[...] = x1
        centre = x1 - jnp.mean(x1, axis=-1, keepdims=True)
        rstd = lax.rsqrt(jnp.mean(centre * centre, axis=-1, keepdims=True) + NORM_EPS)
        normed[...] = centre * rstd * norm[15:16, :] + norm[16:17, :]


def rec_backward(
    nc, n, half, d_mc, edge, gy, middle, norm, wo, down, up, h_o, gated, gg, o, rr, kr, vr, wl, al, vec,
    reff, mt, turned, xs, us, zs,
    d_mid, dgg, g_down, g_up, drr, dkr, dvr, dwl, dal,
    low, dh, k_dy, k_do, k_es, move, add, *hand,
):
    step = pl.program_id(0)
    ones = head_ones()

    @pl.when(step == 0)
    def _():
        moved = d_mc[...] * norm[17:18, :]
        size = moved.shape[0]
        up_one = pltpu.roll(moved, size - 1, axis=0)
        up_one = jnp.where(iota(moved.shape, 0) == size - 1, edge[0:1, :], up_one)
        dn = d_mc[...] - moved + up_one
        x1 = middle[...]
        centre = x1 - jnp.mean(x1, axis=-1, keepdims=True)
        rstd = lax.rsqrt(jnp.mean(centre * centre, axis=-1, keepdims=True) + NORM_EPS)
        hat = centre * rstd
        dhat = dn * norm[15:16, :]
        d = rstd * (
            dhat
            - jnp.mean(dhat, axis=-1, keepdims=True)
            - hat * jnp.mean(dhat * hat, axis=-1, keepdims=True)
        )
        d = d + gy[...].astype(F32)
        d_mid[...] = d
        low[...] = d.astype(BF)
        dh[...] = (SCALE * mm_nt(low[...], up[...])).astype(BF)
        g_up[...] = SCALE * mm_tn(h_o[...], low[...])

    @pl.when(step < half)
    def _():
        dz = mm(low[...], wo[...]) + mm(dh[...], down[...])
        g_down[...] = mm_tn(dh[...], gated[...])
        _, _, same = grid_ids()
        for ln in lanes(rr):
            row = lambda i: vec[i : i + 1, ln]
            a = jax.nn.sigmoid(row(9) + al[:, ln])
            km = kr[:, ln] * (1.0 + (a - 1.0) * row(11))
            hat, rstd = norm_parts(o[:, ln], ones)
            y = hat * row(13) + row(14) + headsum(rr[:, ln] * km * row(12), ones) * vr[:, ln]
            dgg[:, ln] = (dz[:, ln] * y).astype(BF)
            dy = dz[:, ln] * gg[:, ln]
            k_dy[step, :, ln] = dy
            dhat = dy * row(13)
            k_do[step, :, ln] = rstd * (
                dhat
                - headsum(dhat, ones) * (1.0 / D)
                - hat * (headsum(dhat * hat, ones) * (1.0 / D))
            )
        es = {}
        for c in range(nc):
            s = slice(c * C, (c + 1) * C)
            for ln in lanes(rr):
                e = pack2(jnp.where(same, dot3(reff[s, ln], k_do[step, s, ln], "tn"), 0.0))
                k_es[step, s, ln] = e
                es[c, ln.start] = e
        state = [es[nc - 1, ln.start] for ln in lanes(rr)]
        for c in reversed(range(nc - 1)):
            s = slice(c * C, (c + 1) * C)
            state = [es[c, ln.start] + dot3(mt[s, ln], stack2(h)) for h, ln in zip(state, lanes(rr))]
        for h, ln in zip(state, lanes(rr)):
            add[step, :, ln] = h
            move[step, :, ln] = turned[:, ln]

    hand_on(n, half, True, move, add, *hand)

    @pl.when(step >= half)
    def _():
        t = step - half
        tri, tri_up = triangle(False), triangle(True)
        units, where, pre = [], [], []
        hs = {}
        for ln in lanes(rr):
            h = hand[0][t, :, ln]
            for c in reversed(range(nc)):
                s = slice(c * C, (c + 1) * C)
                hs[c, ln.start] = stack2(h)
                if c:
                    h = dot3(mt[s, ln], hs[c, ln.start]) + k_es[t, s, ln]
        for ln in lanes(rr):
            row = lambda i: vec[i : i + 1, ln]
            for c in range(nc):
                s = slice(c * C, (c + 1) * C)
                r, v, k = rr[s, ln], vr[s, ln], kr[s, ln]
                sg, logw, a, rn, kk, km = prelude(
                    k, wl[s, ln], al[s, ln], row(8), row(9), row(10), row(11), ones
                )
                units.append(
                    (r, -kk, kk * a, km, v, logw, stack2(xs[s, ln]), us[s, ln], stack2(zs[s, ln]),
                     hs[c, ln.start], k_do[t, s, ln])
                )
                where.append((s, ln))
                pre.append((sg, a, rn, kk, km))
        done = backward_chunks(units, tri, tri_up)
        for (s, ln), (sg, a, rn, kk, km), (dr, dp, dq, dk, dv, dlogw) in zip(where, pre, done):
            row = lambda i: vec[i : i + 1, ln]
            r, v, k = rr[s, ln], vr[s, ln], kr[s, ln]
            dy = k_dy[t, s, ln]
            dv = dv + headsum(r * km * row(12), ones) * dy
            ds = headsum(dy * v, ones) * row(12)
            dr = dr + ds * km
            dkm = dk + ds * r
            dkk = dq * a - dp
            da = dq * kk + dkm * k * row(11)
            dk = dkm * (1.0 + (a - 1.0) * row(11)) + row(10) * rn * (dkk - kk * headsum(dkk * kk, ones))
            drr[s, ln], dkr[s, ln], dvr[s, ln] = dr.astype(BF), dk.astype(BF), dv.astype(BF)
            dwl[s, ln] = (dlogw * (-DECAY_SCALE) * sg * (1.0 - sg)).astype(BF)
            dal[s, ln] = (da * a * (1.0 - a)).astype(BF)


TILE = 2 * PW


def cut(shape):
    lead = tuple(shape[:-1])
    return pl.BlockSpec(lead + (TILE,), lambda i, n=len(lead): (0,) * n + (i,))


def whole(shape):
    return pl.BlockSpec(tuple(shape), lambda i, n=len(shape): (0,) * n, pipeline_mode=pl.Buffered(1))


def result(shape):
    return pl.BlockSpec(tuple(shape), lambda i, n=len(shape): (0,) * n)


def in_turn(half, which):
    def spec(shape):
        lead = tuple(shape[:-1])
        place = {
            "first": lambda i: jnp.minimum(i, half - 1),
            "second": lambda i: jnp.maximum(i - half, 0),
            "both": lambda i: lax.rem(i, half),
        }[which]
        return pl.BlockSpec(lead + (TILE,), lambda i: (0,) * len(lead) + (place(i),))

    return spec


def tile_rows(shape):
    return pl.BlockSpec((TILE, shape[1]), lambda i: (i, 0))


def over_tiles(body, steps, ins, outs, name, scratch=(), **params):
    made = lambda spec, shape: spec if isinstance(spec, pl.BlockSpec) else spec(shape)
    return pl.pallas_call(
        body,
        grid=(steps,),
        in_specs=[made(spec, x.shape) for spec, x in ins],
        out_specs=[made(spec, x.shape) for spec, x in outs],
        out_shape=[x for _, x in outs],
        scratch_shapes=list(scratch),
        compiler_params=pltpu.CompilerParams(vmem_limit_bytes=60 * 1024 * 1024, **params),
        name=name,
    )(*[x for _, x in ins])


ORDERS = ("zxy", "zyx", "xzy", "yzx")
DIRS = "xyuds"


def gather_events(order, z, x, y):
    other = {"x": lambda q: (q, 1 - x, y), "y": lambda q: (q, x, 1 - y), "z": lambda q: (q, x, y)}
    inside = lambda k: None if k == 0 else jnp.logical_and(z + k >= 0, z + k <= 3)
    if order[0] == "z":
        a, b = order[1], order[2]
        events = [(0, (z, x, y), None, None, [a, b, "u", "d", "s"])]
        for k in (1, 2, 3):
            events.append((k, (z - k, x, y), "u", z >= k, ["u", a, b, "s"]))
            events.append((k, (z + k, x, y), "d", z + k <= 3, ["d", a, b, "s"]))
        for k in range(-3, 4):
            events.append((abs(k) + 1, other[a](z + k), a, inside(k), [b, "s"]))
    else:
        a, b = order[0], order[2]
        events = [(0, (z, x, y), None, None, [a, "u", "d", b, "s"])]
        events.append((1, other[a](z), a, None, ["u", "d", b, "s"]))
        for k in (1, 2, 3):
            for late, at in ((0, other["z"]), (1, other[a])):
                events.append((k + late, at(z - k), "u", z >= k, ["u", b, "s"]))
                events.append((k + late, at(z + k), "d", z + k <= 3, ["d", b, "s"]))
    for k in range(-3, 4):
        events.append((abs(k) + 1, other[b](z + k), b, inside(k), ["s"]))
        events.append((abs(k) + 2, (z + k, 1 - x, 1 - y), b, inside(k), ["s"]))
    return events


def maybe(condition, run):
    if condition is None:
        run()
    else:
        pl.when(condition)(run)


class Gathering:
    def __init__(self, orders, steps, shards, whole, send, recv, near):
        self.shards, self.whole, self.send, self.recv, self.near = shards, whole, send, recv, near
        seq, dp = lax.axis_index("seq"), lax.axis_index("dp")
        z, x, y, self.c = seq // 2, seq % 2, dp // 2, dp % 2
        self.z = z
        self.to = {
            "x": (z * 2 + 1 - x, dp),
            "y": (seq, (1 - y) * 2 + self.c),
            "u": (seq + 2, dp),
            "d": (seq - 2, dp),
            "s": (seq, y * 2 + 1 - self.c),
        }
        self.exists = {"u": z < 3, "d": z > 0}
        todo = [
            (steps[t][i] if steps else e[0], t, e)
            for t, o in enumerate(orders)
            for i, e in enumerate(gather_events(o, z, x, y))
        ]
        todo.sort(key=lambda q: q[0])
        self.todo = todo
        self.times = sorted({q[0] for q in todo})

    def enter(self, beside=None, count=0):
        barrier = pltpu.get_barrier_semaphore()
        if beside is not None:
            pl.when(count == 1)(
                lambda: pl.semaphore_signal(barrier, inc=1, device_id=beside, device_id_type=MESH)
            )
        for k in DIRS:
            maybe(
                self.exists.get(k),
                lambda k=k: pl.semaphore_signal(
                    barrier, inc=1, device_id=self.to[k], device_id_type=MESH
                ),
            )
        pl.semaphore_wait(barrier, 3 + (self.z + 2) // 3 + (5 - self.z) // 3 + count)

    def chip(self, b):
        return b[0] * 4 + b[1] * 2 + b[2]

    def copy(self, t, own, b, k):
        slot = self.whole[t].at[self.chip(b) * 2 + self.c]
        return pltpu.make_async_remote_copy(
            src_ref=self.shards[t] if own else slot,
            dst_ref=slot,
            send_sem=self.send.at[DIRS.index(k), t, self.chip(b)],
            recv_sem=self.recv.at[1 if k == "s" else 0, t, self.chip(b)],
            device_id=self.to[k],
            device_id_type=MESH,
        )

    def local(self, t, b):
        return pltpu.make_async_copy(
            self.shards[t], self.whole[t].at[self.chip(b) * 2 + self.c], self.near.at[t]
        )

    def goes(self, event):
        _, b, came, condition, ways = event
        for k in ways:
            both = self.exists.get(k) if condition is None else condition
            if condition is not None and k in self.exists:
                both = jnp.logical_and(condition, self.exists[k])
            yield b, came is None, k, both

    def take(self, time):
        for at, t, event in self.todo:
            if at != time:
                continue
            _, b, came, condition, _ = event
            if came is None:
                self.local(t, b).start()
            else:
                maybe(condition, lambda: self.copy(t, False, b, came).wait_recv())
            for _, own, k, both in self.goes(event):
                maybe(both, lambda: self.copy(t, own, b, k).start())

    def finish(self):
        for t in range(len(self.shards)):
            for i in range(16):
                pltpu.make_async_remote_copy(
                    src_ref=self.shards[t],
                    dst_ref=self.whole[t].at[i * 2 + 1 - self.c],
                    send_sem=self.send.at[4, t, i],
                    recv_sem=self.recv.at[1, t, i],
                    device_id=self.to["s"],
                    device_id_type=MESH,
                ).wait_recv()
        for _, t, event in self.todo:
            for b, own, k, both in self.goes(event):
                maybe(both, lambda: self.copy(t, own, b, k).wait_send())
            if event[2] is None:
                self.local(t, event[1]).wait()


def gather_scratch(n):
    return [
        pltpu.SemaphoreType.DMA((5, n, 16)),
        pltpu.SemaphoreType.DMA((2, n, 16)),
        pltpu.SemaphoreType.DMA((n,)),
    ]


def gather_kernel(orders, *refs):
    n = len(orders)
    g = Gathering(orders, None, refs[:n], refs[n : 2 * n], *refs[2 * n :])
    g.enter()
    for time in g.times:
        g.take(time)
    g.finish()


def gather(shards):
    n_seq, n_dp, n = lax.axis_size("seq"), lax.axis_size("dp"), len(shards)
    if (n_seq, n_dp) != (8, 4):
        return [lax.all_gather(s, ("seq", "dp"), axis=0) for s in shards]
    return pl.pallas_call(
        functools.partial(gather_kernel, [ORDERS[i % len(ORDERS)] for i in range(n)]),
        out_shape=[jax.ShapeDtypeStruct((n_seq * n_dp,) + s.shape, s.dtype) for s in shards],
        in_specs=[pl.BlockSpec(memory_space=pl.ANY)] * n,
        out_specs=[pl.BlockSpec(memory_space=pl.ANY)] * n,
        scratch_shapes=gather_scratch(n),
        compiler_params=pltpu.CompilerParams(collective_id=2, has_side_effects=True),
        name="gather_time",
    )(*shards)


LATE_ORDERS = ("zxy", "yzx")
LATE_STEPS = (
    (0, 2, 2, 4, 4, 7, 7, 11, 9, 4, 2, 5, 9, 11, 9, 13, 7, 11, 4, 8, 2, 6, 5, 9, 7, 11, 9, 13),
    (0, 3, 3, 3, 5, 5, 6, 6, 8, 8, 9, 9, 11, 11, 13, 14, 13, 14, 7, 11, 3, 6, 8, 12, 13, 14, 13, 14),
)


def channel_kernel(
    late, n2, edge, norm, gy, middle, down_c, up_f, kv, hidden, *refs,
):
    if late:
        key_shard, value_shard, hidden_late, *refs = refs
    out, dmc, first, g_hidden, g_up_f, g_down_c, *refs = refs
    if late:
        g_late, d_edge, *refs = refs
    mc, mct, gyt, ffo, h_c, dh_f, acc_f, acc_c, *refs = refs
    step, last = pl.program_id(0), pl.num_programs(0) - 1
    per, ff = kv.shape[0], kv.shape[1] // 2
    if late:
        key_late, value_late, mine, came, edge_sem, *sems = refs
        g = Gathering(LATE_ORDERS, LATE_STEPS, (key_shard, value_shard), (key_late, value_late), *sems)
        seq, dp = lax.axis_index("seq"), lax.axis_index("dp")
        x, z = seq % 2, seq // 2
        beside = seq + 2 * x - 1
        count = (1 - x) * ((z + 2) // 3) + x * ((5 - z) // 3)
        starts, ends = seq == 0, seq == 7

        def edges(i, to):
            return pltpu.make_async_remote_copy(
                src_ref=mine.at[i],
                dst_ref=came.at[i],
                send_sem=edge_sem.at[0, i],
                recv_sem=edge_sem.at[1, i],
                device_id=(to, dp),
                device_id_type=MESH,
            )

        def trade(i, has_from, has_to, shift):
            pl.when(has_to)(lambda: edges(i, seq + shift).start())
            pl.when(has_from)(lambda: edges(i, seq - shift).wait_recv())
            pl.when(has_to)(lambda: edges(i, seq + shift).wait_send())

        @pl.when(step == 0)
        def _():
            came[...] = jnp.zeros_like(came)
            g.enter((beside, dp), count)
            size = n2.shape[0]
            mine[0] = n2[size - 8 :, :]

        for time in g.times:

            @pl.when(step == time)
            def _():
                g.take(time)

        @pl.when(step == 0)
        def _():
            trade(0, jnp.logical_not(starts), jnp.logical_not(ends), 1)

    @pl.when(step == 0)
    def _():
        x = n2[...]
        row = came[0, 7:8, :] if late else edge[...]
        before = jnp.where(iota(x.shape, 0) == 0, row, pltpu.roll(x, 1, axis=0))
        m = x + (before - x) * norm[17:18, :]
        mc[...] = m.astype(BF)
        mct[...] = m.T.astype(BF)
        gyt[...] = gy[...].astype(F32).T.astype(BF)
        h_c[...] = mm_nt(down_c[...], mc[...]).astype(BF)
        dh_f[...] = (SCALE * mm_nt(up_f[...], gy[...])).astype(BF)
        acc_f[...] = jnp.zeros_like(acc_f)
        acc_c[...] = jnp.zeros_like(acc_c)
        ffo[...] = jnp.zeros_like(ffo)
        dmc[...] = jnp.zeros_like(dmc)

    def units(key, value, smalls):
        pre, dsq = mm(key, mct[...]), mm(value, gyt[...])
        rows = key.shape[0] // len(smalls)
        hqs, dps, grads = [], [], []
        for b, small in enumerate(smalls):
            s = slice(b * rows, (b + 1) * rows)
            down_f, up_c = small[:RANK], small[RANK:]
            active = jnp.maximum(pre[s] + SCALE * mm_tn(up_c, h_c[...]), 0.0)
            hq = (active * active).astype(BF)
            dpre = ((dsq[s] + mm_tn(down_f, dh_f[...])) * (2.0 * active)).astype(BF)
            grads.append((mm_nt(dh_f[...], hq), SCALE * mm_nt(h_c[...], dpre)))
            acc_f[...] += mm(down_f, hq)
            acc_c[...] += mm(up_c, dpre)
            hqs.append(hq)
            dps.append(dpre)
        ffo[...] += mm_tn(jnp.concatenate(hqs, 0), value)
        dmc[...] += mm_tn(jnp.concatenate(dps, 0), key)
        return grads

    @pl.when(step < last + (0 if late else 1))
    def _():
        key = jnp.concatenate([kv[b, :ff] for b in range(per)], 0)
        value = jnp.concatenate([kv[b, ff:] for b in range(per)], 0)
        grads = units(key, value, [hidden[b, :, :ff] for b in range(per)])
        for b, (low, high) in enumerate(grads):
            if late:
                g_hidden[b] = jnp.zeros(g_hidden.shape[1:], F32)
            g_hidden[b, :RANK, :ff], g_hidden[b, RANK:, :ff] = low, high

    @pl.when(step == last)
    def _():
        if late:
            g.finish()
            flat = lambda ref: ref[...].reshape(-1, ref.shape[-1])
            ((low, high),) = units(flat(key_late), flat(value_late), [hidden_late[...]])
            part = low.shape[1] // 8
            for p in range(8):
                at = slice(p * part, (p + 1) * part)
                g_late[p, :, :part], g_late[p, :, part:] = low[:, at], high[:, at]
        h_f = acc_f[...].astype(BF)
        out[...] = (middle[...] + ffo[...] + SCALE * mm_tn(h_f, up_f[...])).astype(BF)
        g_up_f[...] = SCALE * mm(h_f, gy[...])
        dh_c = (SCALE * acc_c[...]).astype(BF)
        d = dmc[...] + mm_tn(dh_c, down_c[...])
        dmc[...] = d
        first[...] = d[:8] * norm[17:18, :]
        if late:
            mine[1] = first[...]
            trade(1, jnp.logical_not(ends), jnp.logical_not(starts), -1)
            d_edge[...] = came[1]
        g_down_c[...] = mm(dh_c, mc[...])


def late_units(n_seq, n_dp, ff):
    return ff // 8 if (n_seq, n_dp) == (8, 4) and ff % 128 == 0 else 0


def channel(n2, edge, norm, gy, middle, down_c, up_f, kv, hidden, key_shard, value_shard):
    n, both, width = kv.shape
    ff, length, late = hidden.shape[2], n2.shape[0], key_shard.shape[0]
    per = max(1, min(n, 512 // ff))
    steps = n // per
    block = lambda shape: pl.BlockSpec(
        (per,) + tuple(shape[1:]), lambda i: (jnp.minimum(i, steps - 1), 0, 0)
    )
    far = lambda shape: pl.BlockSpec(memory_space=pl.ANY)
    shape = jax.ShapeDtypeStruct
    rank = shape((RANK, width), F32)
    ins = [(whole, a) for a in (n2, edge, norm, gy, middle, down_c, up_f)] + [(block, kv), (block, hidden)]
    outs = [
        (result, shape((length, width), BF)),
        (result, shape((length, width), F32)),
        (result, shape((8, width), F32)),
        (block, shape((n, 2 * RANK, ff), F32)),
        (result, rank),
        (result, rank),
    ]
    scratch = [
        pltpu.VMEM((length, width), BF),
        pltpu.VMEM((width, length), BF),
        pltpu.VMEM((width, length), BF),
        pltpu.VMEM((length, width), F32),
        pltpu.VMEM((RANK, length), BF),
        pltpu.VMEM((RANK, length), BF),
        pltpu.VMEM((RANK, length), F32),
        pltpu.VMEM((RANK, length), F32),
    ]
    params = {}
    if late:
        hidden_late = jnp.swapaxes(hidden[:, :, ff - late :], 0, 1).reshape(2 * RANK, n * late)
        ins += [(far, key_shard), (far, value_shard), (whole, hidden_late)]
        outs += [(result, shape((8, RANK, 2 * n * late // 8), F32)), (result, shape((8, width), F32))]
        scratch += [pltpu.VMEM((n, late, width), BF)] * 2
        scratch += [pltpu.VMEM((2, 8, width), F32)] * 2 + [pltpu.SemaphoreType.DMA((2, 2))]
        scratch += gather_scratch(2)
        params = dict(collective_id=4, has_side_effects=True)
    return over_tiles(
        functools.partial(channel_kernel, late), steps + (1 if late else 0), ins, outs, "channel", scratch, **params
    )


HALF = 512


def branch_masks(shape):
    lane = iota(shape, 1)
    lo, hi = DECAY_INNER, DECAY_INNER + RATE_INNER
    return lane < lo, (lane >= lo) & (lane < hi), (lane >= hi) & (lane < hi + GATE_INNER)


def project_kernel(
    hat, hat_prev, valid, vec, first, chosen, second, w_r, w_k, w_v, up,
    rr, kr, vr, wl, al, gg, m_r, m_k, m_v, hs, act, act_low,
):
    @pl.when(pl.program_id(0) == 0)
    def _():
        n1 = hat[...] * vec[0:1, :] + vec[1:2, :]
        change = (hat_prev[...] * vec[0:1, :] + vec[1:2, :]) * valid[...] - n1
        mixed = lambda i: (n1 + change * vec[2 + i : 3 + i, :]).astype(BF)
        m_r[...], m_k[...], m_v[...] = mixed(0), mixed(2), mixed(3)
        for i, m in enumerate((m_r, m_k, m_v)):
            hs[i] = mm_nt(m[...], chosen[i * RANK : (i + 1) * RANK, :]).astype(BF)
        t_w = mm(mixed(1), first[...])
        t_a = mm(mixed(4), first[...])
        t_g = mm(mixed(5), first[...])
        is_w, is_a, is_g = branch_masks(t_w.shape)
        zero = jnp.zeros_like(t_w)
        t_w = jnp.where(is_w, jnp.tanh(t_w), zero)
        t_a = jnp.where(is_a, t_a, zero)
        t_g = jnp.where(is_g, jax.nn.sigmoid(t_g), zero)
        act[...] = t_w + t_a + t_g
        act_low[0], act_low[1], act_low[2] = t_w.astype(BF), t_a.astype(BF), t_g.astype(BF)

    for i, (m, w, out) in enumerate(((m_r, w_r, rr), (m_k, w_k, kr), (m_v, w_v, vr))):
        out[...] = mm_nt(m[...], w[...]) + SCALE * mm(hs[i], up[(5 + i) * RANK : (6 + i) * RANK, :])
    for i, out in enumerate((wl, al, gg)):
        out[...] = mm_nt(act_low[i], second[...])


def final_kernel(
    n, drr, dkr, dvr, dwl, dal, dgg, m_r, m_k, m_v, hs, act, chosen, second, down_o, up_o, hat, rstd, d_mid, vecs,
    w_r, w_k, w_v, down, first, vec,
    grad, summed, stay, go, dhs, d_act, parts, here, came, send_sem, recv_sem, edge_sem,
):
    step, last = pl.program_id(0), pl.num_programs(0) - 1
    me, dp = lax.axis_index("seq"), lax.axis_index("dp")

    def copy(k):
        peer = lax.rem(me + k, n)
        return pltpu.make_async_remote_copy(
            src_ref=parts.at[peer],
            dst_ref=here.at[k - 1],
            send_sem=send_sem.at[k - 1],
            recv_sem=recv_sem.at[k - 1],
            device_id=(peer, dp),
            device_id_type=MESH,
        )

    def edge(to):
        return pltpu.make_async_remote_copy(
            src_ref=go.at[0:8],
            dst_ref=came,
            send_sem=edge_sem.at[0],
            recv_sem=edge_sem.at[1],
            device_id=(to, dp),
            device_id_type=MESH,
        )

    @pl.when(step == 0)
    def _():
        came[...] = jnp.zeros_like(came)
        barrier = pltpu.get_barrier_semaphore()
        for k in range(1, n):
            pl.semaphore_signal(
                barrier, inc=1, device_id=(lax.rem(me + k, n), dp), device_id_type=MESH
            )
        rows = [None] * 6 + [down_o[...], up_o[...]]
        for i, (d, m) in enumerate(((drr, m_r), (dkr, m_k), (dvr, m_v))):
            dh = (SCALE * mm_nt(d[...], chosen[(5 + i) * RANK : (6 + i) * RANK, :])).astype(BF)
            dhs[i] = dh
            rows[i], rows[3 + i] = mm_tn(dh, m[...]), SCALE * mm_tn(hs[i], d[...])
        wide = parts.shape[2]
        for i, r in enumerate(rows):
            for p in range(n):
                parts[p, i * RANK : (i + 1) * RANK, :] = r[:, p * wide : (p + 1) * wide].astype(BF)
        pl.semaphore_wait(barrier, n - 1)
        for k in range(1, n):
            copy(k).start()
        is_w, is_a, is_g = branch_masks(act.shape)
        a = act[...]
        zero = jnp.zeros_like(a)
        d_act[0] = jnp.where(is_w, mm(dwl[...], second[...]) * (1.0 - a * a), zero).astype(BF)
        d_act[1] = jnp.where(is_a, mm(dal[...], second[...]), zero).astype(BF)
        d_act[2] = jnp.where(is_g, mm(dgg[...], second[...]) * a * (1.0 - a), zero).astype(BF)

    total, moved = None, None
    for i, (d, w, at) in enumerate(((drr, w_r, 2), (dkr, w_k, 4), (dvr, w_v, 5))):
        g = mm(d[...], w[...]) + mm(dhs[i], down[i * RANK : (i + 1) * RANK, :])
        move = g * vec[at : at + 1, :]
        total, moved = (g, move) if total is None else (total + g, moved + move)
    for i, at in enumerate((3, 6, 7)):
        g = mm_nt(d_act[i], first[...])
        total, moved = total + g, moved + g * vec[at : at + 1, :]
    tile = pl.ds(pl.multiple_of(step * TILE, TILE), TILE)
    stay[:, tile] = total - moved
    go[:, tile] = moved

    @pl.when(step == last)
    def _():
        pl.when(me > 0)(lambda: edge(me - 1).start())
        for k in range(1, n):
            copy(k).wait()
        t = parts[me].astype(F32)
        for k in range(1, n):
            t = t + here[k - 1].astype(F32)
        summed[...] = t
        pl.when(me < n - 1)(lambda: edge(me + 1).wait_recv())
        size = go.shape[0]
        g = pltpu.roll(go[...], size - 1, axis=0)
        g = stay[...] + jnp.where(iota(g.shape, 0) == size - 1, came[0:1, :], g)
        dhat = g * vecs[0:1, :]
        grad[...] = d_mid[...] + rstd[...] * (
            dhat
            - jnp.mean(dhat, axis=-1, keepdims=True)
            - hat[...] * jnp.mean(dhat * hat[...], axis=-1, keepdims=True)
        )
        pl.when(me > 0)(lambda: edge(me - 1).wait_send())


def shifted(block, axis, distance):
    devices = range(lax.axis_size(axis))
    route = [(i - distance, i) for i in devices if i - distance in devices]
    return lax.ppermute(block, axis, route)


def mm(a, b):
    return lax.dot_general(a, b, DIMS["nn"], preferred_element_type=F32)


def mm_nt(a, b):
    return lax.dot_general(a, b, DIMS["nt"], preferred_element_type=F32)


def mm_tn(a, b):
    return lax.dot_general(a, b, DIMS["tn"], preferred_element_type=F32)


def body(tokens, output_gradient, index, proj, first, second, vectors, ckey, cvalue, model_rows, hidden_rows):
    axes = ("seq", "dp")
    n_seq, n_dp = lax.axis_size("seq"), lax.axis_size("dp")
    n = n_seq * n_dp
    tokens, gy = tokens[0], output_gradient[0]
    length, width = tokens.shape
    nc, tiles = length // C, width // TILE
    adapters, kinds, cols = model_rows.shape
    ff, inner, nvec = ckey.shape[1], first.shape[1], vectors.shape[0]

    key_shard, soon = ckey.T, ff - late_units(n_seq, n_dp, ff)
    kv = lax.all_gather(jnp.concatenate([key_shard[:soon], cvalue[:soon]], 0), axes, axis=0)

    index_all = lax.all_gather(index, "dp", axis=0, tiled=True)
    pick = index_all[:, None] == jnp.arange(adapters, dtype=jnp.int32)[None, :]
    few = jnp.concatenate([model_rows.reshape(adapters, -1), hidden_rows.reshape(adapters, -1)], 1)
    few = jnp.einsum("sa,ax->sx", pick.astype(BF), few, preferred_element_type=F32).astype(BF)
    pad = lambda k: jnp.zeros((cols, k), BF)
    misc = jnp.concatenate(
        [first, pad(HALF - inner), second.T, vectors.T, pad(HALF - inner - nvec)], axis=1
    )
    turned = jnp.swapaxes(proj, 1, 2)

    wide = tokens.astype(F32)
    ahead = shifted(tokens[-1:], "seq", 1).astype(F32)
    rows = jnp.concatenate([ahead, wide], 0)
    centre = rows - jnp.mean(rows, axis=-1, keepdims=True)
    rstd = lax.rsqrt(jnp.mean(centre * centre, axis=-1, keepdims=True) + NORM_EPS)
    hat = centre * rstd
    start = (jnp.arange(length)[:, None] == 0) & (lax.axis_index("seq") == 0)
    valid = jnp.where(start, 0.0, 1.0).astype(F32)
    hat_prev, hat, rstd = hat[:-1], hat[1:], rstd[1:]

    *mats, misc, few_all = gather([turned[0], turned[1], turned[2], turned[3], misc, few.reshape(-1, 128)])
    mats = [m.reshape(width, width) for m in mats]
    misc = misc.reshape(width, -1)
    vec = misc[:, HALF + inner : HALF + inner + nvec].T.astype(F32)
    own = lax.dynamic_index_in_dim(few_all.reshape(n, n_dp, -1, 128), lax.axis_index("dp"), 1, False)
    own = own.reshape(n, -1)
    chosen = own[:, : kinds * cols].reshape(n, kinds, cols).transpose(1, 0, 2).reshape(kinds, width)
    hidden = own[:, kinds * cols :].reshape(n, 2 * RANK, ff)
    down = lambda i: chosen[i * RANK : (i + 1) * RANK]
    up = lambda i: chosen[(5 + i) * RANK : (6 + i) * RANK]

    shape = jax.ShapeDtypeStruct
    full, low = shape((length, width), F32), shape((length, width), BF)
    small, rank = shape((D, width), F32), shape((RANK, width), F32)
    firsts = pl.BlockSpec((width, HALF), lambda i: (0, 0))
    seconds = pl.BlockSpec((width, HALF), lambda i: (0, 1))
    first_rows = pl.BlockSpec((TILE, HALF), lambda i: (i, 0))
    second_rows = pl.BlockSpec((TILE, HALF), lambda i: (i, 1))
    rr, kr, vr, wl, al, gg, m_r, m_k, m_v, hs, act = over_tiles(
        project_kernel, tiles,
        [
            (whole, hat), (whole, hat_prev), (whole, valid), (whole, vec), (firsts, misc), (whole, chosen),
            (second_rows, misc), (tile_rows, mats[0]), (tile_rows, mats[1]), (tile_rows, mats[2]), (cut, chosen),
        ],
        [(cut, full)] * 6
        + [(result, low)] * 3
        + [(result, shape((3, length, RANK), BF)), (result, shape((length, HALF), F32))],
        "project",
        [pltpu.VMEM((3, length, HALF), BF)],
    )
    one, two, each = in_turn(tiles, "first"), in_turn(tiles, "second"), in_turn(tiles, "both")
    keep = pltpu.VMEM((tiles, length, TILE), F32)
    keep_small = pltpu.VMEM((tiles, D, TILE), F32)
    reff, xs, mt, turned, gated, o, us, zs, middle, n2, h_o = over_tiles(
        functools.partial(rec_forward, nc, n_seq, tiles), 2 * tiles,
        [
            (each, rr), (each, kr), (each, vr), (one, wl), (each, al), (two, gg), (each, vec),
            (whole, tokens), (two, mats[3]), (two, down(3)), (whole, up(3)), (whole, vec),
        ],
        [(one, full), (one, full), (one, full), (one, small), (two, low), (two, full), (two, full), (two, full)]
        + [(result, full), (result, full), (result, shape((length, RANK), BF))],
        "rec_forward",
        [keep] * 6 + [keep_small] * 2 + [pltpu.VMEM((length, RANK), F32)] + hand_scratch(tiles),
        collective_id=0, has_side_effects=True,
    )
    soon_only = soon == ff
    row = shifted(n2[-1:], "seq", 1) if soon_only else n2[-1:]
    out, d_mc, moved, g_hidden, up_f, down_c, *more = channel(
        n2, row, vec, gy, middle, down(4), up(4), kv, hidden,
        key_shard[soon:], cvalue[soon:],
    )
    wide = n_dp * cols
    by_piece = lambda rows: jnp.swapaxes(rows.reshape(-1, n_seq, wide), 0, 1)
    parts = [by_piece(jnp.concatenate([down_c, up_f], 0)), g_hidden.reshape(n_seq, -1, wide)]
    if soon_only:
        edge = jnp.broadcast_to(shifted(moved[:1], "seq", -1), (8, width))
    else:
        g_late, edge = more
        parts.append(g_late)
    early, edge = lax.optimization_barrier((jnp.concatenate(parts, 1), edge))
    early = lax.psum_scatter(early, "seq", scatter_dimension=0, tiled=True)[0]
    d_mid, dgg, down_o, up_o, drr, dkr, dvr, dwl, dal = over_tiles(
        functools.partial(rec_backward, nc, n_seq, tiles), 2 * tiles,
        [
            (whole, d_mc), (whole, edge), (whole, gy), (whole, middle), (whole, vec), (one, mats[3]),
            (one, down(3)), (whole, up(3)), (whole, h_o), (one, gated), (one, gg), (one, o),
            (each, rr), (each, kr), (each, vr), (two, wl), (each, al), (each, vec),
            (one, reff), (each, mt), (one, turned), (two, xs), (two, us), (two, zs),
        ],
        [(result, full), (one, low), (one, rank), (result, rank)] + [(two, low)] * 5,
        "rec_backward",
        [pltpu.VMEM((length, width), BF), pltpu.VMEM((length, RANK), BF)]
        + [keep] * 3 + [keep_small] * 2 + hand_scratch(tiles),
        collective_id=1, has_side_effects=True,
    )
    early, drr = lax.optimization_barrier((early, drr))
    grad_tokens, late = over_tiles(
        functools.partial(final_kernel, n_seq), tiles,
        [(whole, a) for a in (drr, dkr, dvr, dwl, dal, dgg, m_r, m_k, m_v, hs, act, chosen)]
        + [(pl.BlockSpec((width, HALF), lambda i: (0, 1), pipeline_mode=pl.Buffered(1)), misc)]
        + [(whole, a) for a in (down_o, up_o, hat, rstd, d_mid, vec)]
        + [(cut, mats[0]), (cut, mats[1]), (cut, mats[2]), (cut, chosen), (first_rows, misc), (cut, vec)],
        [(result, full), (result, shape((8 * RANK, wide), F32))], "final",
        [
            pltpu.VMEM((length, width), F32),
            pltpu.VMEM((length, width), F32),
            pltpu.VMEM((3, length, RANK), BF),
            pltpu.VMEM((3, length, HALF), BF),
            pltpu.VMEM((n_seq, 8 * RANK, wide), BF),
            pltpu.VMEM((n_seq - 1, 8 * RANK, wide), BF),
            pltpu.VMEM((8, width), F32),
            pltpu.SemaphoreType.DMA((n_seq - 1,)),
            pltpu.SemaphoreType.DMA((n_seq - 1,)),
            pltpu.SemaphoreType.DMA((2,)),
        ],
        collective_id=3, has_side_effects=True,
    )

    mine = early[2 * RANK : 2 * RANK + 2 * RANK * ff // cols].reshape(n_dp, 2 * RANK, ff)
    if not soon_only:
        tail = early[2 * RANK + 2 * RANK * ff // cols :].reshape(RANK, 2, n_dp, ff - soon)
        tail = tail.transpose(2, 1, 0, 3).reshape(n_dp, 2 * RANK, ff - soon)
        mine = jnp.concatenate([mine[:, :, :soon], tail], 2)
    columns = jnp.concatenate([early[: 2 * RANK], late], 0).reshape(10 * RANK, n_dp, cols)
    both = jnp.concatenate(
        [jnp.swapaxes(columns, 0, 1).reshape(n_dp, -1), mine.reshape(n_dp, -1)], 1
    )
    both = lax.all_to_all(both, "dp", split_axis=0, concat_axis=0, tiled=True)
    both = jnp.einsum("sa,sx->ax", pick.astype(F32), both, precision=PRECISE)
    at = 10 * RANK * cols
    a = both[:, :at].reshape(adapters, 10 * RANK, cols)
    h = both[:, at:].reshape(adapters, 2 * RANK, ff)
    block = lambda i, k: a[:, i * RANK : (i + k) * RANK]
    grad_model = jnp.concatenate(
        [block(2, 3), block(8, 1), block(0, 1), block(5, 3), block(9, 1), block(1, 1)], axis=1
    )
    return out[None], grad_tokens[None], grad_model, h


def solution(mesh):
    cols = P(None, ("seq", "dp"))
    rows = P(("seq", "dp"), None)
    deep = P(None, None, ("seq", "dp"))
    act = P("dp", "seq", None)
    return jax.shard_map(
        body,
        mesh=mesh,
        in_specs=(act, act, P("dp"), deep, rows, cols, cols, cols, rows, deep, deep),
        out_specs=(act, act, deep, deep),
        check_vma=False,
    )
```

```python
import functools
import math

import jax
import jax.numpy as jnp
from jax import lax
from jax.experimental import pallas as pl
from jax.experimental.pallas import tpu as pltpu
from jax.sharding import PartitionSpec as P

F32, BF = jnp.float32, jnp.bfloat16
MESH = pl.DeviceIdType.MESH
D = 64
C = 64
PW = 2 * D
DECAY_INNER, RATE_INNER, GATE_INNER, RANK = 96, 96, 256, 16
SCALE = 4.0
NORM_EPS, GROUP_EPS, UNIT_EPS = 1e-05, 0.00064, 1e-06
DECAY_SCALE = math.exp(-0.5)
PRECISE = lax.Precision.HIGHEST
DIMS = {
    "nn": (((1,), (0,)), ((), ())),
    "nt": (((1,), (1,)), ((), ())),
    "tn": (((0,), (0,)), ((), ())),
}


def split(x):
    hi = x.astype(BF)
    return hi, (x - hi.astype(F32)).astype(BF)


def dot1(a, b, m="nn"):
    return lax.dot_general(a.astype(BF), b.astype(BF), DIMS[m], preferred_element_type=F32)


def dot3(a, b, m="nn"):
    ah, al = split(a)
    bh, bl = split(b)
    ka, kb = (0 if m == "tn" else 1), (1 if m == "nt" else 0)
    n = b.shape[1 - kb]
    aa = jnp.concatenate([ah, al], axis=ka)
    bb = jnp.concatenate([jnp.concatenate([bh, bl], axis=1 - kb)] * 2, axis=kb)
    r = lax.dot_general(aa, bb, DIMS[m], preferred_element_type=F32)
    return r[:, :n] + r[:, n:]


dot_inv = dot_a = dot_w = dot_b = dot3
dot_g = dot1


def iota(shape, axis):
    return lax.broadcasted_iota(jnp.int32, shape, axis)


def stack2(x):
    lane = iota(x.shape, 1)
    zero = jnp.zeros_like(x)
    return jnp.concatenate([jnp.where(lane < D, x, zero), jnp.where(lane < D, zero, x)], axis=0)


def pack2(x):
    h = x.shape[0] // 2
    return x[:h] + x[h:]


def head_ones():
    r, c = iota((2 * PW, PW), 0) % PW, iota((2 * PW, PW), 1)
    return jnp.where((r // D) == (c // D), 1.0, 0.0).astype(BF)


def headsum(x, ones):
    h, l = split(x)
    return lax.dot_general(
        jnp.concatenate([h, l], axis=1), ones, DIMS["nn"], preferred_element_type=F32
    )


def triangle(upper):
    r, c = iota((C, C), 0), iota((C, C), 1)
    return jnp.where((r <= c) if upper else (r >= c), 1.0, 0.0).astype(BF)


def cums(x, tri):
    h, l = split(x)
    m = (x - h.astype(F32) - l.astype(F32)).astype(BF)
    n = x.shape[1]
    r = lax.dot_general(
        tri, jnp.concatenate([h, l, m], axis=1), DIMS["nn"], preferred_element_type=F32
    )
    return r[:, :n] + r[:, n : 2 * n] + r[:, 2 * n :]


def prelude(kr, wl, al, w0, a0, k_k, k_a, ones):
    s = jax.nn.sigmoid(w0 + wl)
    a = jax.nn.sigmoid(a0 + al)
    kx = kr * k_k
    rn = lax.rsqrt(headsum(kx * kx, ones) + UNIT_EPS)
    return s, -DECAY_SCALE * s, a, rn, kx * rn, kr * (1.0 + (a - 1.0) * k_a)


def grid_ids():
    r, c = iota((PW, PW), 0), iota((PW, PW), 1)
    return r, c, (r // D) == (c // D)


def inverses(many):
    r, c, _ = grid_ids()
    eye = jnp.where(r == c, 1.0, 0.0)
    b = 1
    while b < C:
        level = ((r // (2 * b)) == (c // (2 * b))) & ((r // b) % 2 == 1) & ((c // b) % 2 == 0)
        parts = [jnp.where(level, a, 0.0) for a in many]
        if b == 1:
            xs = [eye + p for p in parts]
        else:
            half = [dot_inv(x, p) for x, p in zip(xs, parts)]
            xs = [x + dot_inv(h, x) for h, x in zip(half, xs)]
        b *= 2
    return xs


def factors(logw, tri):
    run = cums(logw, tri)
    return jnp.exp(run - logw), jnp.exp(run), jnp.exp(-run), jnp.exp(run[C - 1 : C])


def forward_chunks(units, tri):
    rows, cols, same = grid_ids()
    zero = jnp.zeros((PW, PW), F32)
    strict, incl = (rows > cols) & same, (rows >= cols) & same
    fs = [factors(u[5], tri) for u in units]
    p2 = [stack2(u[1] * f[0]) for u, f in zip(units, fs)]
    r2 = [stack2(u[0] * f[1]) for u, f in zip(units, fs)]
    q2 = [stack2(u[2] * f[2]) for u, f in zip(units, fs)]
    k2 = [stack2(u[3] * f[2]) for u, f in zip(units, fs)]
    v2 = [stack2(u[4]) for u in units]
    aa = [
        dot_a(jnp.concatenate([p, r], 0), jnp.concatenate([q, k], 0), "nt")
        for p, r, q, k in zip(p2, r2, q2, k2)
    ]
    apk = [jnp.where(strict, a[:PW, PW:], zero) for a in aa]
    y = [dot_w(a, v) for a, v in zip(apk, v2)]
    xs = inverses([jnp.where(strict, a[:PW, :PW], zero) for a in aa])
    ww = [dot_w(x, jnp.concatenate([p, t], 1)) for x, p, t in zip(xs, p2, y)]
    left = [
        jnp.concatenate(
            [
                jnp.concatenate(
                    [jnp.where(incl, a[PW:, :PW], zero), jnp.where(incl, a[PW:, PW:], zero)], 1
                ),
                jnp.concatenate([(q * f[3]).T, (k * f[3]).T], 1),
            ],
            0,
        )
        for a, q, k, f in zip(aa, q2, k2, fs)
    ]
    right = [
        jnp.concatenate([w, jnp.concatenate([zero, v], 1)], 0) for w, v in zip(ww, v2)
    ]
    big = [dot_b(l, r) for l, r in zip(left, right)]
    move = [
        b[PW:, :PW] + jnp.where(rows == cols, jnp.broadcast_to(f[3], (PW, PW)), zero)
        for b, f in zip(big, fs)
    ]
    return [
        (pack2(r + b[:PW, :PW]), pack2(b[:PW, PW:]), m, b[PW:, PW:], pack2(w[:, :PW]), pack2(w[:, PW:]), x)
        for r, b, m, w, x in zip(r2, big, move, ww, xs)
    ]


def backward_chunks(units, tri, tri_up):
    rows, cols, same = grid_ids()
    zero = jnp.zeros((PW, PW), F32)
    strict, incl = (rows < cols) & same, (rows <= cols) & same
    both = jnp.concatenate([jnp.concatenate([strict, incl], 1)] * 2, 0)
    fs = [factors(t[5], tri) for t in units]
    pe = [t[1] * f[0] for t, f in zip(units, fs)]
    re = [t[0] * f[1] for t, f in zip(units, fs)]
    qe = [t[2] * f[2] for t, f in zip(units, fs)]
    ke = [t[3] * f[2] for t, f in zip(units, fs)]
    g2 = [stack2(t[10]) for t in units]
    qk = [jnp.concatenate([stack2(q), stack2(k)], 0) for q, k in zip(qe, ke)]
    pr = [jnp.concatenate([stack2(p), stack2(r)], 0) for p, r in zip(pe, re)]
    at = [dot_a(a, b, "nt") for a, b in zip(qk, pr)]
    qkh = [
        dot_g(jnp.concatenate([q * f[3], k * f[3]], 0), t[9])
        for q, k, f, t in zip(qe, ke, fs, units)
    ]
    sq = [dot_g(jnp.concatenate([t[7], t[4]], 0), t[9], "nt") for t in units]
    du = [
        dot_g(jnp.where(incl, a[:PW, PW:], zero), g) + stack2(h[:C])
        for a, g, h in zip(at, g2, qkh)
    ]
    dm = [dot_g(t[6], d, "tn") for t, d in zip(units, du)]
    dg = [jnp.concatenate([d, g], 0) for d, g in zip(dm, g2)]
    dv = [
        pack2(
            dot_g(
                jnp.concatenate(
                    [jnp.where(strict, a[PW:, :PW], zero), jnp.where(incl, a[PW:, PW:], zero)], 1
                ),
                d,
            )
        )
        + h[C:]
        for a, d, h in zip(at, dg, qkh)
    ]
    dat = [
        dot_g(jnp.concatenate([stack2(t[7]), stack2(t[4])], 0), d, "nt")
        for t, d in zip(units, dg)
    ]
    dat = [jnp.where(both, d, jnp.zeros_like(d)) for d in dat]
    dpr = [dot_g(d, a, "tn") for d, a in zip(dat, qk)]
    dqk = [dot_g(d, a) for d, a in zip(dat, pr)]
    sp = [dot_g(jnp.concatenate([pack2(d), t[10]], 0), t[8], "nt") for d, t in zip(dm, units)]
    outs = []
    for i, t in enumerate(units):
        eb, el, en, last = fs[i]
        dp, dr = pack2(dpr[i][:PW]) + sp[i][:C], pack2(dpr[i][PW:]) + sp[i][C:]
        dqh, dkh = sq[i][:C], sq[i][C:]
        dq, dk = pack2(dqk[i][:PW]) + dqh * last, pack2(dqk[i][PW:]) + dkh * last
        tail = jnp.sum((qe[i] * dqh + ke[i] * dkh) * last, axis=0, keepdims=True)
        tail = tail + last * jnp.sum((t[8] * t[9]).T, axis=0, keepdims=True)
        gb = pe[i] * dp
        gl = re[i] * dr - qe[i] * dq - ke[i] * dk
        dlogw = cums(gl + gb, tri_up) - gb + tail
        outs.append((dr * el, dp * eb, dq * en, dk * en, dv[i], dlogw))
    return outs


def lanes(ref):
    return [slice(i * PW, (i + 1) * PW) for i in range(ref.shape[-1] // PW)]


def norm_parts(o, ones):
    centre = o - headsum(o, ones) * (1.0 / D)
    rstd = lax.rsqrt(headsum(centre * centre, ones) * (1.0 / D) + GROUP_EPS)
    return centre * rstd, rstd


def hand_on(n, half, back, move, add, here, send, send_sem, recv_sem):
    step, last = pl.program_id(0), pl.num_programs(0) - 1
    s, d = lax.axis_index("seq"), lax.axis_index("dp")
    at = n - 1 - s if back else s
    first, final = at == 0, at == n - 1
    nxt, prv = (s - 1, s + 1) if back else (s + 1, s - 1)
    begins, goes = jnp.logical_not(first), jnp.logical_not(final)
    tile = step - jnp.minimum(at, half)
    now = jnp.logical_and(tile >= 0, tile < half)

    def copy(i, to):
        return pltpu.make_async_remote_copy(
            src_ref=send.at[i],
            dst_ref=here.at[i],
            send_sem=send_sem.at[i],
            recv_sem=recv_sem.at[i],
            device_id=(to, d),
            device_id_type=MESH,
        )

    @pl.when(jnp.logical_and(step == 0, begins))
    def _():
        pl.semaphore_signal(
            pltpu.get_barrier_semaphore(), inc=1, device_id=(prv, d), device_id_type=MESH
        )

    @pl.when(jnp.logical_and(step == 0, goes))
    def _():
        pl.semaphore_wait(pltpu.get_barrier_semaphore(), 1)

    @pl.when(jnp.logical_and(now, first))
    def _():
        here[tile] = jnp.zeros(here.shape[1:], F32)

    @pl.when(jnp.logical_and(now, begins))
    def _():
        copy(tile, prv).wait_recv()

    @pl.when(jnp.logical_and(now, goes))
    def _():
        for ln in lanes(here):
            send[tile, :, ln] = dot3(move[tile, :, ln], stack2(here[tile, :, ln])) + add[tile, :, ln]
        copy(tile, nxt).start()

    @pl.when(jnp.logical_and(step == last, goes))
    def _():
        for i in range(half):
            copy(i, nxt).wait_send()


def hand_scratch(steps):
    return [
        pltpu.VMEM((steps, D, TILE), F32),
        pltpu.VMEM((steps, D, TILE), F32),
        pltpu.SemaphoreType.DMA((steps,)),
        pltpu.SemaphoreType.DMA((steps,)),
    ]


def rec_forward(
    nc, n, half, rr, kr, vr, wl, al, gg, vec, tokens, wo, down, up, norm,
    reff, xs, mt, turned, z_out, o_out, u_out, zs, middle, normed, h_out,
    k_reff, k_oloc, k_w1, k_w2, k_m, k_n, move, add, acc_h, *hand,
):
    step, last = pl.program_id(0), pl.num_programs(0) - 1
    ones = head_ones()

    @pl.when(step < half)
    def _():
        tri = triangle(False)
        units, where = [], []
        for ln in lanes(rr):
            row = lambda i: vec[i : i + 1, ln]
            _, logw, a, _, kk, km = prelude(
                kr[:, ln], wl[:, ln], al[:, ln], row(8), row(9), row(10), row(11), ones
            )
            r, v, q = rr[:, ln], vr[:, ln], kk * a
            for c in range(nc):
                s = slice(c * C, (c + 1) * C)
                units.append((r[s], -kk[s], q[s], km[s], v[s], logw[s]))
                where.append((s, ln))
        done = forward_chunks(units, tri)
        packed = []
        for (s, ln), (e, o, m, z, y1, y2, x) in zip(where, done):
            reff[s, ln] = e
            k_reff[step, s, ln], k_oloc[step, s, ln] = e, o
            k_w1[step, s, ln], k_w2[step, s, ln] = y1, y2
            xs[s, ln] = pack2(x)
            mp = pack2(m)
            k_m[step, s, ln], k_n[step, s, ln], mt[s, ln] = mp, pack2(z), pack2(m.T)
            packed.append(mp)
        for i, ln in enumerate(lanes(rr)):
            tm, tn = stack2(packed[i * nc]), done[i * nc][3]
            for c in range(1, nc):
                t = dot3(packed[i * nc + c], jnp.concatenate([tm, tn], 1))
                tm, tn = stack2(t[:, :PW]), stack2(t[:, PW:]) + done[i * nc + c][3]
            move[step, :, ln], add[step, :, ln], turned[:, ln] = pack2(tm), pack2(tn), pack2(tm.T)

    hand_on(n, half, False, move, add, *hand)

    @pl.when(step >= half)
    def _():
        t = step - half
        here = hand[0]
        state = [here[t, :, ln] for ln in lanes(rr)]
        for c in range(nc):
            s = slice(c * C, (c + 1) * C)
            ts = [
                dot3(jnp.concatenate([k_m[t, s, ln], k_reff[t, s, ln], k_w1[t, s, ln]], 0), stack2(z))
                for z, ln in zip(state, lanes(rr))
            ]
            for i, (y, ln) in enumerate(zip(ts, lanes(rr))):
                zs[s, ln] = state[i]
                o_out[s, ln] = y[C : 2 * C] + k_oloc[t, s, ln]
                u_out[s, ln] = y[2 * C :] + k_w2[t, s, ln]
                state[i] = y[:C] + k_n[t, s, ln]
        for ln in lanes(rr):
            row = lambda i: vec[i : i + 1, ln]
            a = jax.nn.sigmoid(row(9) + al[:, ln])
            km = kr[:, ln] * (1.0 + (a - 1.0) * row(11))
            hat, _ = norm_parts(o_out[:, ln], ones)
            y = hat * row(13) + row(14) + headsum(rr[:, ln] * km * row(12), ones) * vr[:, ln]
            z_out[:, ln] = (y * gg[:, ln]).astype(BF)

        @pl.when(step == half)
        def _():
            acc_h[...] = jnp.zeros_like(acc_h)
            middle[...] = tokens[...].astype(F32)

        acc_h[...] += mm_nt(z_out[...], down[...])
        middle[...] += mm_nt(z_out[...], wo[...])

    @pl.when(step == last)
    def _():
        h_out[...] = acc_h[...].astype(BF)
        x1 = middle[...] + SCALE * mm(h_out[...], up[...])
        middle[...] = x1
        centre = x1 - jnp.mean(x1, axis=-1, keepdims=True)
        rstd = lax.rsqrt(jnp.mean(centre * centre, axis=-1, keepdims=True) + NORM_EPS)
        normed[...] = centre * rstd * norm[15:16, :] + norm[16:17, :]


def rec_backward(
    nc, n, half, d_mc, edge, gy, middle, norm, wo, down, up, h_o, gated, gg, o, rr, kr, vr, wl, al, vec,
    reff, mt, turned, xs, us, zs,
    d_mid, dgg, g_down, g_up, drr, dkr, dvr, dwl, dal,
    low, dh, k_dy, k_do, k_es, move, add, *hand,
):
    step = pl.program_id(0)
    ones = head_ones()

    @pl.when(step == 0)
    def _():
        moved = d_mc[...] * norm[17:18, :]
        size = moved.shape[0]
        up_one = pltpu.roll(moved, size - 1, axis=0)
        up_one = jnp.where(iota(moved.shape, 0) == size - 1, edge[0:1, :], up_one)
        dn = d_mc[...] - moved + up_one
        x1 = middle[...]
        centre = x1 - jnp.mean(x1, axis=-1, keepdims=True)
        rstd = lax.rsqrt(jnp.mean(centre * centre, axis=-1, keepdims=True) + NORM_EPS)
        hat = centre * rstd
        dhat = dn * norm[15:16, :]
        d = rstd * (
            dhat
            - jnp.mean(dhat, axis=-1, keepdims=True)
            - hat * jnp.mean(dhat * hat, axis=-1, keepdims=True)
        )
        d = d + gy[...].astype(F32)
        d_mid[...] = d
        low[...] = d.astype(BF)
        dh[...] = (SCALE * mm_nt(low[...], up[...])).astype(BF)
        g_up[...] = SCALE * mm_tn(h_o[...], low[...])

    @pl.when(step < half)
    def _():
        dz = mm(low[...], wo[...]) + mm(dh[...], down[...])
        g_down[...] = mm_tn(dh[...], gated[...])
        _, _, same = grid_ids()
        for ln in lanes(rr):
            row = lambda i: vec[i : i + 1, ln]
            a = jax.nn.sigmoid(row(9) + al[:, ln])
            km = kr[:, ln] * (1.0 + (a - 1.0) * row(11))
            hat, rstd = norm_parts(o[:, ln], ones)
            y = hat * row(13) + row(14) + headsum(rr[:, ln] * km * row(12), ones) * vr[:, ln]
            dgg[:, ln] = (dz[:, ln] * y).astype(BF)
            dy = dz[:, ln] * gg[:, ln]
            k_dy[step, :, ln] = dy
            dhat = dy * row(13)
            k_do[step, :, ln] = rstd * (
                dhat
                - headsum(dhat, ones) * (1.0 / D)
                - hat * (headsum(dhat * hat, ones) * (1.0 / D))
            )
        es = {}
        for c in range(nc):
            s = slice(c * C, (c + 1) * C)
            for ln in lanes(rr):
                e = pack2(jnp.where(same, dot3(reff[s, ln], k_do[step, s, ln], "tn"), 0.0))
                k_es[step, s, ln] = e
                es[c, ln.start] = e
        state = [es[nc - 1, ln.start] for ln in lanes(rr)]
        for c in reversed(range(nc - 1)):
            s = slice(c * C, (c + 1) * C)
            state = [es[c, ln.start] + dot3(mt[s, ln], stack2(h)) for h, ln in zip(state, lanes(rr))]
        for h, ln in zip(state, lanes(rr)):
            add[step, :, ln] = h
            move[step, :, ln] = turned[:, ln]

    hand_on(n, half, True, move, add, *hand)

    @pl.when(step >= half)
    def _():
        t = step - half
        tri, tri_up = triangle(False), triangle(True)
        units, where, pre = [], [], []
        hs = {}
        for ln in lanes(rr):
            h = hand[0][t, :, ln]
            for c in reversed(range(nc)):
                s = slice(c * C, (c + 1) * C)
                hs[c, ln.start] = stack2(h)
                if c:
                    h = dot3(mt[s, ln], hs[c, ln.start]) + k_es[t, s, ln]
        for ln in lanes(rr):
            row = lambda i: vec[i : i + 1, ln]
            for c in range(nc):
                s = slice(c * C, (c + 1) * C)
                r, v, k = rr[s, ln], vr[s, ln], kr[s, ln]
                sg, logw, a, rn, kk, km = prelude(
                    k, wl[s, ln], al[s, ln], row(8), row(9), row(10), row(11), ones
                )
                units.append(
                    (r, -kk, kk * a, km, v, logw, stack2(xs[s, ln]), us[s, ln], stack2(zs[s, ln]),
                     hs[c, ln.start], k_do[t, s, ln])
                )
                where.append((s, ln))
                pre.append((sg, a, rn, kk, km))
        done = backward_chunks(units, tri, tri_up)
        for (s, ln), (sg, a, rn, kk, km), (dr, dp, dq, dk, dv, dlogw) in zip(where, pre, done):
            row = lambda i: vec[i : i + 1, ln]
            r, v, k = rr[s, ln], vr[s, ln], kr[s, ln]
            dy = k_dy[t, s, ln]
            dv = dv + headsum(r * km * row(12), ones) * dy
            ds = headsum(dy * v, ones) * row(12)
            dr = dr + ds * km
            dkm = dk + ds * r
            dkk = dq * a - dp
            da = dq * kk + dkm * k * row(11)
            dk = dkm * (1.0 + (a - 1.0) * row(11)) + row(10) * rn * (dkk - kk * headsum(dkk * kk, ones))
            drr[s, ln], dkr[s, ln], dvr[s, ln] = dr.astype(BF), dk.astype(BF), dv.astype(BF)
            dwl[s, ln] = (dlogw * (-DECAY_SCALE) * sg * (1.0 - sg)).astype(BF)
            dal[s, ln] = (da * a * (1.0 - a)).astype(BF)


TILE = 2 * PW


def cut(shape):
    lead = tuple(shape[:-1])
    return pl.BlockSpec(lead + (TILE,), lambda i, n=len(lead): (0,) * n + (i,))


def whole(shape):
    return pl.BlockSpec(tuple(shape), lambda i, n=len(shape): (0,) * n, pipeline_mode=pl.Buffered(1))


def result(shape):
    return pl.BlockSpec(tuple(shape), lambda i, n=len(shape): (0,) * n)


def in_turn(half, which):
    def spec(shape):
        lead = tuple(shape[:-1])
        place = {
            "first": lambda i: jnp.minimum(i, half - 1),
            "second": lambda i: jnp.maximum(i - half, 0),
            "both": lambda i: lax.rem(i, half),
        }[which]
        return pl.BlockSpec(lead + (TILE,), lambda i: (0,) * len(lead) + (place(i),))

    return spec


def tile_rows(shape):
    return pl.BlockSpec((TILE, shape[1]), lambda i: (i, 0))


def over_tiles(body, steps, ins, outs, name, scratch=(), **params):
    made = lambda spec, shape: spec if isinstance(spec, pl.BlockSpec) else spec(shape)
    return pl.pallas_call(
        body,
        grid=(steps,),
        in_specs=[made(spec, x.shape) for spec, x in ins],
        out_specs=[made(spec, x.shape) for spec, x in outs],
        out_shape=[x for _, x in outs],
        scratch_shapes=list(scratch),
        compiler_params=pltpu.CompilerParams(vmem_limit_bytes=60 * 1024 * 1024, **params),
        name=name,
    )(*[x for _, x in ins])


ORDERS = ("zxy", "zyx", "xzy", "yzx", "zxy", "yzx")
DIRS = "xyuds"


def gather_events(order, z, x, y):
    other = {"x": lambda q: (q, 1 - x, y), "y": lambda q: (q, x, 1 - y), "z": lambda q: (q, x, y)}
    inside = lambda k: None if k == 0 else jnp.logical_and(z + k >= 0, z + k <= 3)
    if order[0] == "z":
        a, b = order[1], order[2]
        events = [(0, (z, x, y), None, None, [a, b, "u", "d", "s"])]
        for k in (1, 2, 3):
            events.append((k, (z - k, x, y), "u", z >= k, ["u", a, b, "s"]))
            events.append((k, (z + k, x, y), "d", z + k <= 3, ["d", a, b, "s"]))
        for k in range(-3, 4):
            events.append((abs(k) + 1, other[a](z + k), a, inside(k), [b, "s"]))
    else:
        a, b = order[0], order[2]
        events = [(0, (z, x, y), None, None, [a, "u", "d", b, "s"])]
        events.append((1, other[a](z), a, None, ["u", "d", b, "s"]))
        for k in (1, 2, 3):
            for late, at in ((0, other["z"]), (1, other[a])):
                events.append((k + late, at(z - k), "u", z >= k, ["u", b, "s"]))
                events.append((k + late, at(z + k), "d", z + k <= 3, ["d", b, "s"]))
    for k in range(-3, 4):
        events.append((abs(k) + 1, other[b](z + k), b, inside(k), ["s"]))
        events.append((abs(k) + 2, (z + k, 1 - x, 1 - y), b, inside(k), ["s"]))
    return events


def maybe(condition, run):
    if condition is None:
        run()
    else:
        pl.when(condition)(run)


class Gathering:
    def __init__(self, orders, steps, shards, whole, send, recv, near):
        self.shards, self.whole, self.send, self.recv, self.near = shards, whole, send, recv, near
        seq, dp = lax.axis_index("seq"), lax.axis_index("dp")
        z, x, y, self.c = seq // 2, seq % 2, dp // 2, dp % 2
        self.y, self.z = y, z
        self.to = {
            "x": (z * 2 + 1 - x, dp),
            "y": (seq, (1 - y) * 2 + self.c),
            "u": (seq + 2, dp),
            "d": (seq - 2, dp),
            "s": (seq, y * 2 + 1 - self.c),
        }
        self.exists = {"u": z < 3, "d": z > 0}
        todo = [
            (steps[t][i] if steps else e[0], t, e)
            for t, o in enumerate(orders)
            for i, e in enumerate(gather_events(o, z, x, y))
        ]
        todo.sort(key=lambda q: q[0])
        self.todo = todo
        self.times = sorted({q[0] for q in todo})

    def enter(self, beside=None, count=0):
        barrier = pltpu.get_barrier_semaphore()
        if beside is not None:
            pl.when(count == 1)(
                lambda: pl.semaphore_signal(barrier, inc=1, device_id=beside, device_id_type=MESH)
            )
        for k in DIRS:
            maybe(
                self.exists.get(k),
                lambda k=k: pl.semaphore_signal(
                    barrier, inc=1, device_id=self.to[k], device_id_type=MESH
                ),
            )
        pl.semaphore_wait(barrier, 3 + (self.z + 2) // 3 + (5 - self.z) // 3 + count)

    def chip(self, b):
        return b[0] * 4 + b[1] * 2 + b[2]

    def shard(self, t, k=None):
        ref = self.shards[t]
        if len(ref.shape) == 2:
            return ref
        return ref.at[1 - self.y if k == "y" else self.y]

    def copy(self, t, own, b, k):
        slot = self.whole[t].at[self.chip(b) * 2 + self.c]
        return pltpu.make_async_remote_copy(
            src_ref=self.shard(t, k) if own else slot,
            dst_ref=slot,
            send_sem=self.send.at[DIRS.index(k), t, self.chip(b)],
            recv_sem=self.recv.at[1 if k == "s" else 0, t, self.chip(b)],
            device_id=self.to[k],
            device_id_type=MESH,
        )

    def local(self, t, b):
        return pltpu.make_async_copy(
            self.shard(t), self.whole[t].at[self.chip(b) * 2 + self.c], self.near.at[t]
        )

    def goes(self, event):
        _, b, came, condition, ways = event
        for k in ways:
            both = self.exists.get(k) if condition is None else condition
            if condition is not None and k in self.exists:
                both = jnp.logical_and(condition, self.exists[k])
            yield b, came is None, k, both

    def take(self, time):
        for at, t, event in self.todo:
            if at != time:
                continue
            _, b, came, condition, _ = event
            if came is None:
                self.local(t, b).start()
            else:
                maybe(condition, lambda: self.copy(t, False, b, came).wait_recv())
            for _, own, k, both in self.goes(event):
                maybe(both, lambda: self.copy(t, own, b, k).start())

    def finish(self):
        for t in range(len(self.shards)):
            for i in range(16):
                pltpu.make_async_remote_copy(
                    src_ref=self.shard(t),
                    dst_ref=self.whole[t].at[i * 2 + 1 - self.c],
                    send_sem=self.send.at[4, t, i],
                    recv_sem=self.recv.at[1, t, i],
                    device_id=self.to["s"],
                    device_id_type=MESH,
                ).wait_recv()
        for _, t, event in self.todo:
            for b, own, k, both in self.goes(event):
                maybe(both, lambda: self.copy(t, own, b, k).wait_send())
            if event[2] is None:
                self.local(t, event[1]).wait()


def gather_scratch(n):
    return [
        pltpu.SemaphoreType.DMA((5, n, 16)),
        pltpu.SemaphoreType.DMA((2, n, 16)),
        pltpu.SemaphoreType.DMA((n,)),
    ]


def gather_kernel(orders, *refs):
    n = len(orders)
    g = Gathering(orders, None, refs[:n], refs[n : 2 * n], *refs[2 * n :])
    g.enter()
    for time in g.times:
        g.take(time)
    g.finish()


def own_gather():
    return (lax.axis_size("seq"), lax.axis_size("dp")) == (8, 4)


def gather(shards):
    if not own_gather():
        return [lax.all_gather(s, ("seq", "dp"), axis=0) for s in shards]
    n, devices = len(shards), 32
    return pl.pallas_call(
        functools.partial(gather_kernel, ORDERS[:n]),
        out_shape=[jax.ShapeDtypeStruct((devices,) + s.shape[-2:], s.dtype) for s in shards],
        in_specs=[pl.BlockSpec(memory_space=pl.ANY)] * n,
        out_specs=[pl.BlockSpec(memory_space=pl.ANY)] * n,
        scratch_shapes=gather_scratch(n),
        compiler_params=pltpu.CompilerParams(collective_id=2, has_side_effects=True),
        name="gather_time",
    )(*shards)


def sort_kernel(kinds, late, few, small, chosen, hidden, hidden_late, vec):
    half = kinds // 2
    base = (lax.axis_index("dp") % 2) * (half + 4 * RANK)
    rows = lambda o, at, n: few[o, pl.ds(pl.multiple_of(base + at, 16), n), :]
    left = iota((half, PW), 1) < D
    for p in range(few.shape[0] // 2):
        one, two = rows(2 * p, 0, half).astype(F32), rows(2 * p + 1, 0, half).astype(F32)
        at = slice(p * PW, (p + 1) * PW)
        chosen[:half, at] = jnp.where(left, one, pltpu.roll(two, D, axis=1)).astype(BF)
        chosen[half:, at] = jnp.where(left, pltpu.roll(one, D, axis=1), two).astype(BF)
    per = PW // late
    lane = iota((2 * RANK, PW), 1) // late
    for g in range(few.shape[0] // per):
        tail = None
        for j in range(per):
            o = g * per + j
            low, high = rows(o, half, 2 * RANK), rows(o, half + 2 * RANK, 2 * RANK)
            hidden[o, :, :PW], hidden[o, :, PW:] = low, high
            shift = (j + 1) * late % PW
            end = pltpu.roll(high.astype(F32), shift, axis=1) if shift else high.astype(F32)
            tail = end if tail is None else jnp.where(lane == j, end, tail)
        hidden_late[:, g * PW : (g + 1) * PW] = tail.astype(BF)
    vec[...] = small[...].astype(F32).T[D : D + vec.shape[0]]


def sort_small(kinds, late, nvec, few, misc):
    n, width = few.shape[0], misc.shape[0]
    shape = jax.ShapeDtypeStruct
    return over_tiles(
        functools.partial(sort_kernel, kinds, late), 1,
        [(whole, few), (pl.BlockSpec((width, PW), lambda i: (0, 7)), misc)],
        [
            (whole, shape((kinds, width), BF)),
            (whole, shape((n, 2 * RANK, 2 * PW), BF)),
            (whole, shape((2 * RANK, n * late), BF)),
            (whole, shape((nvec, width), F32)),
        ],
        "sort_small",
    )


LATE_ORDERS = ("zxy", "yzx")
LATE_STEPS = (
    (0, 2, 2, 4, 4, 7, 7, 11, 9, 4, 2, 5, 9, 11, 9, 13, 7, 11, 4, 8, 2, 6, 5, 9, 7, 11, 9, 13),
    (0, 3, 3, 3, 5, 5, 6, 6, 8, 8, 9, 9, 11, 11, 13, 14, 13, 14, 7, 11, 3, 6, 8, 12, 13, 14, 13, 14),
)


def channel_kernel(
    late, n2, edge, norm, gy, middle, down_c, up_f, kv, hidden, *refs,
):
    if late:
        key_shard, value_shard, hidden_late, *refs = refs
    out, dmc, first, g_hidden, g_up_f, g_down_c, *refs = refs
    if late:
        g_late, d_edge, *refs = refs
    mc, mct, gyt, ffo, h_c, dh_f, acc_f, acc_c, *refs = refs
    step, last = pl.program_id(0), pl.num_programs(0) - 1
    per, ff = kv.shape[0], kv.shape[1] // 2
    if late:
        key_late, value_late, mine, came, edge_sem, *sems = refs
        g = Gathering(LATE_ORDERS, LATE_STEPS, (key_shard, value_shard), (key_late, value_late), *sems)
        seq, dp = lax.axis_index("seq"), lax.axis_index("dp")
        x, z = seq % 2, seq // 2
        beside = seq + 2 * x - 1
        count = (1 - x) * ((z + 2) // 3) + x * ((5 - z) // 3)
        starts, ends = seq == 0, seq == 7

        def edges(i, to):
            return pltpu.make_async_remote_copy(
                src_ref=mine.at[i],
                dst_ref=came.at[i],
                send_sem=edge_sem.at[0, i],
                recv_sem=edge_sem.at[1, i],
                device_id=(to, dp),
                device_id_type=MESH,
            )

        def trade(i, has_from, has_to, shift):
            pl.when(has_to)(lambda: edges(i, seq + shift).start())
            pl.when(has_from)(lambda: edges(i, seq - shift).wait_recv())
            pl.when(has_to)(lambda: edges(i, seq + shift).wait_send())

        @pl.when(step == 0)
        def _():
            came[...] = jnp.zeros_like(came)
            g.enter((beside, dp), count)
            size = n2.shape[0]
            mine[0] = n2[size - 8 :, :]

        for time in g.times:

            @pl.when(step == time)
            def _():
                g.take(time)

        @pl.when(step == 0)
        def _():
            trade(0, jnp.logical_not(starts), jnp.logical_not(ends), 1)

    @pl.when(step == 0)
    def _():
        x = n2[...]
        row = came[0, 7:8, :] if late else edge[...]
        before = jnp.where(iota(x.shape, 0) == 0, row, pltpu.roll(x, 1, axis=0))
        m = x + (before - x) * norm[17:18, :]
        mc[...] = m.astype(BF)
        mct[...] = m.T.astype(BF)
        gyt[...] = gy[...].astype(F32).T.astype(BF)
        h_c[...] = mm_nt(down_c[...], mc[...]).astype(BF)
        dh_f[...] = (SCALE * mm_nt(up_f[...], gy[...])).astype(BF)
        acc_f[...] = jnp.zeros_like(acc_f)
        acc_c[...] = jnp.zeros_like(acc_c)
        ffo[...] = jnp.zeros_like(ffo)
        dmc[...] = jnp.zeros_like(dmc)

    def units(key, value, smalls):
        pre, dsq = mm(key, mct[...]), mm(value, gyt[...])
        rows = key.shape[0] // len(smalls)
        hqs, dps, grads = [], [], []
        for b, small in enumerate(smalls):
            s = slice(b * rows, (b + 1) * rows)
            down_f, up_c = small[:RANK], small[RANK:]
            active = jnp.maximum(pre[s] + SCALE * mm_tn(up_c, h_c[...]), 0.0)
            hq = (active * active).astype(BF)
            dpre = ((dsq[s] + mm_tn(down_f, dh_f[...])) * (2.0 * active)).astype(BF)
            grads.append((mm_nt(dh_f[...], hq), SCALE * mm_nt(h_c[...], dpre)))
            acc_f[...] += mm(down_f, hq)
            acc_c[...] += mm(up_c, dpre)
            hqs.append(hq)
            dps.append(dpre)
        ffo[...] += mm_tn(jnp.concatenate(hqs, 0), value)
        dmc[...] += mm_tn(jnp.concatenate(dps, 0), key)
        return grads

    @pl.when(step < last + (0 if late else 1))
    def _():
        key = jnp.concatenate([kv[b, :ff] for b in range(per)], 0)
        value = jnp.concatenate([kv[b, ff:] for b in range(per)], 0)
        grads = units(key, value, [hidden[b, :, :ff] for b in range(per)])
        for b, (low, high) in enumerate(grads):
            if late:
                g_hidden[b] = jnp.zeros(g_hidden.shape[1:], F32)
            g_hidden[b, :RANK, :ff], g_hidden[b, RANK:, :ff] = low, high

    @pl.when(step == last)
    def _():
        if late:
            g.finish()
            flat = lambda ref: ref[...].reshape(-1, ref.shape[-1])
            ((low, high),) = units(flat(key_late), flat(value_late), [hidden_late[...]])
            part = low.shape[1] // 8
            for p in range(8):
                at = slice(p * part, (p + 1) * part)
                g_late[p, :, :part], g_late[p, :, part:] = low[:, at], high[:, at]
        h_f = acc_f[...].astype(BF)
        out[...] = (middle[...] + ffo[...] + SCALE * mm_tn(h_f, up_f[...])).astype(BF)
        g_up_f[...] = SCALE * mm(h_f, gy[...])
        dh_c = (SCALE * acc_c[...]).astype(BF)
        d = dmc[...] + mm_tn(dh_c, down_c[...])
        dmc[...] = d
        first[...] = d[:8] * norm[17:18, :]
        if late:
            mine[1] = first[...]
            trade(1, jnp.logical_not(ends), jnp.logical_not(starts), -1)
            d_edge[...] = came[1]
        g_down_c[...] = mm(dh_c, mc[...])


def late_units(n_seq, n_dp, ff):
    return ff // 8 if (n_seq, n_dp) == (8, 4) and ff % 128 == 0 else 0


def channel(n2, edge, norm, gy, middle, down_c, up_f, kv, hidden, key_shard, value_shard, hidden_late):
    n, both, width = kv.shape
    ff, length, late = hidden.shape[2], n2.shape[0], key_shard.shape[0]
    per = max(1, min(n, 512 // ff))
    steps = n // per
    block = lambda shape: pl.BlockSpec(
        (per,) + tuple(shape[1:]), lambda i: (jnp.minimum(i, steps - 1), 0, 0)
    )
    far = lambda shape: pl.BlockSpec(memory_space=pl.ANY)
    shape = jax.ShapeDtypeStruct
    rank = shape((RANK, width), F32)
    ins = [(whole, a) for a in (n2, edge, norm, gy, middle, down_c, up_f)] + [(block, kv), (block, hidden)]
    outs = [
        (result, shape((length, width), BF)),
        (result, shape((length, width), F32)),
        (result, shape((8, width), F32)),
        (block, shape((n, 2 * RANK, ff), F32)),
        (result, rank),
        (result, rank),
    ]
    scratch = [
        pltpu.VMEM((length, width), BF),
        pltpu.VMEM((width, length), BF),
        pltpu.VMEM((width, length), BF),
        pltpu.VMEM((length, width), F32),
        pltpu.VMEM((RANK, length), BF),
        pltpu.VMEM((RANK, length), BF),
        pltpu.VMEM((RANK, length), F32),
        pltpu.VMEM((RANK, length), F32),
    ]
    params = {}
    if late:
        ins += [(far, key_shard), (far, value_shard), (whole, hidden_late)]
        outs += [(result, shape((8, RANK, 2 * n * late // 8), F32)), (result, shape((8, width), F32))]
        scratch += [pltpu.VMEM((n, late, width), BF)] * 2
        scratch += [pltpu.VMEM((2, 8, width), F32)] * 2 + [pltpu.SemaphoreType.DMA((2, 2))]
        scratch += gather_scratch(2)
        params = dict(collective_id=4, has_side_effects=True)
    return over_tiles(
        functools.partial(channel_kernel, late), steps + (1 if late else 0), ins, outs, "channel", scratch, **params
    )


HALF = 512


def branch_masks(shape):
    lane = iota(shape, 1)
    lo, hi = DECAY_INNER, DECAY_INNER + RATE_INNER
    return lane < lo, (lane >= lo) & (lane < hi), (lane >= hi) & (lane < hi + GATE_INNER)


def project_kernel(
    hat, hat_prev, valid, vec, first, chosen, second, w_r, w_k, w_v, up,
    rr, kr, vr, wl, al, gg, m_r, m_k, m_v, hs, act, act_low,
):
    @pl.when(pl.program_id(0) == 0)
    def _():
        n1 = hat[...] * vec[0:1, :] + vec[1:2, :]
        change = (hat_prev[...] * vec[0:1, :] + vec[1:2, :]) * valid[...] - n1
        mixed = lambda i: (n1 + change * vec[2 + i : 3 + i, :]).astype(BF)
        m_r[...], m_k[...], m_v[...] = mixed(0), mixed(2), mixed(3)
        for i, m in enumerate((m_r, m_k, m_v)):
            hs[i] = mm_nt(m[...], chosen[i * RANK : (i + 1) * RANK, :]).astype(BF)
        t_w = mm(mixed(1), first[...])
        t_a = mm(mixed(4), first[...])
        t_g = mm(mixed(5), first[...])
        is_w, is_a, is_g = branch_masks(t_w.shape)
        zero = jnp.zeros_like(t_w)
        t_w = jnp.where(is_w, jnp.tanh(t_w), zero)
        t_a = jnp.where(is_a, t_a, zero)
        t_g = jnp.where(is_g, jax.nn.sigmoid(t_g), zero)
        act[...] = t_w + t_a + t_g
        act_low[0], act_low[1], act_low[2] = t_w.astype(BF), t_a.astype(BF), t_g.astype(BF)

    for i, (m, w, out) in enumerate(((m_r, w_r, rr), (m_k, w_k, kr), (m_v, w_v, vr))):
        out[...] = mm_nt(m[...], w[...]) + SCALE * mm(hs[i], up[(5 + i) * RANK : (6 + i) * RANK, :])
    for i, out in enumerate((wl, al, gg)):
        out[...] = mm_nt(act_low[i], second[...])


def final_kernel(
    n, fast, drr, dkr, dvr, dwl, dal, dgg, m_r, m_k, m_v, hs, act, chosen, second, down_o, up_o, hat, rstd, d_mid, vecs,
    w_r, w_k, w_v, down, first, vec, *refs,
):
    step, last = pl.program_id(0), pl.num_programs(0) - 1
    me, dp = lax.axis_index("seq"), lax.axis_index("dp")
    if fast:
        early, picks, grad, g_model, g_hidden, *refs = refs
        stage_m, stage_h, from_m, from_h, own_send, own_recv, *refs = refs
    else:
        grad, summed, *refs = refs
    stay, go, dhs, d_act, parts, here, came, send_sem, recv_sem, edge_sem = refs

    def to_owner(k, i):
        peer = lax.rem(dp + k, 4)
        stage, slots = ((stage_m, from_m), (stage_h, from_h))[i]
        return pltpu.make_async_remote_copy(
            src_ref=stage.at[peer],
            dst_ref=slots.at[k - 1],
            send_sem=own_send.at[i, k - 1],
            recv_sem=own_recv.at[i, k - 1],
            device_id=(me, peer),
            device_id_type=MESH,
        )

    def copy(k):
        peer = lax.rem(me + k, n)
        return pltpu.make_async_remote_copy(
            src_ref=parts.at[peer],
            dst_ref=here.at[k - 1],
            send_sem=send_sem.at[k - 1],
            recv_sem=recv_sem.at[k - 1],
            device_id=(peer, dp),
            device_id_type=MESH,
        )

    def edge(to):
        return pltpu.make_async_remote_copy(
            src_ref=go.at[0:8],
            dst_ref=came,
            send_sem=edge_sem.at[0],
            recv_sem=edge_sem.at[1],
            device_id=(to, dp),
            device_id_type=MESH,
        )

    @pl.when(step == 0)
    def _():
        came[...] = jnp.zeros_like(came)
        barrier = pltpu.get_barrier_semaphore()
        for k in range(1, n):
            pl.semaphore_signal(
                barrier, inc=1, device_id=(lax.rem(me + k, n), dp), device_id_type=MESH
            )
        if fast:
            for k in range(1, 4):
                pl.semaphore_signal(
                    barrier, inc=1, device_id=(me, lax.rem(dp + k, 4)), device_id_type=MESH
                )
        rows = [None] * 6 + [down_o[...], up_o[...]]
        for i, (d, m) in enumerate(((drr, m_r), (dkr, m_k), (dvr, m_v))):
            dh = (SCALE * mm_nt(d[...], chosen[(5 + i) * RANK : (6 + i) * RANK, :])).astype(BF)
            dhs[i] = dh
            rows[i], rows[3 + i] = mm_tn(dh, m[...]), SCALE * mm_tn(hs[i], d[...])
        wide = parts.shape[2]
        for i, r in enumerate(rows):
            for p in range(n):
                parts[p, i * RANK : (i + 1) * RANK, :] = r[:, p * wide : (p + 1) * wide].astype(BF)
        pl.semaphore_wait(barrier, n - 1 + (3 if fast else 0))
        for k in range(1, n):
            copy(k).start()
        is_w, is_a, is_g = branch_masks(act.shape)
        a = act[...]
        zero = jnp.zeros_like(a)
        d_act[0] = jnp.where(is_w, mm(dwl[...], second[...]) * (1.0 - a * a), zero).astype(BF)
        d_act[1] = jnp.where(is_a, mm(dal[...], second[...]), zero).astype(BF)
        d_act[2] = jnp.where(is_g, mm(dgg[...], second[...]) * a * (1.0 - a), zero).astype(BF)

    total, moved = None, None
    for i, (d, w, at) in enumerate(((drr, w_r, 2), (dkr, w_k, 4), (dvr, w_v, 5))):
        g = mm(d[...], w[...]) + mm(dhs[i], down[i * RANK : (i + 1) * RANK, :])
        move = g * vec[at : at + 1, :]
        total, moved = (g, move) if total is None else (total + g, moved + move)
    for i, at in enumerate((3, 6, 7)):
        g = mm_nt(d_act[i], first[...])
        total, moved = total + g, moved + g * vec[at : at + 1, :]
    tile = pl.ds(pl.multiple_of(step * TILE, TILE), TILE)
    stay[:, tile] = total - moved
    go[:, tile] = moved

    @pl.when(step == last)
    def _():
        pl.when(me > 0)(lambda: edge(me - 1).start())
        for k in range(1, n):
            copy(k).wait()
        t = parts[me].astype(F32)
        for k in range(1, n):
            t = t + here[k - 1].astype(F32)
        if fast:
            e = early[...]
            r = lambda x, i, k: x[i * RANK : (i + k) * RANK]
            rows = jnp.concatenate(
                [r(t, 0, 3), r(t, 6, 1), r(e, 0, 1), r(t, 3, 3), r(t, 7, 1), r(e, 1, 1)], 0
            )
            tails = e[10 * RANK : 11 * RANK]
            lane = iota((2 * RANK, PW), 1)
            for j in range(4):
                two = rows[:, (j // 2) * PW : (j // 2 + 1) * PW]
                stage_m[j] = pltpu.roll(two, D, axis=1) if j % 2 else two
                mine = e[(2 + 2 * j) * RANK : (4 + 2 * j) * RANK]
                tail = jnp.concatenate([tails[:, :PW], tails[:, PW:]], 0)
                shift = (3 - j) * (PW // 4)
                tail = pltpu.roll(tail, shift, axis=1) if shift else tail
                stage_h[j, :, :PW] = mine[:, :PW]
                stage_h[j, :, PW:] = jnp.where(lane >= 3 * PW // 4, tail, mine[:, PW:])
            for k in range(1, 4):
                to_owner(k, 0).start()
                to_owner(k, 1).start()
        else:
            summed[...] = t
        pl.when(me < n - 1)(lambda: edge(me + 1).wait_recv())
        size = go.shape[0]
        g = pltpu.roll(go[...], size - 1, axis=0)
        g = stay[...] + jnp.where(iota(g.shape, 0) == size - 1, came[0:1, :], g)
        dhat = g * vecs[0:1, :]
        grad[...] = d_mid[...] + rstd[...] * (
            dhat
            - jnp.mean(dhat, axis=-1, keepdims=True)
            - hat[...] * jnp.mean(dhat * hat[...], axis=-1, keepdims=True)
        )
        pl.when(me > 0)(lambda: edge(me - 1).wait_send())
        if fast:
            for k in range(1, 4):
                to_owner(k, 0).wait()
                to_owner(k, 1).wait()
            found = [(dp, stage_m[dp], stage_h[dp])]
            found += [(lax.rem(dp + 4 - k, 4), from_m[k - 1], from_h[k - 1]) for k in range(1, 4)]
            adapters = g_model.shape[0]
            weights = [picks[pl.ds(pl.multiple_of(q * adapters, 8), adapters), :] for q, _, _ in found]
            for a in range(adapters):
                m, h = None, None
                for w, (_, x, y) in zip(weights, found):
                    w = w[a : a + 1, :]
                    x, y = x * w, y * jnp.concatenate([w, w], 1)
                    m, h = (x, y) if m is None else (m + x, h + y)
                g_model[a], g_hidden[a] = m[:, :D], h


def shifted(block, axis, distance):
    devices = range(lax.axis_size(axis))
    route = [(i - distance, i) for i in devices if i - distance in devices]
    return lax.ppermute(block, axis, route)


def mm(a, b):
    return lax.dot_general(a, b, DIMS["nn"], preferred_element_type=F32)


def mm_nt(a, b):
    return lax.dot_general(a, b, DIMS["nt"], preferred_element_type=F32)


def mm_tn(a, b):
    return lax.dot_general(a, b, DIMS["tn"], preferred_element_type=F32)


def body(tokens, output_gradient, index, proj, first, second, vectors, ckey, cvalue, model_rows, hidden_rows):
    axes = ("seq", "dp")
    n_seq, n_dp = lax.axis_size("seq"), lax.axis_size("dp")
    n = n_seq * n_dp
    tokens, gy = tokens[0], output_gradient[0]
    length, width = tokens.shape
    nc, tiles = length // C, width // TILE
    adapters, kinds, cols = model_rows.shape
    ff, inner, nvec = ckey.shape[1], first.shape[1], vectors.shape[0]

    key_shard, soon = ckey.T, ff - late_units(n_seq, n_dp, ff)
    kv = lax.all_gather(jnp.concatenate([key_shard[:soon], cvalue[:soon]], 0), axes, axis=0)

    index_all = lax.all_gather(index, "dp", axis=0, tiled=True)
    pick = index_all[:, None] == jnp.arange(adapters, dtype=jnp.int32)[None, :]
    pick_low = pick.astype(BF)
    fast = own_gather() and (cols, ff, 2 * inner + nvec) == (D, 2 * PW, 914)
    if fast:
        half = kinds // 2
        few = jnp.concatenate(
            [
                jnp.concatenate([model_rows[:, :half], model_rows[:, half:]], 2),
                hidden_rows[:, :, :PW],
                hidden_rows[:, :, PW:],
            ],
            1,
        )
    else:
        few = jnp.concatenate([model_rows.reshape(adapters, -1), hidden_rows.reshape(adapters, -1)], 1)
        few = few.reshape(adapters, -1, 128)
    few = jnp.einsum("sa,arx->srx", pick_low, few, preferred_element_type=F32).astype(BF)
    pad = lambda k: jnp.zeros((cols, k), BF)
    misc = jnp.concatenate(
        [first, pad(HALF - inner), second.T, vectors.T, pad(HALF - inner - nvec)], axis=1
    )
    turned = jnp.swapaxes(proj, 1, 2)

    wide = tokens.astype(F32)
    ahead = shifted(tokens[-1:], "seq", 1).astype(F32)
    rows = jnp.concatenate([ahead, wide], 0)
    centre = rows - jnp.mean(rows, axis=-1, keepdims=True)
    rstd = lax.rsqrt(jnp.mean(centre * centre, axis=-1, keepdims=True) + NORM_EPS)
    hat = centre * rstd
    start = (jnp.arange(length)[:, None] == 0) & (lax.axis_index("seq") == 0)
    valid = jnp.where(start, 0.0, 1.0).astype(F32)
    hat_prev, hat, rstd = hat[:-1], hat[1:], rstd[1:]

    few = few.reshape((2, -1, 128) if fast else (-1, 128))
    *mats, misc, few_all = gather([turned[0], turned[1], turned[2], turned[3], misc, few])
    mats = [m.reshape(width, width) for m in mats]
    misc = misc.reshape(width, -1)
    if fast:
        chosen, hidden, hidden_late, vec = sort_small(kinds, ff - soon, nvec, few_all, misc)
    else:
        vec = misc[:, HALF + inner : HALF + inner + nvec].T.astype(F32)
        own = lax.dynamic_index_in_dim(few_all.reshape(n, n_dp, -1, 128), lax.axis_index("dp"), 1, False)
        own = own.reshape(n, -1)
        chosen = own[:, : kinds * cols].reshape(n, kinds, cols).transpose(1, 0, 2).reshape(kinds, width)
        hidden, hidden_late = own[:, kinds * cols :].reshape(n, 2 * RANK, ff), None
    down = lambda i: chosen[i * RANK : (i + 1) * RANK]
    up = lambda i: chosen[(5 + i) * RANK : (6 + i) * RANK]

    shape = jax.ShapeDtypeStruct
    full, low = shape((length, width), F32), shape((length, width), BF)
    small, rank = shape((D, width), F32), shape((RANK, width), F32)
    firsts = pl.BlockSpec((width, HALF), lambda i: (0, 0))
    seconds = pl.BlockSpec((width, HALF), lambda i: (0, 1))
    first_rows = pl.BlockSpec((TILE, HALF), lambda i: (i, 0))
    second_rows = pl.BlockSpec((TILE, HALF), lambda i: (i, 1))
    rr, kr, vr, wl, al, gg, m_r, m_k, m_v, hs, act = over_tiles(
        project_kernel, tiles,
        [
            (whole, hat), (whole, hat_prev), (whole, valid), (whole, vec), (firsts, misc), (whole, chosen),
            (second_rows, misc), (tile_rows, mats[0]), (tile_rows, mats[1]), (tile_rows, mats[2]), (cut, chosen),
        ],
        [(cut, full)] * 6
        + [(result, low)] * 3
        + [(result, shape((3, length, RANK), BF)), (result, shape((length, HALF), F32))],
        "project",
        [pltpu.VMEM((3, length, HALF), BF)],
    )
    one, two, each = in_turn(tiles, "first"), in_turn(tiles, "second"), in_turn(tiles, "both")
    keep = pltpu.VMEM((tiles, length, TILE), F32)
    keep_small = pltpu.VMEM((tiles, D, TILE), F32)
    reff, xs, mt, turned, gated, o, us, zs, middle, n2, h_o = over_tiles(
        functools.partial(rec_forward, nc, n_seq, tiles), 2 * tiles,
        [
            (each, rr), (each, kr), (each, vr), (one, wl), (each, al), (two, gg), (each, vec),
            (whole, tokens), (two, mats[3]), (two, down(3)), (whole, up(3)), (whole, vec),
        ],
        [(one, full), (one, full), (one, full), (one, small), (two, low), (two, full), (two, full), (two, full)]
        + [(result, full), (result, full), (result, shape((length, RANK), BF))],
        "rec_forward",
        [keep] * 6 + [keep_small] * 2 + [pltpu.VMEM((length, RANK), F32)] + hand_scratch(tiles),
        collective_id=0, has_side_effects=True,
    )
    soon_only = soon == ff
    row = shifted(n2[-1:], "seq", 1) if soon_only else n2[-1:]
    out, d_mc, moved, g_hidden, up_f, down_c, *more = channel(
        n2, row, vec, gy, middle, down(4), up(4), kv, hidden,
        key_shard[soon:], cvalue[soon:], hidden_late,
    )
    wide = n_dp * cols
    by_piece = lambda rows: jnp.swapaxes(rows.reshape(-1, n_seq, wide), 0, 1)
    parts = [by_piece(jnp.concatenate([down_c, up_f], 0)), g_hidden.reshape(n_seq, -1, wide)]
    if soon_only:
        edge = jnp.broadcast_to(shifted(moved[:1], "seq", -1), (8, width))
    else:
        g_late, edge = more
        parts.append(g_late)
    early, edge = lax.optimization_barrier((jnp.concatenate(parts, 1), edge))
    early = lax.psum_scatter(early, "seq", scatter_dimension=0, tiled=True)[0]
    d_mid, dgg, down_o, up_o, drr, dkr, dvr, dwl, dal = over_tiles(
        functools.partial(rec_backward, nc, n_seq, tiles), 2 * tiles,
        [
            (whole, d_mc), (whole, edge), (whole, gy), (whole, middle), (whole, vec), (one, mats[3]),
            (one, down(3)), (whole, up(3)), (whole, h_o), (one, gated), (one, gg), (one, o),
            (each, rr), (each, kr), (each, vr), (two, wl), (each, al), (each, vec),
            (one, reff), (each, mt), (one, turned), (two, xs), (two, us), (two, zs),
        ],
        [(result, full), (one, low), (one, rank), (result, rank)] + [(two, low)] * 5,
        "rec_backward",
        [pltpu.VMEM((length, width), BF), pltpu.VMEM((length, RANK), BF)]
        + [keep] * 3 + [keep_small] * 2 + hand_scratch(tiles),
        collective_id=1, has_side_effects=True,
    )
    early, drr = lax.optimization_barrier((early, drr))
    ins = [(whole, a) for a in (drr, dkr, dvr, dwl, dal, dgg, m_r, m_k, m_v, hs, act, chosen)]
    ins += [(pl.BlockSpec((width, HALF), lambda i: (0, 1), pipeline_mode=pl.Buffered(1)), misc)]
    ins += [(whole, a) for a in (down_o, up_o, hat, rstd, d_mid, vec)]
    ins += [(cut, mats[0]), (cut, mats[1]), (cut, mats[2]), (cut, chosen), (first_rows, misc), (cut, vec)]
    scratch = [
        pltpu.VMEM((length, width), F32),
        pltpu.VMEM((length, width), F32),
        pltpu.VMEM((3, length, RANK), BF),
        pltpu.VMEM((3, length, HALF), BF),
        pltpu.VMEM((n_seq, 8 * RANK, wide), BF),
        pltpu.VMEM((n_seq - 1, 8 * RANK, wide), BF),
        pltpu.VMEM((8, width), F32),
        pltpu.SemaphoreType.DMA((n_seq - 1,)),
        pltpu.SemaphoreType.DMA((n_seq - 1,)),
        pltpu.SemaphoreType.DMA((2,)),
    ]
    ready = fast and adapters == 8 and not soon_only
    call = lambda ins, outs, scratch: over_tiles(
        functools.partial(final_kernel, n_seq, ready), tiles, ins, [(result, full)] + outs, "final", scratch,
        collective_id=3, has_side_effects=True,
    )
    if ready:
        picks = jnp.broadcast_to(pick.astype(F32).reshape(-1, 1), (n_dp * adapters, PW))
        grad_tokens, grad_model, h = call(
            ins + [(whole, early), (whole, picks)],
            [(result, shape((adapters, kinds, cols), F32)), (result, shape((adapters, 2 * RANK, ff), F32))],
            [pltpu.VMEM((4, kinds, PW), F32), pltpu.VMEM((4, 2 * RANK, ff), F32)]
            + [pltpu.VMEM((3, kinds, PW), F32), pltpu.VMEM((3, 2 * RANK, ff), F32)]
            + [pltpu.SemaphoreType.DMA((2, 3))] * 2
            + scratch,
        )
        return out[None], grad_tokens[None], grad_model, h
    grad_tokens, late = call(ins, [(result, shape((8 * RANK, wide), F32))], scratch)
    mine = early[2 * RANK : 2 * RANK + 2 * RANK * ff // cols].reshape(n_dp, 2 * RANK, ff)
    if not soon_only:
        tail = early[2 * RANK + 2 * RANK * ff // cols :].reshape(RANK, 2, n_dp, ff - soon)
        tail = tail.transpose(2, 1, 0, 3).reshape(n_dp, 2 * RANK, ff - soon)
        mine = jnp.concatenate([mine[:, :, :soon], tail], 2)
    columns = jnp.concatenate([early[: 2 * RANK], late], 0).reshape(10 * RANK, n_dp, cols)
    both = jnp.concatenate(
        [jnp.swapaxes(columns, 0, 1).reshape(n_dp, -1), mine.reshape(n_dp, -1)], 1
    )
    both = lax.all_to_all(both, "dp", split_axis=0, concat_axis=0, tiled=True)
    both = jnp.einsum("sa,sx->ax", pick.astype(F32), both, precision=PRECISE)
    at = 10 * RANK * cols
    a = both[:, :at].reshape(adapters, 10 * RANK, cols)
    h = both[:, at:].reshape(adapters, 2 * RANK, ff)
    block = lambda i, k: a[:, i * RANK : (i + k) * RANK]
    grad_model = jnp.concatenate(
        [block(2, 3), block(8, 1), block(0, 1), block(5, 3), block(9, 1), block(1, 1)], axis=1
    )
    return out[None], grad_tokens[None], grad_model, h


def solution(mesh):
    cols = P(None, ("seq", "dp"))
    rows = P(("seq", "dp"), None)
    deep = P(None, None, ("seq", "dp"))
    act = P("dp", "seq", None)
    return jax.shard_map(
        body,
        mesh=mesh,
        in_specs=(act, act, P("dp"), deep, rows, cols, cols, cols, rows, deep, deep),
        out_specs=(act, act, deep, deep),
        check_vma=False,
    )
```

```python
import functools
import math

import jax
import jax.numpy as jnp
from jax import lax
from jax.experimental import pallas as pl
from jax.experimental.pallas import tpu as pltpu
from jax.sharding import PartitionSpec as P

F32, BF = jnp.float32, jnp.bfloat16
MESH = pl.DeviceIdType.MESH
D = 64
C = 64
PW = 2 * D
DECAY_INNER, RATE_INNER, GATE_INNER, RANK = 96, 96, 256, 16
SCALE = 4.0
NORM_EPS, GROUP_EPS, UNIT_EPS = 1e-05, 0.00064, 1e-06
DECAY_SCALE = math.exp(-0.5)
PRECISE = lax.Precision.HIGHEST
DIMS = {
    "nn": (((1,), (0,)), ((), ())),
    "nt": (((1,), (1,)), ((), ())),
    "tn": (((0,), (0,)), ((), ())),
}


def split(x):
    hi = x.astype(BF)
    return hi, (x - hi.astype(F32)).astype(BF)


def dot1(a, b, m="nn"):
    return lax.dot_general(a.astype(BF), b.astype(BF), DIMS[m], preferred_element_type=F32)


def dot3(a, b, m="nn"):
    ah, al = split(a)
    bh, bl = split(b)
    ka, kb = (0 if m == "tn" else 1), (1 if m == "nt" else 0)
    n = b.shape[1 - kb]
    aa = jnp.concatenate([ah, al], axis=ka)
    bb = jnp.concatenate([jnp.concatenate([bh, bl], axis=1 - kb)] * 2, axis=kb)
    r = lax.dot_general(aa, bb, DIMS[m], preferred_element_type=F32)
    return r[:, :n] + r[:, n:]


dot_inv = dot_a = dot3
dot_w = dot_b = dot_g = dot1


def iota(shape, axis):
    return lax.broadcasted_iota(jnp.int32, shape, axis)


def stack2(x):
    lane = iota(x.shape, 1)
    zero = jnp.zeros_like(x)
    return jnp.concatenate([jnp.where(lane < D, x, zero), jnp.where(lane < D, zero, x)], axis=0)


def pack2(x):
    h = x.shape[0] // 2
    return x[:h] + x[h:]


def head_ones():
    r, c = iota((2 * PW, PW), 0) % PW, iota((2 * PW, PW), 1)
    return jnp.where((r // D) == (c // D), 1.0, 0.0).astype(BF)


def headsum(x, ones):
    h, l = split(x)
    return lax.dot_general(
        jnp.concatenate([h, l], axis=1), ones, DIMS["nn"], preferred_element_type=F32
    )


def triangle(upper):
    r, c = iota((C, C), 0), iota((C, C), 1)
    return jnp.where((r <= c) if upper else (r >= c), 1.0, 0.0).astype(BF)


def cums(x, tri):
    h, l = split(x)
    m = (x - h.astype(F32) - l.astype(F32)).astype(BF)
    n = x.shape[1]
    r = lax.dot_general(
        tri, jnp.concatenate([h, l, m], axis=1), DIMS["nn"], preferred_element_type=F32
    )
    return r[:, :n] + r[:, n : 2 * n] + r[:, 2 * n :]


def prelude(kr, wl, al, w0, a0, k_k, k_a, ones):
    s = jax.nn.sigmoid(w0 + wl)
    a = jax.nn.sigmoid(a0 + al)
    kx = kr * k_k
    rn = lax.rsqrt(headsum(kx * kx, ones) + UNIT_EPS)
    return s, -DECAY_SCALE * s, a, rn, kx * rn, kr * (1.0 + (a - 1.0) * k_a)


def grid_ids():
    r, c = iota((PW, PW), 0), iota((PW, PW), 1)
    return r, c, (r // D) == (c // D)


def inverses(many):
    r, c, _ = grid_ids()
    eye = jnp.where(r == c, 1.0, 0.0)
    b = 1
    while b < C:
        level = ((r // (2 * b)) == (c // (2 * b))) & ((r // b) % 2 == 1) & ((c // b) % 2 == 0)
        parts = [jnp.where(level, a, 0.0) for a in many]
        if b == 1:
            xs = [eye + p for p in parts]
        else:
            half = [dot_inv(x, p) for x, p in zip(xs, parts)]
            xs = [x + dot_inv(h, x) for h, x in zip(half, xs)]
        b *= 2
    return xs


def factors(logw, tri):
    run = cums(logw, tri)
    return jnp.exp(run - logw), jnp.exp(run), jnp.exp(-run), jnp.exp(run[C - 1 : C])


def forward_chunks(units, tri):
    rows, cols, same = grid_ids()
    zero = jnp.zeros((PW, PW), F32)
    strict, incl = (rows > cols) & same, (rows >= cols) & same
    fs = [factors(u[5], tri) for u in units]
    p2 = [stack2(u[1] * f[0]) for u, f in zip(units, fs)]
    r2 = [stack2(u[0] * f[1]) for u, f in zip(units, fs)]
    q2 = [stack2(u[2] * f[2]) for u, f in zip(units, fs)]
    k2 = [stack2(u[3] * f[2]) for u, f in zip(units, fs)]
    v2 = [stack2(u[4]) for u in units]
    aa = [
        dot_a(jnp.concatenate([p, r], 0), jnp.concatenate([q, k], 0), "nt")
        for p, r, q, k in zip(p2, r2, q2, k2)
    ]
    apk = [jnp.where(strict, a[:PW, PW:], zero) for a in aa]
    y = [dot_w(a, v) for a, v in zip(apk, v2)]
    xs = inverses([jnp.where(strict, a[:PW, :PW], zero) for a in aa])
    ww = [dot_w(x, jnp.concatenate([p, t], 1)) for x, p, t in zip(xs, p2, y)]
    left = [
        jnp.concatenate(
            [
                jnp.concatenate(
                    [jnp.where(incl, a[PW:, :PW], zero), jnp.where(incl, a[PW:, PW:], zero)], 1
                ),
                jnp.concatenate([(q * f[3]).T, (k * f[3]).T], 1),
            ],
            0,
        )
        for a, q, k, f in zip(aa, q2, k2, fs)
    ]
    right = [
        jnp.concatenate([w, jnp.concatenate([zero, v], 1)], 0) for w, v in zip(ww, v2)
    ]
    big = [dot_b(l, r) for l, r in zip(left, right)]
    move = [
        b[PW:, :PW] + jnp.where(rows == cols, jnp.broadcast_to(f[3], (PW, PW)), zero)
        for b, f in zip(big, fs)
    ]
    return [
        (pack2(r + b[:PW, :PW]), pack2(b[:PW, PW:]), m, b[PW:, PW:], pack2(w[:, :PW]), pack2(w[:, PW:]), x)
        for r, b, m, w, x in zip(r2, big, move, ww, xs)
    ]


def backward_chunks(units, tri, tri_up):
    rows, cols, same = grid_ids()
    zero = jnp.zeros((PW, PW), F32)
    strict, incl = (rows < cols) & same, (rows <= cols) & same
    both = jnp.concatenate([jnp.concatenate([strict, incl], 1)] * 2, 0)
    fs = [factors(t[5], tri) for t in units]
    pe = [t[1] * f[0] for t, f in zip(units, fs)]
    re = [t[0] * f[1] for t, f in zip(units, fs)]
    qe = [t[2] * f[2] for t, f in zip(units, fs)]
    ke = [t[3] * f[2] for t, f in zip(units, fs)]
    g2 = [stack2(t[10]) for t in units]
    qk = [jnp.concatenate([stack2(q), stack2(k)], 0) for q, k in zip(qe, ke)]
    pr = [jnp.concatenate([stack2(p), stack2(r)], 0) for p, r in zip(pe, re)]
    at = [dot_a(a, b, "nt") for a, b in zip(qk, pr)]
    qkh = [
        dot_g(jnp.concatenate([q * f[3], k * f[3]], 0), t[9])
        for q, k, f, t in zip(qe, ke, fs, units)
    ]
    sq = [dot_g(jnp.concatenate([t[7], t[4]], 0), t[9], "nt") for t in units]
    du = [
        dot_g(jnp.where(incl, a[:PW, PW:], zero), g) + stack2(h[:C])
        for a, g, h in zip(at, g2, qkh)
    ]
    dm = [dot_g(t[6], d, "tn") for t, d in zip(units, du)]
    dg = [jnp.concatenate([d, g], 0) for d, g in zip(dm, g2)]
    dv = [
        pack2(
            dot_g(
                jnp.concatenate(
                    [jnp.where(strict, a[PW:, :PW], zero), jnp.where(incl, a[PW:, PW:], zero)], 1
                ),
                d,
            )
        )
        + h[C:]
        for a, d, h in zip(at, dg, qkh)
    ]
    dat = [
        dot_g(jnp.concatenate([stack2(t[7]), stack2(t[4])], 0), d, "nt")
        for t, d in zip(units, dg)
    ]
    dat = [jnp.where(both, d, jnp.zeros_like(d)) for d in dat]
    dpr = [dot_g(d, a, "tn") for d, a in zip(dat, qk)]
    dqk = [dot_g(d, a) for d, a in zip(dat, pr)]
    sp = [dot_g(jnp.concatenate([pack2(d), t[10]], 0), t[8], "nt") for d, t in zip(dm, units)]
    outs = []
    for i, t in enumerate(units):
        eb, el, en, last = fs[i]
        dp, dr = pack2(dpr[i][:PW]) + sp[i][:C], pack2(dpr[i][PW:]) + sp[i][C:]
        dqh, dkh = sq[i][:C], sq[i][C:]
        dq, dk = pack2(dqk[i][:PW]) + dqh * last, pack2(dqk[i][PW:]) + dkh * last
        tail = jnp.sum((qe[i] * dqh + ke[i] * dkh) * last, axis=0, keepdims=True)
        tail = tail + last * jnp.sum((t[8] * t[9]).T, axis=0, keepdims=True)
        gb = pe[i] * dp
        gl = re[i] * dr - qe[i] * dq - ke[i] * dk
        dlogw = cums(gl + gb, tri_up) - gb + tail
        outs.append((dr * el, dp * eb, dq * en, dk * en, dv[i], dlogw))
    return outs


def lanes(ref):
    return [slice(i * PW, (i + 1) * PW) for i in range(ref.shape[-1] // PW)]


def norm_parts(o, ones):
    centre = o - headsum(o, ones) * (1.0 / D)
    rstd = lax.rsqrt(headsum(centre * centre, ones) * (1.0 / D) + GROUP_EPS)
    return centre * rstd, rstd


def hand_on(n, half, back, move, add, here, send, send_sem, recv_sem):
    step, last = pl.program_id(0), pl.num_programs(0) - 1
    s, d = lax.axis_index("seq"), lax.axis_index("dp")
    at = n - 1 - s if back else s
    first, final = at == 0, at == n - 1
    nxt, prv = (s - 1, s + 1) if back else (s + 1, s - 1)
    begins, goes = jnp.logical_not(first), jnp.logical_not(final)
    tile = step - jnp.minimum(at, half)
    now = jnp.logical_and(tile >= 0, tile < half)

    def copy(i, to):
        return pltpu.make_async_remote_copy(
            src_ref=send.at[i],
            dst_ref=here.at[i],
            send_sem=send_sem.at[i],
            recv_sem=recv_sem.at[i],
            device_id=(to, d),
            device_id_type=MESH,
        )

    @pl.when(jnp.logical_and(step == 0, begins))
    def _():
        pl.semaphore_signal(
            pltpu.get_barrier_semaphore(), inc=1, device_id=(prv, d), device_id_type=MESH
        )

    @pl.when(jnp.logical_and(step == 0, goes))
    def _():
        pl.semaphore_wait(pltpu.get_barrier_semaphore(), 1)

    @pl.when(jnp.logical_and(now, first))
    def _():
        here[tile] = jnp.zeros(here.shape[1:], F32)

    @pl.when(jnp.logical_and(now, begins))
    def _():
        copy(tile, prv).wait_recv()

    @pl.when(jnp.logical_and(now, goes))
    def _():
        for ln in lanes(here):
            send[tile, :, ln] = dot3(move[tile, :, ln], stack2(here[tile, :, ln])) + add[tile, :, ln]
        copy(tile, nxt).start()

    @pl.when(jnp.logical_and(step == last, goes))
    def _():
        for i in range(half):
            copy(i, nxt).wait_send()


def hand_scratch(steps):
    return [
        pltpu.VMEM((steps, D, TILE), F32),
        pltpu.VMEM((steps, D, TILE), F32),
        pltpu.SemaphoreType.DMA((steps,)),
        pltpu.SemaphoreType.DMA((steps,)),
    ]


def rec_forward(
    nc, n, half, rr, kr, vr, wl, al, gg, vec, tokens, wo, down, up, norm,
    reff, xs, mt, turned, z_out, o_out, u_out, zs, middle, normed, h_out,
    k_reff, k_oloc, k_w1, k_w2, k_m, k_n, move, add, acc_h, *hand,
):
    step, last = pl.program_id(0), pl.num_programs(0) - 1
    ones = head_ones()

    @pl.when(step < half)
    def _():
        tri = triangle(False)
        units, where = [], []
        for ln in lanes(rr):
            row = lambda i: vec[i : i + 1, ln]
            _, logw, a, _, kk, km = prelude(
                kr[:, ln], wl[:, ln], al[:, ln], row(8), row(9), row(10), row(11), ones
            )
            r, v, q = rr[:, ln], vr[:, ln], kk * a
            for c in range(nc):
                s = slice(c * C, (c + 1) * C)
                units.append((r[s], -kk[s], q[s], km[s], v[s], logw[s]))
                where.append((s, ln))
        done = forward_chunks(units, tri)
        packed = []
        for (s, ln), (e, o, m, z, y1, y2, x) in zip(where, done):
            reff[s, ln] = e
            k_reff[step, s, ln], k_oloc[step, s, ln] = e, o
            k_w1[step, s, ln], k_w2[step, s, ln] = y1, y2
            xs[s, ln] = pack2(x)
            mp = pack2(m)
            k_m[step, s, ln], k_n[step, s, ln], mt[s, ln] = mp, pack2(z), pack2(m.T)
            packed.append(mp)
        for i, ln in enumerate(lanes(rr)):
            tm, tn = stack2(packed[i * nc]), done[i * nc][3]
            for c in range(1, nc):
                t = dot3(packed[i * nc + c], jnp.concatenate([tm, tn], 1))
                tm, tn = stack2(t[:, :PW]), stack2(t[:, PW:]) + done[i * nc + c][3]
            move[step, :, ln], add[step, :, ln], turned[:, ln] = pack2(tm), pack2(tn), pack2(tm.T)

    hand_on(n, half, False, move, add, *hand)

    @pl.when(step >= half)
    def _():
        t = step - half
        here = hand[0]
        state = [here[t, :, ln] for ln in lanes(rr)]
        for c in range(nc):
            s = slice(c * C, (c + 1) * C)
            ts = [
                dot3(jnp.concatenate([k_m[t, s, ln], k_reff[t, s, ln], k_w1[t, s, ln]], 0), stack2(z))
                for z, ln in zip(state, lanes(rr))
            ]
            for i, (y, ln) in enumerate(zip(ts, lanes(rr))):
                zs[s, ln] = state[i]
                o_out[s, ln] = y[C : 2 * C] + k_oloc[t, s, ln]
                u_out[s, ln] = y[2 * C :] + k_w2[t, s, ln]
                state[i] = y[:C] + k_n[t, s, ln]
        for ln in lanes(rr):
            row = lambda i: vec[i : i + 1, ln]
            a = jax.nn.sigmoid(row(9) + al[:, ln])
            km = kr[:, ln] * (1.0 + (a - 1.0) * row(11))
            hat, _ = norm_parts(o_out[:, ln], ones)
            y = hat * row(13) + row(14) + headsum(rr[:, ln] * km * row(12), ones) * vr[:, ln]
            z_out[:, ln] = (y * gg[:, ln]).astype(BF)

        @pl.when(step == half)
        def _():
            acc_h[...] = jnp.zeros_like(acc_h)
            middle[...] = tokens[...].astype(F32)

        acc_h[...] += mm_nt(z_out[...], down[...])
        middle[...] += mm_nt(z_out[...], wo[...])

    @pl.when(step == last)
    def _():
        h_out[...] = acc_h[...].astype(BF)
        x1 = middle[...] + SCALE * mm(h_out[...], up[...])
        middle[...] = x1
        centre = x1 - jnp.mean(x1, axis=-1, keepdims=True)
        rstd = lax.rsqrt(jnp.mean(centre * centre, axis=-1, keepdims=True) + NORM_EPS)
        normed[...] = centre * rstd * norm[15:16, :] + norm[16:17, :]


def rec_backward(
    nc, n, half, d_mc, edge, gy, middle, norm, wo, down, up, h_o, gated, gg, o, rr, kr, vr, wl, al, vec,
    reff, mt, turned, xs, us, zs,
    d_mid, dgg, g_down, g_up, drr, dkr, dvr, dwl, dal,
    low, dh, k_dy, k_do, k_es, move, add, *hand,
):
    step = pl.program_id(0)
    ones = head_ones()

    @pl.when(step == 0)
    def _():
        moved = d_mc[...] * norm[17:18, :]
        size = moved.shape[0]
        up_one = pltpu.roll(moved, size - 1, axis=0)
        up_one = jnp.where(iota(moved.shape, 0) == size - 1, edge[0:1, :], up_one)
        dn = d_mc[...] - moved + up_one
        x1 = middle[...]
        centre = x1 - jnp.mean(x1, axis=-1, keepdims=True)
        rstd = lax.rsqrt(jnp.mean(centre * centre, axis=-1, keepdims=True) + NORM_EPS)
        hat = centre * rstd
        dhat = dn * norm[15:16, :]
        d = rstd * (
            dhat
            - jnp.mean(dhat, axis=-1, keepdims=True)
            - hat * jnp.mean(dhat * hat, axis=-1, keepdims=True)
        )
        d = d + gy[...].astype(F32)
        d_mid[...] = d
        low[...] = d.astype(BF)
        dh[...] = (SCALE * mm_nt(low[...], up[...])).astype(BF)
        g_up[...] = SCALE * mm_tn(h_o[...], low[...])

    @pl.when(step < half)
    def _():
        dz = mm(low[...], wo[...]) + mm(dh[...], down[...])
        g_down[...] = mm_tn(dh[...], gated[...])
        _, _, same = grid_ids()
        for ln in lanes(rr):
            row = lambda i: vec[i : i + 1, ln]
            a = jax.nn.sigmoid(row(9) + al[:, ln])
            km = kr[:, ln] * (1.0 + (a - 1.0) * row(11))
            hat, rstd = norm_parts(o[:, ln], ones)
            y = hat * row(13) + row(14) + headsum(rr[:, ln] * km * row(12), ones) * vr[:, ln]
            dgg[:, ln] = (dz[:, ln] * y).astype(BF)
            dy = dz[:, ln] * gg[:, ln]
            k_dy[step, :, ln] = dy
            dhat = dy * row(13)
            k_do[step, :, ln] = rstd * (
                dhat
                - headsum(dhat, ones) * (1.0 / D)
                - hat * (headsum(dhat * hat, ones) * (1.0 / D))
            )
        es = {}
        for c in range(nc):
            s = slice(c * C, (c + 1) * C)
            for ln in lanes(rr):
                e = pack2(jnp.where(same, dot3(reff[s, ln], k_do[step, s, ln], "tn"), 0.0))
                k_es[step, s, ln] = e
                es[c, ln.start] = e
        state = [es[nc - 1, ln.start] for ln in lanes(rr)]
        for c in reversed(range(nc - 1)):
            s = slice(c * C, (c + 1) * C)
            state = [es[c, ln.start] + dot3(mt[s, ln], stack2(h)) for h, ln in zip(state, lanes(rr))]
        for h, ln in zip(state, lanes(rr)):
            add[step, :, ln] = h
            move[step, :, ln] = turned[:, ln]

    hand_on(n, half, True, move, add, *hand)

    @pl.when(step >= half)
    def _():
        t = step - half
        tri, tri_up = triangle(False), triangle(True)
        units, where, pre = [], [], []
        hs = {}
        for ln in lanes(rr):
            h = hand[0][t, :, ln]
            for c in reversed(range(nc)):
                s = slice(c * C, (c + 1) * C)
                hs[c, ln.start] = stack2(h)
                if c:
                    h = dot3(mt[s, ln], hs[c, ln.start]) + k_es[t, s, ln]
        for ln in lanes(rr):
            row = lambda i: vec[i : i + 1, ln]
            for c in range(nc):
                s = slice(c * C, (c + 1) * C)
                r, v, k = rr[s, ln], vr[s, ln], kr[s, ln]
                sg, logw, a, rn, kk, km = prelude(
                    k, wl[s, ln], al[s, ln], row(8), row(9), row(10), row(11), ones
                )
                units.append(
                    (r, -kk, kk * a, km, v, logw, stack2(xs[s, ln]), us[s, ln], stack2(zs[s, ln]),
                     hs[c, ln.start], k_do[t, s, ln])
                )
                where.append((s, ln))
                pre.append((sg, a, rn, kk, km))
        done = backward_chunks(units, tri, tri_up)
        for (s, ln), (sg, a, rn, kk, km), (dr, dp, dq, dk, dv, dlogw) in zip(where, pre, done):
            row = lambda i: vec[i : i + 1, ln]
            r, v, k = rr[s, ln], vr[s, ln], kr[s, ln]
            dy = k_dy[t, s, ln]
            dv = dv + headsum(r * km * row(12), ones) * dy
            ds = headsum(dy * v, ones) * row(12)
            dr = dr + ds * km
            dkm = dk + ds * r
            dkk = dq * a - dp
            da = dq * kk + dkm * k * row(11)
            dk = dkm * (1.0 + (a - 1.0) * row(11)) + row(10) * rn * (dkk - kk * headsum(dkk * kk, ones))
            drr[s, ln], dkr[s, ln], dvr[s, ln] = dr.astype(BF), dk.astype(BF), dv.astype(BF)
            dwl[s, ln] = (dlogw * (-DECAY_SCALE) * sg * (1.0 - sg)).astype(BF)
            dal[s, ln] = (da * a * (1.0 - a)).astype(BF)


TILE = 2 * PW


def cut(shape):
    lead = tuple(shape[:-1])
    return pl.BlockSpec(lead + (TILE,), lambda i, n=len(lead): (0,) * n + (i,))


def whole(shape):
    return pl.BlockSpec(tuple(shape), lambda i, n=len(shape): (0,) * n, pipeline_mode=pl.Buffered(1))


def result(shape):
    return pl.BlockSpec(tuple(shape), lambda i, n=len(shape): (0,) * n)


def in_turn(half, which):
    def spec(shape):
        lead = tuple(shape[:-1])
        place = {
            "first": lambda i: jnp.minimum(i, half - 1),
            "second": lambda i: jnp.maximum(i - half, 0),
            "both": lambda i: lax.rem(i, half),
        }[which]
        return pl.BlockSpec(lead + (TILE,), lambda i: (0,) * len(lead) + (place(i),))

    return spec


def tile_rows(shape):
    return pl.BlockSpec((TILE, shape[1]), lambda i: (i, 0))


def over_tiles(body, steps, ins, outs, name, scratch=(), **params):
    made = lambda spec, shape: spec if isinstance(spec, pl.BlockSpec) else spec(shape)
    return pl.pallas_call(
        body,
        grid=(steps,),
        in_specs=[made(spec, x.shape) for spec, x in ins],
        out_specs=[made(spec, x.shape) for spec, x in outs],
        out_shape=[x for _, x in outs],
        scratch_shapes=list(scratch),
        compiler_params=pltpu.CompilerParams(vmem_limit_bytes=60 * 1024 * 1024, **params),
        name=name,
    )(*[x for _, x in ins])


ORDERS = ("zxy", "zyx", "xzy", "yzx", "zxy", "yzx", "zyx")
DIRS = "xyuds"


def gather_events(order, z, x, y):
    other = {"x": lambda q: (q, 1 - x, y), "y": lambda q: (q, x, 1 - y), "z": lambda q: (q, x, y)}
    inside = lambda k: None if k == 0 else jnp.logical_and(z + k >= 0, z + k <= 3)
    if order[0] == "z":
        a, b = order[1], order[2]
        events = [(0, (z, x, y), None, None, [a, b, "u", "d", "s"])]
        for k in (1, 2, 3):
            events.append((k, (z - k, x, y), "u", z >= k, ["u", a, b, "s"]))
            events.append((k, (z + k, x, y), "d", z + k <= 3, ["d", a, b, "s"]))
        for k in range(-3, 4):
            events.append((abs(k) + 1, other[a](z + k), a, inside(k), [b, "s"]))
    else:
        a, b = order[0], order[2]
        events = [(0, (z, x, y), None, None, [a, "u", "d", b, "s"])]
        events.append((1, other[a](z), a, None, ["u", "d", b, "s"]))
        for k in (1, 2, 3):
            for late, at in ((0, other["z"]), (1, other[a])):
                events.append((k + late, at(z - k), "u", z >= k, ["u", b, "s"]))
                events.append((k + late, at(z + k), "d", z + k <= 3, ["d", b, "s"]))
    for k in range(-3, 4):
        events.append((abs(k) + 1, other[b](z + k), b, inside(k), ["s"]))
        events.append((abs(k) + 2, (z + k, 1 - x, 1 - y), b, inside(k), ["s"]))
    return events


def maybe(condition, run):
    if condition is None:
        run()
    else:
        pl.when(condition)(run)


class Gathering:
    def __init__(self, orders, steps, shards, whole, send, recv, near):
        self.shards, self.whole, self.send, self.recv, self.near = shards, whole, send, recv, near
        seq, dp = lax.axis_index("seq"), lax.axis_index("dp")
        z, x, y, self.c = seq // 2, seq % 2, dp // 2, dp % 2
        self.y, self.z = y, z
        self.to = {
            "x": (z * 2 + 1 - x, dp),
            "y": (seq, (1 - y) * 2 + self.c),
            "u": (seq + 2, dp),
            "d": (seq - 2, dp),
            "s": (seq, y * 2 + 1 - self.c),
        }
        self.exists = {"u": z < 3, "d": z > 0}
        todo = [
            (steps[t][i] if steps else e[0], t, e)
            for t, o in enumerate(orders)
            for i, e in enumerate(gather_events(o, z, x, y))
        ]
        todo.sort(key=lambda q: q[0])
        self.todo = todo
        self.times = sorted({q[0] for q in todo})

    def enter(self, beside=None, count=0):
        barrier = pltpu.get_barrier_semaphore()
        if beside is not None:
            pl.when(count == 1)(
                lambda: pl.semaphore_signal(barrier, inc=1, device_id=beside, device_id_type=MESH)
            )
        for k in DIRS:
            maybe(
                self.exists.get(k),
                lambda k=k: pl.semaphore_signal(
                    barrier, inc=1, device_id=self.to[k], device_id_type=MESH
                ),
            )
        pl.semaphore_wait(barrier, 3 + (self.z + 2) // 3 + (5 - self.z) // 3 + count)

    def chip(self, b):
        return b[0] * 4 + b[1] * 2 + b[2]

    def shard(self, t, k=None):
        ref = self.shards[t]
        if len(ref.shape) == 2:
            return ref
        return ref.at[1 - self.y if k == "y" else self.y]

    def copy(self, t, own, b, k):
        slot = self.whole[t].at[self.chip(b) * 2 + self.c]
        return pltpu.make_async_remote_copy(
            src_ref=self.shard(t, k) if own else slot,
            dst_ref=slot,
            send_sem=self.send.at[DIRS.index(k), t, self.chip(b)],
            recv_sem=self.recv.at[1 if k == "s" else 0, t, self.chip(b)],
            device_id=self.to[k],
            device_id_type=MESH,
        )

    def local(self, t, b):
        return pltpu.make_async_copy(
            self.shard(t), self.whole[t].at[self.chip(b) * 2 + self.c], self.near.at[t]
        )

    def goes(self, event):
        _, b, came, condition, ways = event
        for k in ways:
            both = self.exists.get(k) if condition is None else condition
            if condition is not None and k in self.exists:
                both = jnp.logical_and(condition, self.exists[k])
            yield b, came is None, k, both

    def take(self, time):
        for at, t, event in self.todo:
            if at != time:
                continue
            _, b, came, condition, _ = event
            if came is None:
                self.local(t, b).start()
            else:
                maybe(condition, lambda: self.copy(t, False, b, came).wait_recv())
            for _, own, k, both in self.goes(event):
                maybe(both, lambda: self.copy(t, own, b, k).start())

    def finish(self):
        for t in range(len(self.shards)):
            for i in range(16):
                pltpu.make_async_remote_copy(
                    src_ref=self.shard(t),
                    dst_ref=self.whole[t].at[i * 2 + 1 - self.c],
                    send_sem=self.send.at[4, t, i],
                    recv_sem=self.recv.at[1, t, i],
                    device_id=self.to["s"],
                    device_id_type=MESH,
                ).wait_recv()
        for _, t, event in self.todo:
            for b, own, k, both in self.goes(event):
                maybe(both, lambda: self.copy(t, own, b, k).wait_send())
            if event[2] is None:
                self.local(t, event[1]).wait()


def gather_scratch(n):
    return [
        pltpu.SemaphoreType.DMA((5, n, 16)),
        pltpu.SemaphoreType.DMA((2, n, 16)),
        pltpu.SemaphoreType.DMA((n,)),
    ]


def gather_kernel(orders, *refs):
    n = len(orders)
    g = Gathering(orders, None, refs[:n], refs[n : 2 * n], *refs[2 * n :])
    g.enter()
    for time in g.times:
        g.take(time)
    g.finish()


def own_gather():
    return (lax.axis_size("seq"), lax.axis_size("dp")) == (8, 4)


def gather(shards):
    if not own_gather():
        return [lax.all_gather(s, ("seq", "dp"), axis=0) for s in shards]
    n, devices = len(shards), 32
    made = pl.pallas_call(
        functools.partial(gather_kernel, ORDERS[:n]),
        out_shape=[jax.ShapeDtypeStruct((devices,) + s.shape[-2:], s.dtype) for s in shards],
        in_specs=[pl.BlockSpec(memory_space=pl.ANY)] * n,
        out_specs=[pl.BlockSpec(memory_space=pl.ANY)] * n,
        scratch_shapes=gather_scratch(n),
        compiler_params=pltpu.CompilerParams(collective_id=2, has_side_effects=True),
        name="gather_time",
    )(*shards)
    return list(made)


def sort_kernel(kinds, late, few, small, chosen, hidden, hidden_late, vec):
    half = kinds // 2
    base = (lax.axis_index("dp") % 2) * (half + 4 * RANK)
    rows = lambda o, at, n: few[o, pl.ds(pl.multiple_of(base + at, 16), n), :]
    left = iota((half, PW), 1) < D
    for p in range(few.shape[0] // 2):
        one, two = rows(2 * p, 0, half).astype(F32), rows(2 * p + 1, 0, half).astype(F32)
        at = slice(p * PW, (p + 1) * PW)
        chosen[:half, at] = jnp.where(left, one, pltpu.roll(two, D, axis=1)).astype(BF)
        chosen[half:, at] = jnp.where(left, pltpu.roll(one, D, axis=1), two).astype(BF)
    per = PW // late
    lane = iota((2 * RANK, PW), 1) // late
    for g in range(few.shape[0] // per):
        tail = None
        for j in range(per):
            o = g * per + j
            low, high = rows(o, half, 2 * RANK), rows(o, half + 2 * RANK, 2 * RANK)
            hidden[o, :, :PW], hidden[o, :, PW:] = low, high
            shift = (j + 1) * late % PW
            end = pltpu.roll(high.astype(F32), shift, axis=1) if shift else high.astype(F32)
            tail = end if tail is None else jnp.where(lane == j, end, tail)
        hidden_late[:, g * PW : (g + 1) * PW] = tail.astype(BF)
    vec[...] = small[...].astype(F32).T[D : D + vec.shape[0]]


def sort_small(kinds, late, nvec, few, misc):
    n, width = few.shape[0], misc.shape[0]
    shape = jax.ShapeDtypeStruct
    return over_tiles(
        functools.partial(sort_kernel, kinds, late), 1,
        [(whole, few), (pl.BlockSpec((width, PW), lambda i: (0, 7)), misc)],
        [
            (whole, shape((kinds, width), BF)),
            (whole, shape((n, 2 * RANK, 2 * PW), BF)),
            (whole, shape((2 * RANK, n * late), BF)),
            (whole, shape((nvec, width), F32)),
        ],
        "sort_small",
    )


UNITS = 512
EARLY_UNITS = 16
LATE_ORDERS = ("zxy", "yzx")
LATE_STEPS = (
    (0, 2, 2, 4, 4, 7, 7, 11, 9, 4, 2, 5, 9, 11, 9, 13, 7, 11, 4, 8, 2, 6, 5, 9, 7, 11, 9, 13),
    (0, 3, 3, 3, 5, 5, 6, 6, 8, 8, 9, 9, 11, 11, 13, 14, 13, 14, 7, 11, 3, 6, 8, 12, 13, 14, 13, 14),
)


def channel_kernel(
    late, n2, edge, norm, gy, middle, down_c, up_f, kv, hidden, *refs,
):
    if late:
        kv2, key_shard, value_shard, hidden_late, *refs = refs
    out, dmc, first, g_hidden, g_up_f, g_down_c, *refs = refs
    if late:
        g_late, d_edge, *refs = refs
    mc, mct, gyt, ffo, h_c, dh_f, acc_f, acc_c, *refs = refs
    step, last = pl.program_id(0), pl.num_programs(0) - 1
    per, ff = kv.shape[0], kv.shape[1] // 2
    blocks = [(kv, ff)]
    if late:
        blocks.append((kv2, kv2.shape[1] // 2))
        ff += kv2.shape[1] // 2
        key_late, value_late, mine, came, edge_sem, *sems = refs
        g = Gathering(LATE_ORDERS, LATE_STEPS, (key_shard, value_shard), (key_late, value_late), *sems)
        seq, dp = lax.axis_index("seq"), lax.axis_index("dp")
        x, z = seq % 2, seq // 2
        beside = seq + 2 * x - 1
        count = (1 - x) * ((z + 2) // 3) + x * ((5 - z) // 3)
        starts, ends = seq == 0, seq == 7

        def edges(i, to):
            return pltpu.make_async_remote_copy(
                src_ref=mine.at[i],
                dst_ref=came.at[i],
                send_sem=edge_sem.at[0, i],
                recv_sem=edge_sem.at[1, i],
                device_id=(to, dp),
                device_id_type=MESH,
            )

        def trade(i, has_from, has_to, shift):
            pl.when(has_to)(lambda: edges(i, seq + shift).start())
            pl.when(has_from)(lambda: edges(i, seq - shift).wait_recv())
            pl.when(has_to)(lambda: edges(i, seq + shift).wait_send())

        @pl.when(step == 0)
        def _():
            came[...] = jnp.zeros_like(came)
            g.enter((beside, dp), count)
            size = n2.shape[0]
            mine[0] = n2[size - 8 :, :]

        for time in g.times:

            @pl.when(step == time)
            def _():
                g.take(time)

        @pl.when(step == 0)
        def _():
            trade(0, jnp.logical_not(starts), jnp.logical_not(ends), 1)

    @pl.when(step == 0)
    def _():
        x = n2[...]
        row = came[0, 7:8, :] if late else edge[...]
        before = jnp.where(iota(x.shape, 0) == 0, row, pltpu.roll(x, 1, axis=0))
        m = x + (before - x) * norm[17:18, :]
        mc[...] = m.astype(BF)
        mct[...] = m.T.astype(BF)
        gyt[...] = gy[...].astype(F32).T.astype(BF)
        h_c[...] = mm_nt(down_c[...], mc[...]).astype(BF)
        dh_f[...] = (SCALE * mm_nt(up_f[...], gy[...])).astype(BF)
        acc_f[...] = jnp.zeros_like(acc_f)
        acc_c[...] = jnp.zeros_like(acc_c)
        ffo[...] = jnp.zeros_like(ffo)
        dmc[...] = jnp.zeros_like(dmc)

    def units(key, value, smalls):
        pre, dsq = mm(key, mct[...]), mm(value, gyt[...])
        rows = key.shape[0] // len(smalls)
        hqs, dps, grads = [], [], []
        for b, small in enumerate(smalls):
            s = slice(b * rows, (b + 1) * rows)
            down_f, up_c = small[:RANK], small[RANK:]
            active = jnp.maximum(pre[s] + SCALE * mm_tn(up_c, h_c[...]), 0.0)
            hq = (active * active).astype(BF)
            dpre = ((dsq[s] + mm_tn(down_f, dh_f[...])) * (2.0 * active)).astype(BF)
            grads.append((mm_nt(dh_f[...], hq), SCALE * mm_nt(h_c[...], dpre)))
            acc_f[...] += mm(down_f, hq)
            acc_c[...] += mm(up_c, dpre)
            hqs.append(hq)
            dps.append(dpre)
        ffo[...] += mm_tn(jnp.concatenate(hqs, 0), value)
        dmc[...] += mm_tn(jnp.concatenate(dps, 0), key)
        return grads

    @pl.when(step < last + (0 if late else 1))
    def _():
        key = jnp.concatenate([a[b, :h] for b in range(per) for a, h in blocks], 0)
        value = jnp.concatenate([a[b, h:] for b in range(per) for a, h in blocks], 0)
        grads = units(key, value, [hidden[b, :, :ff] for b in range(per)])
        for b, (low, high) in enumerate(grads):
            if late:
                g_hidden[b] = jnp.zeros(g_hidden.shape[1:], F32)
            g_hidden[b, :RANK, :ff], g_hidden[b, RANK:, :ff] = low, high

    @pl.when(step == last)
    def _():
        if late:
            g.finish()
            flat = lambda ref: ref[...].reshape(-1, ref.shape[-1])
            ((low, high),) = units(flat(key_late), flat(value_late), [hidden_late[...]])
            part = low.shape[1] // 8
            for p in range(8):
                at = slice(p * part, (p + 1) * part)
                g_late[p, :, :part], g_late[p, :, part:] = low[:, at], high[:, at]
        h_f = acc_f[...].astype(BF)
        out[...] = (middle[...] + ffo[...] + SCALE * mm_tn(h_f, up_f[...])).astype(BF)
        g_up_f[...] = SCALE * mm(h_f, gy[...])
        dh_c = (SCALE * acc_c[...]).astype(BF)
        d = dmc[...] + mm_tn(dh_c, down_c[...])
        dmc[...] = d
        first[...] = d[:8] * norm[17:18, :]
        if late:
            mine[1] = first[...]
            trade(1, jnp.logical_not(ends), jnp.logical_not(starts), -1)
            d_edge[...] = came[1]
        g_down_c[...] = mm(dh_c, mc[...])


def late_units(n_seq, n_dp, ff):
    return ff // 8 if (n_seq, n_dp) == (8, 4) and ff % 128 == 0 else 0


def channel(n2, edge, norm, gy, middle, down_c, up_f, kv, hidden, kv2, key_shard, value_shard, hidden_late):
    n, both, width = kv.shape
    ff, length, late = hidden.shape[2], n2.shape[0], key_shard.shape[0]
    per = max(1, min(n, UNITS // ff))
    steps = n // per
    block = lambda shape: pl.BlockSpec(
        (per,) + tuple(shape[1:]), lambda i: (jnp.minimum(i, steps - 1), 0, 0)
    )
    far = lambda shape: pl.BlockSpec(memory_space=pl.ANY)
    shape = jax.ShapeDtypeStruct
    rank = shape((RANK, width), F32)
    ins = [(whole, a) for a in (n2, edge, norm, gy, middle, down_c, up_f)] + [(block, kv), (block, hidden)]
    outs = [
        (result, shape((length, width), BF)),
        (result, shape((length, width), F32)),
        (result, shape((8, width), F32)),
        (block, shape((n, 2 * RANK, ff), F32)),
        (result, rank),
        (result, rank),
    ]
    scratch = [
        pltpu.VMEM((length, width), BF),
        pltpu.VMEM((width, length), BF),
        pltpu.VMEM((width, length), BF),
        pltpu.VMEM((length, width), F32),
        pltpu.VMEM((RANK, length), BF),
        pltpu.VMEM((RANK, length), BF),
        pltpu.VMEM((RANK, length), F32),
        pltpu.VMEM((RANK, length), F32),
    ]
    params = {}
    if late:
        ins += [(block, kv2), (far, key_shard), (far, value_shard), (whole, hidden_late)]
        outs += [(result, shape((8, RANK, 2 * n * late // 8), F32)), (result, shape((8, width), F32))]
        scratch += [pltpu.VMEM((n, late, width), BF)] * 2
        scratch += [pltpu.VMEM((2, 8, width), F32)] * 2 + [pltpu.SemaphoreType.DMA((2, 2))]
        scratch += gather_scratch(2)
        params = dict(collective_id=4, has_side_effects=True)
    return over_tiles(
        functools.partial(channel_kernel, late), steps + (1 if late else 0), ins, outs, "channel", scratch, **params
    )


HALF = 512


def branch_masks(shape):
    lane = iota(shape, 1)
    lo, hi = DECAY_INNER, DECAY_INNER + RATE_INNER
    return lane < lo, (lane >= lo) & (lane < hi), (lane >= hi) & (lane < hi + GATE_INNER)


def project_kernel(
    hat, hat_prev, valid, vec, first, chosen, second, w_r, w_k, w_v, up,
    rr, kr, vr, wl, al, gg, m_r, m_k, m_v, hs, act, act_low,
):
    @pl.when(pl.program_id(0) == 0)
    def _():
        n1 = hat[...] * vec[0:1, :] + vec[1:2, :]
        change = (hat_prev[...] * vec[0:1, :] + vec[1:2, :]) * valid[...] - n1
        mixed = lambda i: (n1 + change * vec[2 + i : 3 + i, :]).astype(BF)
        m_r[...], m_k[...], m_v[...] = mixed(0), mixed(2), mixed(3)
        for i, m in enumerate((m_r, m_k, m_v)):
            hs[i] = mm_nt(m[...], chosen[i * RANK : (i + 1) * RANK, :]).astype(BF)
        t_w = mm(mixed(1), first[...])
        t_a = mm(mixed(4), first[...])
        t_g = mm(mixed(5), first[...])
        is_w, is_a, is_g = branch_masks(t_w.shape)
        zero = jnp.zeros_like(t_w)
        t_w = jnp.where(is_w, jnp.tanh(t_w), zero)
        t_a = jnp.where(is_a, t_a, zero)
        t_g = jnp.where(is_g, jax.nn.sigmoid(t_g), zero)
        act[...] = t_w + t_a + t_g
        act_low[0], act_low[1], act_low[2] = t_w.astype(BF), t_a.astype(BF), t_g.astype(BF)

    for i, (m, w, out) in enumerate(((m_r, w_r, rr), (m_k, w_k, kr), (m_v, w_v, vr))):
        out[...] = mm_nt(m[...], w[...]) + SCALE * mm(hs[i], up[(5 + i) * RANK : (6 + i) * RANK, :])
    for i, out in enumerate((wl, al, gg)):
        out[...] = mm_nt(act_low[i], second[...])


def final_kernel(
    n, fast, drr, dkr, dvr, dwl, dal, dgg, m_r, m_k, m_v, hs, act, chosen, second, down_o, up_o, hat, rstd, d_mid, vecs,
    w_r, w_k, w_v, down, first, vec, *refs,
):
    step, last = pl.program_id(0), pl.num_programs(0) - 1
    me, dp = lax.axis_index("seq"), lax.axis_index("dp")
    if fast:
        early, picks, grad, g_model, g_hidden, *refs = refs
        stage_m, stage_h, from_m, from_h, own_send, own_recv, *refs = refs
    else:
        grad, summed, *refs = refs
    stay, go, dhs, d_act, parts, here, came, send_sem, recv_sem, edge_sem = refs

    def to_owner(k, i):
        peer = lax.rem(dp + k, 4)
        stage, slots = ((stage_m, from_m), (stage_h, from_h))[i]
        return pltpu.make_async_remote_copy(
            src_ref=stage.at[peer],
            dst_ref=slots.at[k - 1],
            send_sem=own_send.at[i, k - 1],
            recv_sem=own_recv.at[i, k - 1],
            device_id=(me, peer),
            device_id_type=MESH,
        )

    def copy(k):
        peer = lax.rem(me + k, n)
        return pltpu.make_async_remote_copy(
            src_ref=parts.at[peer],
            dst_ref=here.at[k - 1],
            send_sem=send_sem.at[k - 1],
            recv_sem=recv_sem.at[k - 1],
            device_id=(peer, dp),
            device_id_type=MESH,
        )

    def edge(to):
        return pltpu.make_async_remote_copy(
            src_ref=go.at[0:8],
            dst_ref=came,
            send_sem=edge_sem.at[0],
            recv_sem=edge_sem.at[1],
            device_id=(to, dp),
            device_id_type=MESH,
        )

    @pl.when(step == 0)
    def _():
        came[...] = jnp.zeros_like(came)
        barrier = pltpu.get_barrier_semaphore()
        for k in range(1, n):
            pl.semaphore_signal(
                barrier, inc=1, device_id=(lax.rem(me + k, n), dp), device_id_type=MESH
            )
        if fast:
            for k in range(1, 4):
                pl.semaphore_signal(
                    barrier, inc=1, device_id=(me, lax.rem(dp + k, 4)), device_id_type=MESH
                )
        rows = [None] * 6 + [down_o[...], up_o[...]]
        for i, (d, m) in enumerate(((drr, m_r), (dkr, m_k), (dvr, m_v))):
            dh = (SCALE * mm_nt(d[...], chosen[(5 + i) * RANK : (6 + i) * RANK, :])).astype(BF)
            dhs[i] = dh
            rows[i], rows[3 + i] = mm_tn(dh, m[...]), SCALE * mm_tn(hs[i], d[...])
        wide = parts.shape[2]
        for i, r in enumerate(rows):
            for p in range(n):
                parts[p, i * RANK : (i + 1) * RANK, :] = r[:, p * wide : (p + 1) * wide].astype(BF)
        pl.semaphore_wait(barrier, n - 1 + (3 if fast else 0))
        for k in range(1, n):
            copy(k).start()
        is_w, is_a, is_g = branch_masks(act.shape)
        a = act[...]
        zero = jnp.zeros_like(a)
        d_act[0] = jnp.where(is_w, mm(dwl[...], second[...]) * (1.0 - a * a), zero).astype(BF)
        d_act[1] = jnp.where(is_a, mm(dal[...], second[...]), zero).astype(BF)
        d_act[2] = jnp.where(is_g, mm(dgg[...], second[...]) * a * (1.0 - a), zero).astype(BF)

    total, moved = None, None
    for i, (d, w, at) in enumerate(((drr, w_r, 2), (dkr, w_k, 4), (dvr, w_v, 5))):
        g = mm(d[...], w[...]) + mm(dhs[i], down[i * RANK : (i + 1) * RANK, :])
        move = g * vec[at : at + 1, :]
        total, moved = (g, move) if total is None else (total + g, moved + move)
    for i, at in enumerate((3, 6, 7)):
        g = mm_nt(d_act[i], first[...])
        total, moved = total + g, moved + g * vec[at : at + 1, :]
    tile = pl.ds(pl.multiple_of(step * TILE, TILE), TILE)
    stay[:, tile] = total - moved
    go[:, tile] = moved

    @pl.when(step == last)
    def _():
        pl.when(me > 0)(lambda: edge(me - 1).start())
        for k in range(1, n):
            copy(k).wait()
        t = parts[me].astype(F32)
        for k in range(1, n):
            t = t + here[k - 1].astype(F32)
        if fast:
            e = early[...]
            r = lambda x, i, k: x[i * RANK : (i + k) * RANK]
            rows = jnp.concatenate(
                [r(t, 0, 3), r(t, 6, 1), r(e, 0, 1), r(t, 3, 3), r(t, 7, 1), r(e, 1, 1)], 0
            )
            tails = e[10 * RANK : 11 * RANK]
            lane = iota((2 * RANK, PW), 1)
            for j in range(4):
                two = rows[:, (j // 2) * PW : (j // 2 + 1) * PW]
                stage_m[j] = pltpu.roll(two, D, axis=1) if j % 2 else two
                mine = e[(2 + 2 * j) * RANK : (4 + 2 * j) * RANK]
                tail = jnp.concatenate([tails[:, :PW], tails[:, PW:]], 0)
                shift = (3 - j) * (PW // 4)
                tail = pltpu.roll(tail, shift, axis=1) if shift else tail
                stage_h[j, :, :PW] = mine[:, :PW]
                stage_h[j, :, PW:] = jnp.where(lane >= 3 * PW // 4, tail, mine[:, PW:])
            for k in range(1, 4):
                to_owner(k, 0).start()
                to_owner(k, 1).start()
        else:
            summed[...] = t
        pl.when(me < n - 1)(lambda: edge(me + 1).wait_recv())
        size = go.shape[0]
        g = pltpu.roll(go[...], size - 1, axis=0)
        g = stay[...] + jnp.where(iota(g.shape, 0) == size - 1, came[0:1, :], g)
        dhat = g * vecs[0:1, :]
        grad[...] = d_mid[...] + rstd[...] * (
            dhat
            - jnp.mean(dhat, axis=-1, keepdims=True)
            - hat[...] * jnp.mean(dhat * hat[...], axis=-1, keepdims=True)
        )
        pl.when(me > 0)(lambda: edge(me - 1).wait_send())
        if fast:
            for k in range(1, 4):
                to_owner(k, 0).wait()
                to_owner(k, 1).wait()
            found = [(dp, stage_m[dp], stage_h[dp])]
            found += [(lax.rem(dp + 4 - k, 4), from_m[k - 1], from_h[k - 1]) for k in range(1, 4)]
            adapters = g_model.shape[0]
            weights = [picks[pl.ds(pl.multiple_of(q * adapters, 8), adapters), :] for q, _, _ in found]
            for a in range(adapters):
                m, h = None, None
                for w, (_, x, y) in zip(weights, found):
                    w = w[a : a + 1, :]
                    x, y = x * w, y * jnp.concatenate([w, w], 1)
                    m, h = (x, y) if m is None else (m + x, h + y)
                g_model[a], g_hidden[a] = m[:, :D], h


def shifted(block, axis, distance):
    devices = range(lax.axis_size(axis))
    route = [(i - distance, i) for i in devices if i - distance in devices]
    return lax.ppermute(block, axis, route)


def mm(a, b):
    return lax.dot_general(a, b, DIMS["nn"], preferred_element_type=F32)


def mm_nt(a, b):
    return lax.dot_general(a, b, DIMS["nt"], preferred_element_type=F32)


def mm_tn(a, b):
    return lax.dot_general(a, b, DIMS["tn"], preferred_element_type=F32)


def body(tokens, output_gradient, index, proj, first, second, vectors, ckey, cvalue, model_rows, hidden_rows):
    axes = ("seq", "dp")
    n_seq, n_dp = lax.axis_size("seq"), lax.axis_size("dp")
    n = n_seq * n_dp
    tokens, gy = tokens[0], output_gradient[0]
    length, width = tokens.shape
    nc, tiles = length // C, width // TILE
    adapters, kinds, cols = model_rows.shape
    ff, inner, nvec = ckey.shape[1], first.shape[1], vectors.shape[0]

    key_shard, soon = ckey.T, ff - late_units(n_seq, n_dp, ff)
    most = soon - EARLY_UNITS if soon < ff else soon
    kv = lax.all_gather(jnp.concatenate([key_shard[:most], cvalue[:most]], 0), axes, axis=0)

    index_all = lax.all_gather(index, "dp", axis=0, tiled=True)
    pick = index_all[:, None] == jnp.arange(adapters, dtype=jnp.int32)[None, :]
    pick_low = pick.astype(BF)
    fast = own_gather() and (cols, ff, 2 * inner + nvec) == (D, 2 * PW, 914)
    if fast:
        half = kinds // 2
        few = jnp.concatenate(
            [
                jnp.concatenate([model_rows[:, :half], model_rows[:, half:]], 2),
                hidden_rows[:, :, :PW],
                hidden_rows[:, :, PW:],
            ],
            1,
        )
    else:
        few = jnp.concatenate([model_rows.reshape(adapters, -1), hidden_rows.reshape(adapters, -1)], 1)
        few = few.reshape(adapters, -1, 128)
    few = jnp.einsum("sa,arx->srx", pick_low, few, preferred_element_type=F32).astype(BF)
    pad = lambda k: jnp.zeros((cols, k), BF)
    misc = jnp.concatenate(
        [first, pad(HALF - inner), second.T, vectors.T, pad(HALF - inner - nvec)], axis=1
    )
    turned = jnp.swapaxes(proj, 1, 2)

    few = few.reshape((2, -1, 128) if fast else (-1, 128))
    more = [jnp.concatenate([key_shard[most:soon], cvalue[most:soon]], 0)] if most < soon else []
    *mats, misc, few_all, kv2 = gather([turned[0], turned[1], turned[2], turned[3], misc, few] + more) + [None] * (
        most == soon
    )
    mats[0], tokens = lax.optimization_barrier((mats[0], tokens))
    wide = tokens.astype(F32)
    ahead = shifted(tokens[-1:], "seq", 1).astype(F32)
    rows = jnp.concatenate([ahead, wide], 0)
    centre = rows - jnp.mean(rows, axis=-1, keepdims=True)
    rstd = lax.rsqrt(jnp.mean(centre * centre, axis=-1, keepdims=True) + NORM_EPS)
    hat = centre * rstd
    start = (jnp.arange(length)[:, None] == 0) & (lax.axis_index("seq") == 0)
    valid = jnp.where(start, 0.0, 1.0).astype(F32)
    hat_prev, hat, rstd = hat[:-1], hat[1:], rstd[1:]

    mats = [m.reshape(width, width) for m in mats]
    misc = misc.reshape(width, -1)
    if fast:
        chosen, hidden, hidden_late, vec = sort_small(kinds, ff - soon, nvec, few_all, misc)
    else:
        vec = misc[:, HALF + inner : HALF + inner + nvec].T.astype(F32)
        own = lax.dynamic_index_in_dim(few_all.reshape(n, n_dp, -1, 128), lax.axis_index("dp"), 1, False)
        own = own.reshape(n, -1)
        chosen = own[:, : kinds * cols].reshape(n, kinds, cols).transpose(1, 0, 2).reshape(kinds, width)
        hidden, hidden_late = own[:, kinds * cols :].reshape(n, 2 * RANK, ff), None
    down = lambda i: chosen[i * RANK : (i + 1) * RANK]
    up = lambda i: chosen[(5 + i) * RANK : (6 + i) * RANK]

    shape = jax.ShapeDtypeStruct
    full, low = shape((length, width), F32), shape((length, width), BF)
    small, rank = shape((D, width), F32), shape((RANK, width), F32)
    firsts = pl.BlockSpec((width, HALF), lambda i: (0, 0))
    seconds = pl.BlockSpec((width, HALF), lambda i: (0, 1))
    first_rows = pl.BlockSpec((TILE, HALF), lambda i: (i, 0))
    second_rows = pl.BlockSpec((TILE, HALF), lambda i: (i, 1))
    rr, kr, vr, wl, al, gg, m_r, m_k, m_v, hs, act = over_tiles(
        project_kernel, tiles,
        [
            (whole, hat), (whole, hat_prev), (whole, valid), (whole, vec), (firsts, misc), (whole, chosen),
            (second_rows, misc), (tile_rows, mats[0]), (tile_rows, mats[1]), (tile_rows, mats[2]), (cut, chosen),
        ],
        [(cut, full)] * 6
        + [(result, low)] * 3
        + [(result, shape((3, length, RANK), BF)), (result, shape((length, HALF), F32))],
        "project",
        [pltpu.VMEM((3, length, HALF), BF)],
    )
    one, two, each = in_turn(tiles, "first"), in_turn(tiles, "second"), in_turn(tiles, "both")
    keep = pltpu.VMEM((tiles, length, TILE), F32)
    keep_small = pltpu.VMEM((tiles, D, TILE), F32)
    reff, xs, mt, turned, gated, o, us, zs, middle, n2, h_o = over_tiles(
        functools.partial(rec_forward, nc, n_seq, tiles), 2 * tiles,
        [
            (each, rr), (each, kr), (each, vr), (one, wl), (each, al), (two, gg), (each, vec),
            (whole, tokens), (two, mats[3]), (two, down(3)), (whole, up(3)), (whole, vec),
        ],
        [(one, full), (one, full), (one, full), (one, small), (two, low), (two, full), (two, full), (two, full)]
        + [(result, full), (result, full), (result, shape((length, RANK), BF))],
        "rec_forward",
        [keep] * 6 + [keep_small] * 2 + [pltpu.VMEM((length, RANK), F32)] + hand_scratch(tiles),
        collective_id=0, has_side_effects=True,
    )
    soon_only = soon == ff
    row = shifted(n2[-1:], "seq", 1) if soon_only else n2[-1:]
    out, d_mc, moved, g_hidden, up_f, down_c, *more = channel(
        n2, row, vec, gy, middle, down(4), up(4), kv, hidden,
        kv2, key_shard[soon:], cvalue[soon:], hidden_late,
    )
    wide = n_dp * cols
    by_piece = lambda rows: jnp.swapaxes(rows.reshape(-1, n_seq, wide), 0, 1)
    parts = [by_piece(jnp.concatenate([down_c, up_f], 0)), g_hidden.reshape(n_seq, -1, wide)]
    if soon_only:
        edge = jnp.broadcast_to(shifted(moved[:1], "seq", -1), (8, width))
    else:
        g_late, edge = more
        parts.append(g_late)
    early, edge = lax.optimization_barrier((jnp.concatenate(parts, 1), edge))
    early = lax.psum_scatter(early, "seq", scatter_dimension=0, tiled=True)[0]
    d_mid, dgg, down_o, up_o, drr, dkr, dvr, dwl, dal = over_tiles(
        functools.partial(rec_backward, nc, n_seq, tiles), 2 * tiles,
        [
            (whole, d_mc), (whole, edge), (whole, gy), (whole, middle), (whole, vec), (one, mats[3]),
            (one, down(3)), (whole, up(3)), (whole, h_o), (one, gated), (one, gg), (one, o),
            (each, rr), (each, kr), (each, vr), (two, wl), (each, al), (each, vec),
            (one, reff), (each, mt), (one, turned), (two, xs), (two, us), (two, zs),
        ],
        [(result, full), (one, low), (one, rank), (result, rank)] + [(two, low)] * 5,
        "rec_backward",
        [pltpu.VMEM((length, width), BF), pltpu.VMEM((length, RANK), BF)]
        + [keep] * 3 + [keep_small] * 2 + hand_scratch(tiles),
        collective_id=1, has_side_effects=True,
    )
    early, drr = lax.optimization_barrier((early, drr))
    ins = [(whole, a) for a in (drr, dkr, dvr, dwl, dal, dgg, m_r, m_k, m_v, hs, act, chosen)]
    ins += [(pl.BlockSpec((width, HALF), lambda i: (0, 1), pipeline_mode=pl.Buffered(1)), misc)]
    ins += [(whole, a) for a in (down_o, up_o, hat, rstd, d_mid, vec)]
    ins += [(cut, mats[0]), (cut, mats[1]), (cut, mats[2]), (cut, chosen), (first_rows, misc), (cut, vec)]
    scratch = [
        pltpu.VMEM((length, width), F32),
        pltpu.VMEM((length, width), F32),
        pltpu.VMEM((3, length, RANK), BF),
        pltpu.VMEM((3, length, HALF), BF),
        pltpu.VMEM((n_seq, 8 * RANK, wide), BF),
        pltpu.VMEM((n_seq - 1, 8 * RANK, wide), BF),
        pltpu.VMEM((8, width), F32),
        pltpu.SemaphoreType.DMA((n_seq - 1,)),
        pltpu.SemaphoreType.DMA((n_seq - 1,)),
        pltpu.SemaphoreType.DMA((2,)),
    ]
    ready = fast and adapters == 8 and not soon_only
    call = lambda ins, outs, scratch: over_tiles(
        functools.partial(final_kernel, n_seq, ready), tiles, ins, [(result, full)] + outs, "final", scratch,
        collective_id=3, has_side_effects=True,
    )
    if ready:
        picks = jnp.broadcast_to(pick.astype(F32).reshape(-1, 1), (n_dp * adapters, PW))
        grad_tokens, grad_model, h = call(
            ins + [(whole, early), (whole, picks)],
            [(result, shape((adapters, kinds, cols), F32)), (result, shape((adapters, 2 * RANK, ff), F32))],
            [pltpu.VMEM((4, kinds, PW), F32), pltpu.VMEM((4, 2 * RANK, ff), F32)]
            + [pltpu.VMEM((3, kinds, PW), F32), pltpu.VMEM((3, 2 * RANK, ff), F32)]
            + [pltpu.SemaphoreType.DMA((2, 3))] * 2
            + scratch,
        )
        return out[None], grad_tokens[None], grad_model, h
    grad_tokens, late = call(ins, [(result, shape((8 * RANK, wide), F32))], scratch)
    mine = early[2 * RANK : 2 * RANK + 2 * RANK * ff // cols].reshape(n_dp, 2 * RANK, ff)
    if not soon_only:
        tail = early[2 * RANK + 2 * RANK * ff // cols :].reshape(RANK, 2, n_dp, ff - soon)
        tail = tail.transpose(2, 1, 0, 3).reshape(n_dp, 2 * RANK, ff - soon)
        mine = jnp.concatenate([mine[:, :, :soon], tail], 2)
    columns = jnp.concatenate([early[: 2 * RANK], late], 0).reshape(10 * RANK, n_dp, cols)
    both = jnp.concatenate(
        [jnp.swapaxes(columns, 0, 1).reshape(n_dp, -1), mine.reshape(n_dp, -1)], 1
    )
    both = lax.all_to_all(both, "dp", split_axis=0, concat_axis=0, tiled=True)
    both = jnp.einsum("sa,sx->ax", pick.astype(F32), both, precision=PRECISE)
    at = 10 * RANK * cols
    a = both[:, :at].reshape(adapters, 10 * RANK, cols)
    h = both[:, at:].reshape(adapters, 2 * RANK, ff)
    block = lambda i, k: a[:, i * RANK : (i + k) * RANK]
    grad_model = jnp.concatenate(
        [block(2, 3), block(8, 1), block(0, 1), block(5, 3), block(9, 1), block(1, 1)], axis=1
    )
    return out[None], grad_tokens[None], grad_model, h


def solution(mesh):
    cols = P(None, ("seq", "dp"))
    rows = P(("seq", "dp"), None)
    deep = P(None, None, ("seq", "dp"))
    act = P("dp", "seq", None)
    return jax.shard_map(
        body,
        mesh=mesh,
        in_specs=(act, act, P("dp"), deep, rows, cols, cols, cols, rows, deep, deep),
        out_specs=(act, act, deep, deep),
        check_vma=False,
    )
```

```python
import functools
import math

import jax
import jax.numpy as jnp
from jax import lax
from jax.experimental import pallas as pl
from jax.experimental.pallas import tpu as pltpu
from jax.sharding import PartitionSpec as P

F32, BF = jnp.float32, jnp.bfloat16
MESH = pl.DeviceIdType.MESH
D = 64
C = 64
PW = 2 * D
DECAY_INNER, RATE_INNER, GATE_INNER, RANK = 96, 96, 256, 16
SCALE = 4.0
NORM_EPS, GROUP_EPS, UNIT_EPS = 1e-05, 0.00064, 1e-06
DECAY_SCALE = math.exp(-0.5)
PRECISE = lax.Precision.HIGHEST
DIMS = {
    "nn": (((1,), (0,)), ((), ())),
    "nt": (((1,), (1,)), ((), ())),
    "tn": (((0,), (0,)), ((), ())),
}


def split(x):
    hi = x.astype(BF)
    return hi, (x - hi.astype(F32)).astype(BF)


def dot1(a, b, m="nn"):
    return lax.dot_general(a.astype(BF), b.astype(BF), DIMS[m], preferred_element_type=F32)


def dot3(a, b, m="nn"):
    ah, al = split(a)
    bh, bl = split(b)
    ka, kb = (0 if m == "tn" else 1), (1 if m == "nt" else 0)
    n = b.shape[1 - kb]
    aa = jnp.concatenate([ah, al], axis=ka)
    bb = jnp.concatenate([jnp.concatenate([bh, bl], axis=1 - kb)] * 2, axis=kb)
    r = lax.dot_general(aa, bb, DIMS[m], preferred_element_type=F32)
    return r[:, :n] + r[:, n:]


dot_inv = dot_a = dot3
dot_w = dot_b = dot_g = dot1


def iota(shape, axis):
    return lax.broadcasted_iota(jnp.int32, shape, axis)


def stack2(x):
    lane = iota(x.shape, 1)
    zero = jnp.zeros_like(x)
    return jnp.concatenate([jnp.where(lane < D, x, zero), jnp.where(lane < D, zero, x)], axis=0)


def pack2(x):
    h = x.shape[0] // 2
    return x[:h] + x[h:]


def head_ones():
    r, c = iota((2 * PW, PW), 0) % PW, iota((2 * PW, PW), 1)
    return jnp.where((r // D) == (c // D), 1.0, 0.0).astype(BF)


def headsum(x, ones):
    h, l = split(x)
    return lax.dot_general(
        jnp.concatenate([h, l], axis=1), ones, DIMS["nn"], preferred_element_type=F32
    )


def triangle(upper):
    r, c = iota((C, C), 0), iota((C, C), 1)
    return jnp.where((r <= c) if upper else (r >= c), 1.0, 0.0).astype(BF)


def cums(x, tri):
    h, l = split(x)
    m = (x - h.astype(F32) - l.astype(F32)).astype(BF)
    n = x.shape[1]
    r = lax.dot_general(
        tri, jnp.concatenate([h, l, m], axis=1), DIMS["nn"], preferred_element_type=F32
    )
    return r[:, :n] + r[:, n : 2 * n] + r[:, 2 * n :]


def prelude(kr, wl, al, w0, a0, k_k, k_a, ones):
    s = jax.nn.sigmoid(w0 + wl)
    a = jax.nn.sigmoid(a0 + al)
    kx = kr * k_k
    rn = lax.rsqrt(headsum(kx * kx, ones) + UNIT_EPS)
    return s, -DECAY_SCALE * s, a, rn, kx * rn, kr * (1.0 + (a - 1.0) * k_a)


def grid_ids():
    r, c = iota((PW, PW), 0), iota((PW, PW), 1)
    return r, c, (r // D) == (c // D)


def inverses(many):
    r, c, _ = grid_ids()
    eye = jnp.where(r == c, 1.0, 0.0)
    b = 1
    while b < C:
        level = ((r // (2 * b)) == (c // (2 * b))) & ((r // b) % 2 == 1) & ((c // b) % 2 == 0)
        parts = [jnp.where(level, a, 0.0) for a in many]
        if b == 1:
            xs = [eye + p for p in parts]
        else:
            half = [dot_inv(x, p) for x, p in zip(xs, parts)]
            xs = [x + dot_inv(h, x) for h, x in zip(half, xs)]
        b *= 2
    return xs


def factors(logw, tri):
    run = cums(logw, tri)
    return jnp.exp(run - logw), jnp.exp(run), jnp.exp(-run), jnp.exp(run[C - 1 : C])


def forward_chunks(units, tri):
    rows, cols, same = grid_ids()
    zero = jnp.zeros((PW, PW), F32)
    strict, incl = (rows > cols) & same, (rows >= cols) & same
    fs = [factors(u[5], tri) for u in units]
    p2 = [stack2(u[1] * f[0]) for u, f in zip(units, fs)]
    r2 = [stack2(u[0] * f[1]) for u, f in zip(units, fs)]
    q2 = [stack2(u[2] * f[2]) for u, f in zip(units, fs)]
    k2 = [stack2(u[3] * f[2]) for u, f in zip(units, fs)]
    v2 = [stack2(u[4]) for u in units]
    aa = [
        dot_a(jnp.concatenate([p, r], 0), jnp.concatenate([q, k], 0), "nt")
        for p, r, q, k in zip(p2, r2, q2, k2)
    ]
    apk = [jnp.where(strict, a[:PW, PW:], zero) for a in aa]
    y = [dot_w(a, v) for a, v in zip(apk, v2)]
    xs = inverses([jnp.where(strict, a[:PW, :PW], zero) for a in aa])
    ww = [dot_w(x, jnp.concatenate([p, t], 1)) for x, p, t in zip(xs, p2, y)]
    left = [
        jnp.concatenate(
            [
                jnp.concatenate(
                    [jnp.where(incl, a[PW:, :PW], zero), jnp.where(incl, a[PW:, PW:], zero)], 1
                ),
                jnp.concatenate([(q * f[3]).T, (k * f[3]).T], 1),
            ],
            0,
        )
        for a, q, k, f in zip(aa, q2, k2, fs)
    ]
    right = [
        jnp.concatenate([w, jnp.concatenate([zero, v], 1)], 0) for w, v in zip(ww, v2)
    ]
    big = [dot_b(l, r) for l, r in zip(left, right)]
    move = [
        b[PW:, :PW] + jnp.where(rows == cols, jnp.broadcast_to(f[3], (PW, PW)), zero)
        for b, f in zip(big, fs)
    ]
    return [
        (pack2(r + b[:PW, :PW]), pack2(b[:PW, PW:]), m, b[PW:, PW:], pack2(w[:, :PW]), pack2(w[:, PW:]), x)
        for r, b, m, w, x in zip(r2, big, move, ww, xs)
    ]


def backward_chunks(units, tri, tri_up):
    rows, cols, same = grid_ids()
    zero = jnp.zeros((PW, PW), F32)
    strict, incl = (rows < cols) & same, (rows <= cols) & same
    both = jnp.concatenate([jnp.concatenate([strict, incl], 1)] * 2, 0)
    fs = [factors(t[5], tri) for t in units]
    pe = [t[1] * f[0] for t, f in zip(units, fs)]
    re = [t[0] * f[1] for t, f in zip(units, fs)]
    qe = [t[2] * f[2] for t, f in zip(units, fs)]
    ke = [t[3] * f[2] for t, f in zip(units, fs)]
    g2 = [stack2(t[10]) for t in units]
    qk = [jnp.concatenate([stack2(q), stack2(k)], 0) for q, k in zip(qe, ke)]
    pr = [jnp.concatenate([stack2(p), stack2(r)], 0) for p, r in zip(pe, re)]
    at = [dot_a(a, b, "nt") for a, b in zip(qk, pr)]
    qkh = [
        dot_g(jnp.concatenate([q * f[3], k * f[3]], 0), t[9])
        for q, k, f, t in zip(qe, ke, fs, units)
    ]
    sq = [dot_g(jnp.concatenate([t[7], t[4]], 0), t[9], "nt") for t in units]
    du = [
        dot_g(jnp.where(incl, a[:PW, PW:], zero), g) + stack2(h[:C])
        for a, g, h in zip(at, g2, qkh)
    ]
    dm = [dot_g(t[6], d, "tn") for t, d in zip(units, du)]
    dg = [jnp.concatenate([d, g], 0) for d, g in zip(dm, g2)]
    dv = [
        pack2(
            dot_g(
                jnp.concatenate(
                    [jnp.where(strict, a[PW:, :PW], zero), jnp.where(incl, a[PW:, PW:], zero)], 1
                ),
                d,
            )
        )
        + h[C:]
        for a, d, h in zip(at, dg, qkh)
    ]
    dat = [
        dot_g(jnp.concatenate([stack2(t[7]), stack2(t[4])], 0), d, "nt")
        for t, d in zip(units, dg)
    ]
    dat = [jnp.where(both, d, jnp.zeros_like(d)) for d in dat]
    dpr = [dot_g(d, a, "tn") for d, a in zip(dat, qk)]
    dqk = [dot_g(d, a) for d, a in zip(dat, pr)]
    sp = [dot_g(jnp.concatenate([pack2(d), t[10]], 0), t[8], "nt") for d, t in zip(dm, units)]
    outs = []
    for i, t in enumerate(units):
        eb, el, en, last = fs[i]
        dp, dr = pack2(dpr[i][:PW]) + sp[i][:C], pack2(dpr[i][PW:]) + sp[i][C:]
        dqh, dkh = sq[i][:C], sq[i][C:]
        dq, dk = pack2(dqk[i][:PW]) + dqh * last, pack2(dqk[i][PW:]) + dkh * last
        tail = jnp.sum((qe[i] * dqh + ke[i] * dkh) * last, axis=0, keepdims=True)
        tail = tail + last * jnp.sum((t[8] * t[9]).T, axis=0, keepdims=True)
        gb = pe[i] * dp
        gl = re[i] * dr - qe[i] * dq - ke[i] * dk
        dlogw = cums(gl + gb, tri_up) - gb + tail
        outs.append((dr * el, dp * eb, dq * en, dk * en, dv[i], dlogw))
    return outs


def lanes(ref):
    return [slice(i * PW, (i + 1) * PW) for i in range(ref.shape[-1] // PW)]


def norm_parts(o, ones):
    centre = o - headsum(o, ones) * (1.0 / D)
    rstd = lax.rsqrt(headsum(centre * centre, ones) * (1.0 / D) + GROUP_EPS)
    return centre * rstd, rstd


def hand_on(n, half, back, move, add, here, send, send_sem, recv_sem):
    step, last = pl.program_id(0), pl.num_programs(0) - 1
    s, d = lax.axis_index("seq"), lax.axis_index("dp")
    at = n - 1 - s if back else s
    first, final = at == 0, at == n - 1
    nxt, prv = (s - 1, s + 1) if back else (s + 1, s - 1)
    begins, goes = jnp.logical_not(first), jnp.logical_not(final)
    tile = step - jnp.minimum(at, half)
    now = jnp.logical_and(tile >= 0, tile < half)

    def copy(i, to):
        return pltpu.make_async_remote_copy(
            src_ref=send.at[i],
            dst_ref=here.at[i],
            send_sem=send_sem.at[i],
            recv_sem=recv_sem.at[i],
            device_id=(to, d),
            device_id_type=MESH,
        )

    @pl.when(jnp.logical_and(step == 0, begins))
    def _():
        pl.semaphore_signal(
            pltpu.get_barrier_semaphore(), inc=1, device_id=(prv, d), device_id_type=MESH
        )

    @pl.when(jnp.logical_and(step == 0, goes))
    def _():
        pl.semaphore_wait(pltpu.get_barrier_semaphore(), 1)

    @pl.when(jnp.logical_and(now, first))
    def _():
        here[tile] = jnp.zeros(here.shape[1:], F32)

    @pl.when(jnp.logical_and(now, begins))
    def _():
        copy(tile, prv).wait_recv()

    @pl.when(jnp.logical_and(now, goes))
    def _():
        for ln in lanes(here):
            send[tile, :, ln] = dot3(move[tile, :, ln], stack2(here[tile, :, ln])) + add[tile, :, ln]
        copy(tile, nxt).start()

    @pl.when(jnp.logical_and(step == last, goes))
    def _():
        for i in range(half):
            copy(i, nxt).wait_send()


def hand_scratch(steps):
    return [
        pltpu.VMEM((steps, D, TILE), F32),
        pltpu.VMEM((steps, D, TILE), F32),
        pltpu.SemaphoreType.DMA((steps,)),
        pltpu.SemaphoreType.DMA((steps,)),
    ]


def rec_forward(
    nc, n, half, rr, kr, vr, wl, al, gg, vec, tokens, wo, down, up, norm,
    reff, xs, mt, turned, z_out, o_out, u_out, zs, middle, normed, h_out,
    k_reff, k_oloc, k_w1, k_w2, k_m, k_n, move, add, acc_h, *hand,
):
    step, last = pl.program_id(0), pl.num_programs(0) - 1
    ones = head_ones()

    @pl.when(step < half)
    def _():
        tri = triangle(False)
        units, where = [], []
        for ln in lanes(rr):
            row = lambda i: vec[i : i + 1, ln]
            _, logw, a, _, kk, km = prelude(
                kr[:, ln], wl[:, ln], al[:, ln], row(8), row(9), row(10), row(11), ones
            )
            r, v, q = rr[:, ln], vr[:, ln], kk * a
            for c in range(nc):
                s = slice(c * C, (c + 1) * C)
                units.append((r[s], -kk[s], q[s], km[s], v[s], logw[s]))
                where.append((s, ln))
        done = forward_chunks(units, tri)
        packed = []
        for (s, ln), (e, o, m, z, y1, y2, x) in zip(where, done):
            reff[s, ln] = e
            k_reff[step, s, ln], k_oloc[step, s, ln] = e, o
            k_w1[step, s, ln], k_w2[step, s, ln] = y1, y2
            xs[s, ln] = pack2(x)
            mp = pack2(m)
            k_m[step, s, ln], k_n[step, s, ln], mt[s, ln] = mp, pack2(z), pack2(m.T)
            packed.append(mp)
        for i, ln in enumerate(lanes(rr)):
            tm, tn = stack2(packed[i * nc]), done[i * nc][3]
            for c in range(1, nc):
                t = dot3(packed[i * nc + c], jnp.concatenate([tm, tn], 1))
                tm, tn = stack2(t[:, :PW]), stack2(t[:, PW:]) + done[i * nc + c][3]
            move[step, :, ln], add[step, :, ln], turned[:, ln] = pack2(tm), pack2(tn), pack2(tm.T)

    hand_on(n, half, False, move, add, *hand)

    @pl.when(step >= half)
    def _():
        t = step - half
        here = hand[0]
        state = [here[t, :, ln] for ln in lanes(rr)]
        for c in range(nc):
            s = slice(c * C, (c + 1) * C)
            ts = [
                dot3(jnp.concatenate([k_m[t, s, ln], k_reff[t, s, ln], k_w1[t, s, ln]], 0), stack2(z))
                for z, ln in zip(state, lanes(rr))
            ]
            for i, (y, ln) in enumerate(zip(ts, lanes(rr))):
                zs[s, ln] = state[i]
                o_out[s, ln] = y[C : 2 * C] + k_oloc[t, s, ln]
                u_out[s, ln] = y[2 * C :] + k_w2[t, s, ln]
                state[i] = y[:C] + k_n[t, s, ln]
        for ln in lanes(rr):
            row = lambda i: vec[i : i + 1, ln]
            a = jax.nn.sigmoid(row(9) + al[:, ln])
            km = kr[:, ln] * (1.0 + (a - 1.0) * row(11))
            hat, _ = norm_parts(o_out[:, ln], ones)
            y = hat * row(13) + row(14) + headsum(rr[:, ln] * km * row(12), ones) * vr[:, ln]
            z_out[:, ln] = (y * gg[:, ln]).astype(BF)

        @pl.when(step == half)
        def _():
            acc_h[...] = jnp.zeros_like(acc_h)
            middle[...] = tokens[...].astype(F32)

        acc_h[...] += mm_nt(z_out[...], down[...])
        middle[...] += mm_nt(z_out[...], wo[...])

    @pl.when(step == last)
    def _():
        h_out[...] = acc_h[...].astype(BF)
        x1 = middle[...] + SCALE * mm(h_out[...], up[...])
        middle[...] = x1
        centre = x1 - jnp.mean(x1, axis=-1, keepdims=True)
        rstd = lax.rsqrt(jnp.mean(centre * centre, axis=-1, keepdims=True) + NORM_EPS)
        normed[...] = centre * rstd * norm[15:16, :] + norm[16:17, :]


def rec_backward(
    nc, n, half, d_mc, edge, gy, middle, norm, wo, down, up, h_o, gated, gg, o, rr, kr, vr, wl, al, vec,
    reff, mt, turned, xs, us, zs,
    d_mid, dgg, g_down, g_up, drr, dkr, dvr, dwl, dal,
    low, dh, k_dy, k_do, k_es, move, add, *hand,
):
    step = pl.program_id(0)
    ones = head_ones()

    @pl.when(step == 0)
    def _():
        moved = d_mc[...] * norm[17:18, :]
        size = moved.shape[0]
        up_one = pltpu.roll(moved, size - 1, axis=0)
        up_one = jnp.where(iota(moved.shape, 0) == size - 1, edge[0:1, :], up_one)
        dn = d_mc[...] - moved + up_one
        x1 = middle[...]
        centre = x1 - jnp.mean(x1, axis=-1, keepdims=True)
        rstd = lax.rsqrt(jnp.mean(centre * centre, axis=-1, keepdims=True) + NORM_EPS)
        hat = centre * rstd
        dhat = dn * norm[15:16, :]
        d = rstd * (
            dhat
            - jnp.mean(dhat, axis=-1, keepdims=True)
            - hat * jnp.mean(dhat * hat, axis=-1, keepdims=True)
        )
        d = d + gy[...].astype(F32)
        d_mid[...] = d
        low[...] = d.astype(BF)
        dh[...] = (SCALE * mm_nt(low[...], up[...])).astype(BF)
        g_up[...] = SCALE * mm_tn(h_o[...], low[...])

    @pl.when(step < half)
    def _():
        dz = mm(low[...], wo[...]) + mm(dh[...], down[...])
        g_down[...] = mm_tn(dh[...], gated[...])
        _, _, same = grid_ids()
        for ln in lanes(rr):
            row = lambda i: vec[i : i + 1, ln]
            a = jax.nn.sigmoid(row(9) + al[:, ln])
            km = kr[:, ln] * (1.0 + (a - 1.0) * row(11))
            hat, rstd = norm_parts(o[:, ln], ones)
            y = hat * row(13) + row(14) + headsum(rr[:, ln] * km * row(12), ones) * vr[:, ln]
            dgg[:, ln] = (dz[:, ln] * y).astype(BF)
            dy = dz[:, ln] * gg[:, ln]
            k_dy[step, :, ln] = dy
            dhat = dy * row(13)
            k_do[step, :, ln] = rstd * (
                dhat
                - headsum(dhat, ones) * (1.0 / D)
                - hat * (headsum(dhat * hat, ones) * (1.0 / D))
            )
        es = {}
        for c in range(nc):
            s = slice(c * C, (c + 1) * C)
            for ln in lanes(rr):
                e = pack2(jnp.where(same, dot3(reff[s, ln], k_do[step, s, ln], "tn"), 0.0))
                k_es[step, s, ln] = e
                es[c, ln.start] = e
        state = [es[nc - 1, ln.start] for ln in lanes(rr)]
        for c in reversed(range(nc - 1)):
            s = slice(c * C, (c + 1) * C)
            state = [es[c, ln.start] + dot3(mt[s, ln], stack2(h)) for h, ln in zip(state, lanes(rr))]
        for h, ln in zip(state, lanes(rr)):
            add[step, :, ln] = h
            move[step, :, ln] = turned[:, ln]

    hand_on(n, half, True, move, add, *hand)

    @pl.when(step >= half)
    def _():
        t = step - half
        tri, tri_up = triangle(False), triangle(True)
        units, where, pre = [], [], []
        hs = {}
        for ln in lanes(rr):
            h = hand[0][t, :, ln]
            for c in reversed(range(nc)):
                s = slice(c * C, (c + 1) * C)
                hs[c, ln.start] = stack2(h)
                if c:
                    h = dot3(mt[s, ln], hs[c, ln.start]) + k_es[t, s, ln]
        for ln in lanes(rr):
            row = lambda i: vec[i : i + 1, ln]
            for c in range(nc):
                s = slice(c * C, (c + 1) * C)
                r, v, k = rr[s, ln], vr[s, ln], kr[s, ln]
                sg, logw, a, rn, kk, km = prelude(
                    k, wl[s, ln], al[s, ln], row(8), row(9), row(10), row(11), ones
                )
                units.append(
                    (r, -kk, kk * a, km, v, logw, stack2(xs[s, ln]), us[s, ln], stack2(zs[s, ln]),
                     hs[c, ln.start], k_do[t, s, ln])
                )
                where.append((s, ln))
                pre.append((sg, a, rn, kk, km))
        done = backward_chunks(units, tri, tri_up)
        for (s, ln), (sg, a, rn, kk, km), (dr, dp, dq, dk, dv, dlogw) in zip(where, pre, done):
            row = lambda i: vec[i : i + 1, ln]
            r, v, k = rr[s, ln], vr[s, ln], kr[s, ln]
            dy = k_dy[t, s, ln]
            dv = dv + headsum(r * km * row(12), ones) * dy
            ds = headsum(dy * v, ones) * row(12)
            dr = dr + ds * km
            dkm = dk + ds * r
            dkk = dq * a - dp
            da = dq * kk + dkm * k * row(11)
            dk = dkm * (1.0 + (a - 1.0) * row(11)) + row(10) * rn * (dkk - kk * headsum(dkk * kk, ones))
            drr[s, ln], dkr[s, ln], dvr[s, ln] = dr.astype(BF), dk.astype(BF), dv.astype(BF)
            dwl[s, ln] = (dlogw * (-DECAY_SCALE) * sg * (1.0 - sg)).astype(BF)
            dal[s, ln] = (da * a * (1.0 - a)).astype(BF)


TILE = 2 * PW


def cut(shape):
    lead = tuple(shape[:-1])
    return pl.BlockSpec(lead + (TILE,), lambda i, n=len(lead): (0,) * n + (i,))


def whole(shape):
    return pl.BlockSpec(tuple(shape), lambda i, n=len(shape): (0,) * n, pipeline_mode=pl.Buffered(1))


def result(shape):
    return pl.BlockSpec(tuple(shape), lambda i, n=len(shape): (0,) * n)


def in_turn(half, which):
    def spec(shape):
        lead = tuple(shape[:-1])
        place = {
            "first": lambda i: jnp.minimum(i, half - 1),
            "second": lambda i: jnp.maximum(i - half, 0),
            "both": lambda i: lax.rem(i, half),
        }[which]
        return pl.BlockSpec(lead + (TILE,), lambda i: (0,) * len(lead) + (place(i),))

    return spec


def tile_rows(shape):
    return pl.BlockSpec((TILE, shape[1]), lambda i: (i, 0))


def over_tiles(body, steps, ins, outs, name, scratch=(), **params):
    made = lambda spec, shape: spec if isinstance(spec, pl.BlockSpec) else spec(shape)
    return pl.pallas_call(
        body,
        grid=(steps,),
        in_specs=[made(spec, x.shape) for spec, x in ins],
        out_specs=[made(spec, x.shape) for spec, x in outs],
        out_shape=[x for _, x in outs],
        scratch_shapes=list(scratch),
        compiler_params=pltpu.CompilerParams(vmem_limit_bytes=60 * 1024 * 1024, **params),
        name=name,
    )(*[x for _, x in ins])


ORDERS = ("zxy", "zyx", "xzy", "yzx", "zxy", "yzx", "zyx")
DIRS = "xyuds"


def gather_events(order, z, x, y):
    other = {"x": lambda q: (q, 1 - x, y), "y": lambda q: (q, x, 1 - y), "z": lambda q: (q, x, y)}
    inside = lambda k: None if k == 0 else jnp.logical_and(z + k >= 0, z + k <= 3)
    if order[0] == "z":
        a, b = order[1], order[2]
        events = [(0, (z, x, y), None, None, [a, b, "u", "d", "s"])]
        for k in (1, 2, 3):
            events.append((k, (z - k, x, y), "u", z >= k, ["u", a, b, "s"]))
            events.append((k, (z + k, x, y), "d", z + k <= 3, ["d", a, b, "s"]))
        for k in range(-3, 4):
            events.append((abs(k) + 1, other[a](z + k), a, inside(k), [b, "s"]))
    else:
        a, b = order[0], order[2]
        events = [(0, (z, x, y), None, None, [a, "u", "d", b, "s"])]
        events.append((1, other[a](z), a, None, ["u", "d", b, "s"]))
        for k in (1, 2, 3):
            for late, at in ((0, other["z"]), (1, other[a])):
                events.append((k + late, at(z - k), "u", z >= k, ["u", b, "s"]))
                events.append((k + late, at(z + k), "d", z + k <= 3, ["d", b, "s"]))
    for k in range(-3, 4):
        events.append((abs(k) + 1, other[b](z + k), b, inside(k), ["s"]))
        events.append((abs(k) + 2, (z + k, 1 - x, 1 - y), b, inside(k), ["s"]))
    return events


def maybe(condition, run):
    if condition is None:
        run()
    else:
        pl.when(condition)(run)


class Gathering:
    def __init__(self, orders, steps, shards, whole, send, recv, near):
        self.shards, self.whole, self.send, self.recv, self.near = shards, whole, send, recv, near
        seq, dp = lax.axis_index("seq"), lax.axis_index("dp")
        z, x, y, self.c = seq // 2, seq % 2, dp // 2, dp % 2
        self.y, self.z = y, z
        self.to = {
            "x": (z * 2 + 1 - x, dp),
            "y": (seq, (1 - y) * 2 + self.c),
            "u": (seq + 2, dp),
            "d": (seq - 2, dp),
            "s": (seq, y * 2 + 1 - self.c),
        }
        self.exists = {"u": z < 3, "d": z > 0}
        todo = [
            (steps[t][i] if steps else e[0], t, e)
            for t, o in enumerate(orders)
            for i, e in enumerate(gather_events(o, z, x, y))
        ]
        todo.sort(key=lambda q: q[0])
        self.todo = todo
        self.times = sorted({q[0] for q in todo})

    def enter(self, beside=None, count=0):
        barrier = pltpu.get_barrier_semaphore()
        if beside is not None:
            pl.when(count == 1)(
                lambda: pl.semaphore_signal(barrier, inc=1, device_id=beside, device_id_type=MESH)
            )
        for k in DIRS:
            maybe(
                self.exists.get(k),
                lambda k=k: pl.semaphore_signal(
                    barrier, inc=1, device_id=self.to[k], device_id_type=MESH
                ),
            )
        pl.semaphore_wait(barrier, 3 + (self.z + 2) // 3 + (5 - self.z) // 3 + count)

    def chip(self, b):
        return b[0] * 4 + b[1] * 2 + b[2]

    def shard(self, t, k=None):
        ref = self.shards[t]
        if len(ref.shape) == 2:
            return ref
        return ref.at[1 - self.y if k == "y" else self.y]

    def copy(self, t, own, b, k):
        slot = self.whole[t].at[self.chip(b) * 2 + self.c]
        return pltpu.make_async_remote_copy(
            src_ref=self.shard(t, k) if own else slot,
            dst_ref=slot,
            send_sem=self.send.at[DIRS.index(k), t, self.chip(b)],
            recv_sem=self.recv.at[1 if k == "s" else 0, t, self.chip(b)],
            device_id=self.to[k],
            device_id_type=MESH,
        )

    def local(self, t, b):
        return pltpu.make_async_copy(
            self.shard(t), self.whole[t].at[self.chip(b) * 2 + self.c], self.near.at[t]
        )

    def goes(self, event):
        _, b, came, condition, ways = event
        for k in ways:
            both = self.exists.get(k) if condition is None else condition
            if condition is not None and k in self.exists:
                both = jnp.logical_and(condition, self.exists[k])
            yield b, came is None, k, both

    def take(self, time):
        for at, t, event in self.todo:
            if at != time:
                continue
            _, b, came, condition, _ = event
            if came is None:
                self.local(t, b).start()
            else:
                maybe(condition, lambda: self.copy(t, False, b, came).wait_recv())
            for _, own, k, both in self.goes(event):
                maybe(both, lambda: self.copy(t, own, b, k).start())

    def finish(self):
        for t in range(len(self.shards)):
            for i in range(16):
                pltpu.make_async_remote_copy(
                    src_ref=self.shard(t),
                    dst_ref=self.whole[t].at[i * 2 + 1 - self.c],
                    send_sem=self.send.at[4, t, i],
                    recv_sem=self.recv.at[1, t, i],
                    device_id=self.to["s"],
                    device_id_type=MESH,
                ).wait_recv()
        for _, t, event in self.todo:
            for b, own, k, both in self.goes(event):
                maybe(both, lambda: self.copy(t, own, b, k).wait_send())
            if event[2] is None:
                self.local(t, event[1]).wait()


def gather_scratch(n):
    return [
        pltpu.SemaphoreType.DMA((5, n, 16)),
        pltpu.SemaphoreType.DMA((2, n, 16)),
        pltpu.SemaphoreType.DMA((n,)),
    ]


def gather_kernel(orders, *refs):
    n = len(orders)
    g = Gathering(orders, None, refs[:n], refs[n : 2 * n], *refs[2 * n :])
    g.enter()
    for time in g.times:
        g.take(time)
    g.finish()


def own_gather():
    return (lax.axis_size("seq"), lax.axis_size("dp")) == (8, 4)


def gather(shards):
    if not own_gather():
        return [lax.all_gather(s, ("seq", "dp"), axis=0) for s in shards]
    n, devices = len(shards), 32
    made = pl.pallas_call(
        functools.partial(gather_kernel, ORDERS[:n]),
        out_shape=[jax.ShapeDtypeStruct((devices,) + s.shape[-2:], s.dtype) for s in shards],
        in_specs=[pl.BlockSpec(memory_space=pl.ANY)] * n,
        out_specs=[pl.BlockSpec(memory_space=pl.ANY)] * n,
        scratch_shapes=gather_scratch(n),
        compiler_params=pltpu.CompilerParams(collective_id=2, has_side_effects=True),
        name="gather_time",
    )(*shards)
    return list(made)


def sort_kernel(kinds, late, few, small, chosen, hidden, hidden_late, vec):
    half = kinds // 2
    base = (lax.axis_index("dp") % 2) * (half + 4 * RANK)
    rows = lambda o, at, n: few[o, pl.ds(pl.multiple_of(base + at, 16), n), :]
    left = iota((half, PW), 1) < D
    for p in range(few.shape[0] // 2):
        one, two = rows(2 * p, 0, half).astype(F32), rows(2 * p + 1, 0, half).astype(F32)
        at = slice(p * PW, (p + 1) * PW)
        chosen[:half, at] = jnp.where(left, one, pltpu.roll(two, D, axis=1)).astype(BF)
        chosen[half:, at] = jnp.where(left, pltpu.roll(one, D, axis=1), two).astype(BF)
    per = PW // late
    lane = iota((2 * RANK, PW), 1) // late
    for g in range(few.shape[0] // per):
        tail = None
        for j in range(per):
            o = g * per + j
            low, high = rows(o, half, 2 * RANK), rows(o, half + 2 * RANK, 2 * RANK)
            hidden[o, :, :PW], hidden[o, :, PW:] = low, high
            shift = (j + 1) * late % PW
            end = pltpu.roll(high.astype(F32), shift, axis=1) if shift else high.astype(F32)
            tail = end if tail is None else jnp.where(lane == j, end, tail)
        hidden_late[:, g * PW : (g + 1) * PW] = tail.astype(BF)
    vec[...] = small[...].astype(F32).T[D : D + vec.shape[0]]


def sort_small(kinds, late, nvec, few, misc):
    n, width = few.shape[0], misc.shape[0]
    shape = jax.ShapeDtypeStruct
    return over_tiles(
        functools.partial(sort_kernel, kinds, late), 1,
        [(whole, few), (pl.BlockSpec((width, PW), lambda i: (0, 7)), misc)],
        [
            (whole, shape((kinds, width), BF)),
            (whole, shape((n, 2 * RANK, 2 * PW), BF)),
            (whole, shape((2 * RANK, n * late), BF)),
            (whole, shape((nvec, width), F32)),
        ],
        "sort_small",
    )


UNITS = 512
EARLY_UNITS = 16
LATE_ORDERS = ("zxy", "yzx")
LATE_STEPS = (
    (0, 2, 2, 4, 4, 7, 7, 11, 9, 4, 2, 5, 9, 11, 9, 13, 7, 11, 4, 8, 2, 6, 5, 9, 7, 11, 9, 13),
    (0, 3, 3, 3, 5, 5, 6, 6, 8, 8, 9, 9, 11, 11, 13, 14, 13, 14, 7, 11, 3, 6, 8, 12, 13, 14, 13, 14),
)


def channel_kernel(
    late, n2, edge, norm, gy, middle, down_c, up_f, kv, hidden, *refs,
):
    if late:
        kv2, key_shard, value_shard, hidden_late, *refs = refs
    out, dmc, first, g_hidden, g_up_f, g_down_c, *refs = refs
    if late:
        g_late, d_edge, *refs = refs
    mc, mct, gyt, ffo, h_c, dh_f, acc_f, acc_c, *refs = refs
    step, last = pl.program_id(0), pl.num_programs(0) - 1
    per, ff = kv.shape[0], kv.shape[1] // 2
    blocks = [(kv, ff)]
    if late:
        blocks.append((kv2, kv2.shape[1] // 2))
        ff += kv2.shape[1] // 2
        key_late, value_late, mine, came, edge_sem, *sems = refs
        g = Gathering(LATE_ORDERS, LATE_STEPS, (key_shard, value_shard), (key_late, value_late), *sems)
        seq, dp = lax.axis_index("seq"), lax.axis_index("dp")
        x, z = seq % 2, seq // 2
        beside = seq + 2 * x - 1
        count = (1 - x) * ((z + 2) // 3) + x * ((5 - z) // 3)
        starts, ends = seq == 0, seq == 7

        def edges(i, to):
            return pltpu.make_async_remote_copy(
                src_ref=mine.at[i],
                dst_ref=came.at[i],
                send_sem=edge_sem.at[0, i],
                recv_sem=edge_sem.at[1, i],
                device_id=(to, dp),
                device_id_type=MESH,
            )

        def trade(i, has_from, has_to, shift):
            pl.when(has_to)(lambda: edges(i, seq + shift).start())
            pl.when(has_from)(lambda: edges(i, seq - shift).wait_recv())
            pl.when(has_to)(lambda: edges(i, seq + shift).wait_send())

        @pl.when(step == 0)
        def _():
            came[...] = jnp.zeros_like(came)
            g.enter((beside, dp), count)
            size = n2.shape[0]
            mine[0] = n2[size - 8 :, :]

        for time in g.times:

            @pl.when(step == time)
            def _():
                g.take(time)

        @pl.when(step == 0)
        def _():
            trade(0, jnp.logical_not(starts), jnp.logical_not(ends), 1)

    @pl.when(step == 0)
    def _():
        x = n2[...]
        row = came[0, 7:8, :] if late else edge[...]
        before = jnp.where(iota(x.shape, 0) == 0, row, pltpu.roll(x, 1, axis=0))
        m = x + (before - x) * norm[17:18, :]
        mc[...] = m.astype(BF)
        mct[...] = m.T.astype(BF)
        gyt[...] = gy[...].astype(F32).T.astype(BF)
        h_c[...] = mm_nt(down_c[...], mc[...]).astype(BF)
        dh_f[...] = (SCALE * mm_nt(up_f[...], gy[...])).astype(BF)
        acc_f[...] = jnp.zeros_like(acc_f)
        acc_c[...] = jnp.zeros_like(acc_c)
        ffo[...] = jnp.zeros_like(ffo)
        dmc[...] = jnp.zeros_like(dmc)

    def units(key, value, smalls):
        pre, dsq = mm(key, mct[...]), mm(value, gyt[...])
        rows = key.shape[0] // len(smalls)
        hqs, dps, grads = [], [], []
        for b, small in enumerate(smalls):
            s = slice(b * rows, (b + 1) * rows)
            down_f, up_c = small[:RANK], small[RANK:]
            active = jnp.maximum(pre[s] + SCALE * mm_tn(up_c, h_c[...]), 0.0)
            hq = (active * active).astype(BF)
            dpre = ((dsq[s] + mm_tn(down_f, dh_f[...])) * (2.0 * active)).astype(BF)
            grads.append((mm_nt(dh_f[...], hq), SCALE * mm_nt(h_c[...], dpre)))
            acc_f[...] += mm(down_f, hq)
            acc_c[...] += mm(up_c, dpre)
            hqs.append(hq)
            dps.append(dpre)
        ffo[...] += mm_tn(jnp.concatenate(hqs, 0), value)
        dmc[...] += mm_tn(jnp.concatenate(dps, 0), key)
        return grads

    @pl.when(step < last + (0 if late else 1))
    def _():
        key = jnp.concatenate([a[b, :h] for b in range(per) for a, h in blocks], 0)
        value = jnp.concatenate([a[b, h:] for b in range(per) for a, h in blocks], 0)
        grads = units(key, value, [hidden[b, :, :ff] for b in range(per)])
        for b, (low, high) in enumerate(grads):
            if late:
                g_hidden[b] = jnp.zeros(g_hidden.shape[1:], F32)
            g_hidden[b, :RANK, :ff], g_hidden[b, RANK:, :ff] = low, high

    @pl.when(step == last)
    def _():
        if late:
            g.finish()
            flat = lambda ref: ref[...].reshape(-1, ref.shape[-1])
            ((low, high),) = units(flat(key_late), flat(value_late), [hidden_late[...]])
            part = low.shape[1] // 8
            for p in range(8):
                at = slice(p * part, (p + 1) * part)
                g_late[p, :, :part], g_late[p, :, part:] = low[:, at], high[:, at]
        h_f = acc_f[...].astype(BF)
        out[...] = (middle[...] + ffo[...] + SCALE * mm_tn(h_f, up_f[...])).astype(BF)
        g_up_f[...] = SCALE * mm(h_f, gy[...])
        dh_c = (SCALE * acc_c[...]).astype(BF)
        d = dmc[...] + mm_tn(dh_c, down_c[...])
        dmc[...] = d
        first[...] = d[:8] * norm[17:18, :]
        if late:
            mine[1] = first[...]
            trade(1, jnp.logical_not(ends), jnp.logical_not(starts), -1)
            d_edge[...] = came[1]
        g_down_c[...] = mm(dh_c, mc[...])


def late_units(n_seq, n_dp, ff):
    return ff // 8 if (n_seq, n_dp) == (8, 4) and ff % 128 == 0 else 0


def channel(n2, edge, norm, gy, middle, down_c, up_f, kv, hidden, kv2, key_shard, value_shard, hidden_late):
    n, both, width = kv.shape
    ff, length, late = hidden.shape[2], n2.shape[0], key_shard.shape[0]
    per = max(1, min(n, UNITS // ff))
    steps = n // per
    block = lambda shape: pl.BlockSpec(
        (per,) + tuple(shape[1:]), lambda i: (jnp.minimum(i, steps - 1), 0, 0)
    )
    far = lambda shape: pl.BlockSpec(memory_space=pl.ANY)
    shape = jax.ShapeDtypeStruct
    rank = shape((RANK, width), F32)
    ins = [(whole, a) for a in (n2, edge, norm, gy, middle, down_c, up_f)] + [(block, kv), (block, hidden)]
    outs = [
        (result, shape((length, width), BF)),
        (result, shape((length, width), F32)),
        (result, shape((8, width), F32)),
        (block, shape((n, 2 * RANK, ff), F32)),
        (result, rank),
        (result, rank),
    ]
    scratch = [
        pltpu.VMEM((length, width), BF),
        pltpu.VMEM((width, length), BF),
        pltpu.VMEM((width, length), BF),
        pltpu.VMEM((length, width), F32),
        pltpu.VMEM((RANK, length), BF),
        pltpu.VMEM((RANK, length), BF),
        pltpu.VMEM((RANK, length), F32),
        pltpu.VMEM((RANK, length), F32),
    ]
    params = {}
    if late:
        ins += [(block, kv2), (far, key_shard), (far, value_shard), (whole, hidden_late)]
        outs += [(result, shape((8, RANK, 2 * n * late // 8), F32)), (result, shape((8, width), F32))]
        scratch += [pltpu.VMEM((n, late, width), BF)] * 2
        scratch += [pltpu.VMEM((2, 8, width), F32)] * 2 + [pltpu.SemaphoreType.DMA((2, 2))]
        scratch += gather_scratch(2)
        params = dict(collective_id=4, has_side_effects=True)
    return over_tiles(
        functools.partial(channel_kernel, late), steps + (1 if late else 0), ins, outs, "channel", scratch, **params
    )


HALF = 512


def branch_masks(shape):
    lane = iota(shape, 1)
    lo, hi = DECAY_INNER, DECAY_INNER + RATE_INNER
    return lane < lo, (lane >= lo) & (lane < hi), (lane >= hi) & (lane < hi + GATE_INNER)


def project_kernel(
    hat, edge, valid, vec, first, chosen, second, w_r, w_k, w_v, up,
    rr, kr, vr, wl, al, gg, m_r, m_k, m_v, hs, act, act_low,
):
    @pl.when(pl.program_id(0) == 0)
    def _():
        n1 = hat[...] * vec[0:1, :] + vec[1:2, :]
        before = jnp.where(iota(hat.shape, 0) == 0, edge[...], pltpu.roll(hat[...], 1, axis=0))
        change = (before * vec[0:1, :] + vec[1:2, :]) * valid[...] - n1
        mixed = lambda i: (n1 + change * vec[2 + i : 3 + i, :]).astype(BF)
        m_r[...], m_k[...], m_v[...] = mixed(0), mixed(2), mixed(3)
        for i, m in enumerate((m_r, m_k, m_v)):
            hs[i] = mm_nt(m[...], chosen[i * RANK : (i + 1) * RANK, :]).astype(BF)
        t_w = mm(mixed(1), first[...])
        t_a = mm(mixed(4), first[...])
        t_g = mm(mixed(5), first[...])
        is_w, is_a, is_g = branch_masks(t_w.shape)
        zero = jnp.zeros_like(t_w)
        t_w = jnp.where(is_w, jnp.tanh(t_w), zero)
        t_a = jnp.where(is_a, t_a, zero)
        t_g = jnp.where(is_g, jax.nn.sigmoid(t_g), zero)
        act[...] = t_w + t_a + t_g
        act_low[0], act_low[1], act_low[2] = t_w.astype(BF), t_a.astype(BF), t_g.astype(BF)

    for i, (m, w, out) in enumerate(((m_r, w_r, rr), (m_k, w_k, kr), (m_v, w_v, vr))):
        out[...] = mm_nt(m[...], w[...]) + SCALE * mm(hs[i], up[(5 + i) * RANK : (6 + i) * RANK, :])
    for i, out in enumerate((wl, al, gg)):
        out[...] = mm_nt(act_low[i], second[...])


def final_kernel(
    n, fast, drr, dkr, dvr, dwl, dal, dgg, m_r, m_k, m_v, hs, act, chosen, second, down_o, up_o, hat, rstd, d_mid, vecs,
    w_r, w_k, w_v, down, first, vec, *refs,
):
    step, last = pl.program_id(0), pl.num_programs(0) - 1
    me, dp = lax.axis_index("seq"), lax.axis_index("dp")
    if fast:
        early, picks, grad, g_model, g_hidden, *refs = refs
        stage_m, stage_h, from_m, from_h, own_send, own_recv, *refs = refs
    else:
        grad, summed, *refs = refs
    stay, go, dhs, d_act, parts, here, came, send_sem, recv_sem, edge_sem = refs

    def to_owner(k, i):
        peer = lax.rem(dp + k, 4)
        stage, slots = ((stage_m, from_m), (stage_h, from_h))[i]
        return pltpu.make_async_remote_copy(
            src_ref=stage.at[peer],
            dst_ref=slots.at[k - 1],
            send_sem=own_send.at[i, k - 1],
            recv_sem=own_recv.at[i, k - 1],
            device_id=(me, peer),
            device_id_type=MESH,
        )

    def copy(k):
        peer = lax.rem(me + k, n)
        return pltpu.make_async_remote_copy(
            src_ref=parts.at[peer],
            dst_ref=here.at[k - 1],
            send_sem=send_sem.at[k - 1],
            recv_sem=recv_sem.at[k - 1],
            device_id=(peer, dp),
            device_id_type=MESH,
        )

    def edge(to):
        return pltpu.make_async_remote_copy(
            src_ref=go.at[0:8],
            dst_ref=came,
            send_sem=edge_sem.at[0],
            recv_sem=edge_sem.at[1],
            device_id=(to, dp),
            device_id_type=MESH,
        )

    @pl.when(step == 0)
    def _():
        came[...] = jnp.zeros_like(came)
        barrier = pltpu.get_barrier_semaphore()
        for k in range(1, n):
            pl.semaphore_signal(
                barrier, inc=1, device_id=(lax.rem(me + k, n), dp), device_id_type=MESH
            )
        if fast:
            for k in range(1, 4):
                pl.semaphore_signal(
                    barrier, inc=1, device_id=(me, lax.rem(dp + k, 4)), device_id_type=MESH
                )
        rows = [None] * 6 + [down_o[...], up_o[...]]
        for i, (d, m) in enumerate(((drr, m_r), (dkr, m_k), (dvr, m_v))):
            dh = (SCALE * mm_nt(d[...], chosen[(5 + i) * RANK : (6 + i) * RANK, :])).astype(BF)
            dhs[i] = dh
            rows[i], rows[3 + i] = mm_tn(dh, m[...]), SCALE * mm_tn(hs[i], d[...])
        wide = parts.shape[2]
        for i, r in enumerate(rows):
            for p in range(n):
                parts[p, i * RANK : (i + 1) * RANK, :] = r[:, p * wide : (p + 1) * wide].astype(BF)
        pl.semaphore_wait(barrier, n - 1 + (3 if fast else 0))
        for k in range(1, n):
            copy(k).start()
        is_w, is_a, is_g = branch_masks(act.shape)
        a = act[...]
        zero = jnp.zeros_like(a)
        d_act[0] = jnp.where(is_w, mm(dwl[...], second[...]) * (1.0 - a * a), zero).astype(BF)
        d_act[1] = jnp.where(is_a, mm(dal[...], second[...]), zero).astype(BF)
        d_act[2] = jnp.where(is_g, mm(dgg[...], second[...]) * a * (1.0 - a), zero).astype(BF)

    total, moved = None, None
    for i, (d, w, at) in enumerate(((drr, w_r, 2), (dkr, w_k, 4), (dvr, w_v, 5))):
        g = mm(d[...], w[...]) + mm(dhs[i], down[i * RANK : (i + 1) * RANK, :])
        move = g * vec[at : at + 1, :]
        total, moved = (g, move) if total is None else (total + g, moved + move)
    for i, at in enumerate((3, 6, 7)):
        g = mm_nt(d_act[i], first[...])
        total, moved = total + g, moved + g * vec[at : at + 1, :]
    tile = pl.ds(pl.multiple_of(step * TILE, TILE), TILE)
    stay[:, tile] = total - moved
    go[:, tile] = moved

    @pl.when(step == last)
    def _():
        pl.when(me > 0)(lambda: edge(me - 1).start())
        for k in range(1, n):
            copy(k).wait()
        t = parts[me].astype(F32)
        for k in range(1, n):
            t = t + here[k - 1].astype(F32)
        if fast:
            e = early[...]
            r = lambda x, i, k: x[i * RANK : (i + k) * RANK]
            rows = jnp.concatenate(
                [r(t, 0, 3), r(t, 6, 1), r(e, 0, 1), r(t, 3, 3), r(t, 7, 1), r(e, 1, 1)], 0
            )
            tails = e[10 * RANK : 11 * RANK]
            lane = iota((2 * RANK, PW), 1)
            for j in range(4):
                two = rows[:, (j // 2) * PW : (j // 2 + 1) * PW]
                stage_m[j] = pltpu.roll(two, D, axis=1) if j % 2 else two
                mine = e[(2 + 2 * j) * RANK : (4 + 2 * j) * RANK]
                tail = jnp.concatenate([tails[:, :PW], tails[:, PW:]], 0)
                shift = (3 - j) * (PW // 4)
                tail = pltpu.roll(tail, shift, axis=1) if shift else tail
                stage_h[j, :, :PW] = mine[:, :PW]
                stage_h[j, :, PW:] = jnp.where(lane >= 3 * PW // 4, tail, mine[:, PW:])
            for k in range(1, 4):
                to_owner(k, 0).start()
                to_owner(k, 1).start()
        else:
            summed[...] = t
        pl.when(me < n - 1)(lambda: edge(me + 1).wait_recv())
        size = go.shape[0]
        g = pltpu.roll(go[...], size - 1, axis=0)
        g = stay[...] + jnp.where(iota(g.shape, 0) == size - 1, came[0:1, :], g)
        dhat = g * vecs[0:1, :]
        grad[...] = d_mid[...] + rstd[...] * (
            dhat
            - jnp.mean(dhat, axis=-1, keepdims=True)
            - hat[...] * jnp.mean(dhat * hat[...], axis=-1, keepdims=True)
        )
        pl.when(me > 0)(lambda: edge(me - 1).wait_send())
        if fast:
            for k in range(1, 4):
                to_owner(k, 0).wait()
                to_owner(k, 1).wait()
            found = [(dp, stage_m[dp], stage_h[dp])]
            found += [(lax.rem(dp + 4 - k, 4), from_m[k - 1], from_h[k - 1]) for k in range(1, 4)]
            adapters = g_model.shape[0]
            weights = [picks[pl.ds(pl.multiple_of(q * adapters, 8), adapters), :] for q, _, _ in found]
            for a in range(adapters):
                m, h = None, None
                for w, (_, x, y) in zip(weights, found):
                    w = w[a : a + 1, :]
                    x, y = x * w, y * jnp.concatenate([w, w], 1)
                    m, h = (x, y) if m is None else (m + x, h + y)
                g_model[a], g_hidden[a] = m[:, :D], h


def shifted(block, axis, distance):
    devices = range(lax.axis_size(axis))
    route = [(i - distance, i) for i in devices if i - distance in devices]
    return lax.ppermute(block, axis, route)


def mm(a, b):
    return lax.dot_general(a, b, DIMS["nn"], preferred_element_type=F32)


def mm_nt(a, b):
    return lax.dot_general(a, b, DIMS["nt"], preferred_element_type=F32)


def mm_tn(a, b):
    return lax.dot_general(a, b, DIMS["tn"], preferred_element_type=F32)


def body(tokens, output_gradient, index, proj, first, second, vectors, ckey, cvalue, model_rows, hidden_rows):
    axes = ("seq", "dp")
    n_seq, n_dp = lax.axis_size("seq"), lax.axis_size("dp")
    n = n_seq * n_dp
    tokens, gy = tokens[0], output_gradient[0]
    length, width = tokens.shape
    nc, tiles = length // C, width // TILE
    adapters, kinds, cols = model_rows.shape
    ff, inner, nvec = ckey.shape[1], first.shape[1], vectors.shape[0]

    key_shard, soon = ckey.T, ff - late_units(n_seq, n_dp, ff)
    most = soon - EARLY_UNITS if soon < ff else soon
    kv = lax.all_gather(jnp.concatenate([key_shard[:most], cvalue[:most]], 0), axes, axis=0)

    index_all = lax.all_gather(index, "dp", axis=0, tiled=True)
    pick = index_all[:, None] == jnp.arange(adapters, dtype=jnp.int32)[None, :]
    pick_low = pick.astype(BF)
    fast = own_gather() and (cols, ff, 2 * inner + nvec) == (D, 2 * PW, 914)
    if fast:
        half = kinds // 2
        few = jnp.concatenate(
            [
                jnp.concatenate([model_rows[:, :half], model_rows[:, half:]], 2),
                hidden_rows[:, :, :PW],
                hidden_rows[:, :, PW:],
            ],
            1,
        )
    else:
        few = jnp.concatenate([model_rows.reshape(adapters, -1), hidden_rows.reshape(adapters, -1)], 1)
        few = few.reshape(adapters, -1, 128)
    few = jnp.einsum("sa,arx->srx", pick_low, few, preferred_element_type=F32).astype(BF)
    pad = lambda k: jnp.zeros((cols, k), BF)
    misc = jnp.concatenate(
        [first, pad(HALF - inner), second.T, vectors.T, pad(HALF - inner - nvec)], axis=1
    )
    turned = jnp.swapaxes(proj, 1, 2)

    few = few.reshape((2, -1, 128) if fast else (-1, 128))
    more = [jnp.concatenate([key_shard[most:soon], cvalue[most:soon]], 0)] if most < soon else []
    *mats, misc, few_all, kv2 = gather([turned[0], turned[1], turned[2], turned[3], misc, few] + more) + [None] * (
        most == soon
    )
    mats[0], tokens = lax.optimization_barrier((mats[0], tokens))
    wide = tokens.astype(F32)
    ahead = shifted(tokens[-1:], "seq", 1).astype(F32)
    def normal(rows):
        centre = rows - jnp.mean(rows, axis=-1, keepdims=True)
        rstd = lax.rsqrt(jnp.mean(centre * centre, axis=-1, keepdims=True) + NORM_EPS)
        return centre * rstd, rstd

    hat, rstd = normal(wide)
    row, _ = normal(ahead)
    start = (jnp.arange(length)[:, None] == 0) & (lax.axis_index("seq") == 0)
    valid = jnp.where(start, 0.0, 1.0).astype(F32)

    mats = [m.reshape(width, width) for m in mats]
    misc = misc.reshape(width, -1)
    if fast:
        chosen, hidden, hidden_late, vec = sort_small(kinds, ff - soon, nvec, few_all, misc)
    else:
        vec = misc[:, HALF + inner : HALF + inner + nvec].T.astype(F32)
        own = lax.dynamic_index_in_dim(few_all.reshape(n, n_dp, -1, 128), lax.axis_index("dp"), 1, False)
        own = own.reshape(n, -1)
        chosen = own[:, : kinds * cols].reshape(n, kinds, cols).transpose(1, 0, 2).reshape(kinds, width)
        hidden, hidden_late = own[:, kinds * cols :].reshape(n, 2 * RANK, ff), None
    down = lambda i: chosen[i * RANK : (i + 1) * RANK]
    up = lambda i: chosen[(5 + i) * RANK : (6 + i) * RANK]

    shape = jax.ShapeDtypeStruct
    full, low = shape((length, width), F32), shape((length, width), BF)
    small, rank = shape((D, width), F32), shape((RANK, width), F32)
    firsts = pl.BlockSpec((width, HALF), lambda i: (0, 0))
    seconds = pl.BlockSpec((width, HALF), lambda i: (0, 1))
    first_rows = pl.BlockSpec((TILE, HALF), lambda i: (i, 0))
    second_rows = pl.BlockSpec((TILE, HALF), lambda i: (i, 1))
    rr, kr, vr, wl, al, gg, m_r, m_k, m_v, hs, act = over_tiles(
        project_kernel, tiles,
        [
            (whole, hat), (whole, row), (whole, valid), (whole, vec), (firsts, misc), (whole, chosen),
            (second_rows, misc), (tile_rows, mats[0]), (tile_rows, mats[1]), (tile_rows, mats[2]), (cut, chosen),
        ],
        [(cut, full)] * 6
        + [(result, low)] * 3
        + [(result, shape((3, length, RANK), BF)), (result, shape((length, HALF), F32))],
        "project",
        [pltpu.VMEM((3, length, HALF), BF)],
    )
    one, two, each = in_turn(tiles, "first"), in_turn(tiles, "second"), in_turn(tiles, "both")
    keep = pltpu.VMEM((tiles, length, TILE), F32)
    keep_small = pltpu.VMEM((tiles, D, TILE), F32)
    reff, xs, mt, turned, gated, o, us, zs, middle, n2, h_o = over_tiles(
        functools.partial(rec_forward, nc, n_seq, tiles), 2 * tiles,
        [
            (each, rr), (each, kr), (each, vr), (one, wl), (each, al), (two, gg), (each, vec),
            (whole, tokens), (two, mats[3]), (two, down(3)), (whole, up(3)), (whole, vec),
        ],
        [(one, full), (one, full), (one, full), (one, small), (two, low), (two, full), (two, full), (two, full)]
        + [(result, full), (result, full), (result, shape((length, RANK), BF))],
        "rec_forward",
        [keep] * 6 + [keep_small] * 2 + [pltpu.VMEM((length, RANK), F32)] + hand_scratch(tiles),
        collective_id=0, has_side_effects=True,
    )
    soon_only = soon == ff
    row = shifted(n2[-1:], "seq", 1) if soon_only else n2[-1:]
    out, d_mc, moved, g_hidden, up_f, down_c, *more = channel(
        n2, row, vec, gy, middle, down(4), up(4), kv, hidden,
        kv2, key_shard[soon:], cvalue[soon:], hidden_late,
    )
    wide = n_dp * cols
    by_piece = lambda rows: jnp.swapaxes(rows.reshape(-1, n_seq, wide), 0, 1)
    parts = [by_piece(jnp.concatenate([down_c, up_f], 0)), g_hidden.reshape(n_seq, -1, wide)]
    if soon_only:
        edge = jnp.broadcast_to(shifted(moved[:1], "seq", -1), (8, width))
    else:
        g_late, edge = more
        parts.append(g_late)
    early, edge = lax.optimization_barrier((jnp.concatenate(parts, 1), edge))
    early = lax.psum_scatter(early, "seq", scatter_dimension=0, tiled=True)[0]
    d_mid, dgg, down_o, up_o, drr, dkr, dvr, dwl, dal = over_tiles(
        functools.partial(rec_backward, nc, n_seq, tiles), 2 * tiles,
        [
            (whole, d_mc), (whole, edge), (whole, gy), (whole, middle), (whole, vec), (one, mats[3]),
            (one, down(3)), (whole, up(3)), (whole, h_o), (one, gated), (one, gg), (one, o),
            (each, rr), (each, kr), (each, vr), (two, wl), (each, al), (each, vec),
            (one, reff), (each, mt), (one, turned), (two, xs), (two, us), (two, zs),
        ],
        [(result, full), (one, low), (one, rank), (result, rank)] + [(two, low)] * 5,
        "rec_backward",
        [pltpu.VMEM((length, width), BF), pltpu.VMEM((length, RANK), BF)]
        + [keep] * 3 + [keep_small] * 2 + hand_scratch(tiles),
        collective_id=1, has_side_effects=True,
    )
    early, drr = lax.optimization_barrier((early, drr))
    ins = [(whole, a) for a in (drr, dkr, dvr, dwl, dal, dgg, m_r, m_k, m_v, hs, act, chosen)]
    ins += [(pl.BlockSpec((width, HALF), lambda i: (0, 1), pipeline_mode=pl.Buffered(1)), misc)]
    ins += [(whole, a) for a in (down_o, up_o, hat, rstd, d_mid, vec)]
    ins += [(cut, mats[0]), (cut, mats[1]), (cut, mats[2]), (cut, chosen), (first_rows, misc), (cut, vec)]
    scratch = [
        pltpu.VMEM((length, width), F32),
        pltpu.VMEM((length, width), F32),
        pltpu.VMEM((3, length, RANK), BF),
        pltpu.VMEM((3, length, HALF), BF),
        pltpu.VMEM((n_seq, 8 * RANK, wide), BF),
        pltpu.VMEM((n_seq - 1, 8 * RANK, wide), BF),
        pltpu.VMEM((8, width), F32),
        pltpu.SemaphoreType.DMA((n_seq - 1,)),
        pltpu.SemaphoreType.DMA((n_seq - 1,)),
        pltpu.SemaphoreType.DMA((2,)),
    ]
    ready = fast and adapters == 8 and not soon_only
    call = lambda ins, outs, scratch: over_tiles(
        functools.partial(final_kernel, n_seq, ready), tiles, ins, [(result, full)] + outs, "final", scratch,
        collective_id=3, has_side_effects=True,
    )
    if ready:
        picks = jnp.broadcast_to(pick.astype(F32).reshape(-1, 1), (n_dp * adapters, PW))
        grad_tokens, grad_model, h = call(
            ins + [(whole, early), (whole, picks)],
            [(result, shape((adapters, kinds, cols), F32)), (result, shape((adapters, 2 * RANK, ff), F32))],
            [pltpu.VMEM((4, kinds, PW), F32), pltpu.VMEM((4, 2 * RANK, ff), F32)]
            + [pltpu.VMEM((3, kinds, PW), F32), pltpu.VMEM((3, 2 * RANK, ff), F32)]
            + [pltpu.SemaphoreType.DMA((2, 3))] * 2
            + scratch,
        )
        return out[None], grad_tokens[None], grad_model, h
    grad_tokens, late = call(ins, [(result, shape((8 * RANK, wide), F32))], scratch)
    mine = early[2 * RANK : 2 * RANK + 2 * RANK * ff // cols].reshape(n_dp, 2 * RANK, ff)
    if not soon_only:
        tail = early[2 * RANK + 2 * RANK * ff // cols :].reshape(RANK, 2, n_dp, ff - soon)
        tail = tail.transpose(2, 1, 0, 3).reshape(n_dp, 2 * RANK, ff - soon)
        mine = jnp.concatenate([mine[:, :, :soon], tail], 2)
    columns = jnp.concatenate([early[: 2 * RANK], late], 0).reshape(10 * RANK, n_dp, cols)
    both = jnp.concatenate(
        [jnp.swapaxes(columns, 0, 1).reshape(n_dp, -1), mine.reshape(n_dp, -1)], 1
    )
    both = lax.all_to_all(both, "dp", split_axis=0, concat_axis=0, tiled=True)
    both = jnp.einsum("sa,sx->ax", pick.astype(F32), both, precision=PRECISE)
    at = 10 * RANK * cols
    a = both[:, :at].reshape(adapters, 10 * RANK, cols)
    h = both[:, at:].reshape(adapters, 2 * RANK, ff)
    block = lambda i, k: a[:, i * RANK : (i + k) * RANK]
    grad_model = jnp.concatenate(
        [block(2, 3), block(8, 1), block(0, 1), block(5, 3), block(9, 1), block(1, 1)], axis=1
    )
    return out[None], grad_tokens[None], grad_model, h


def solution(mesh):
    cols = P(None, ("seq", "dp"))
    rows = P(("seq", "dp"), None)
    deep = P(None, None, ("seq", "dp"))
    act = P("dp", "seq", None)
    return jax.shard_map(
        body,
        mesh=mesh,
        in_specs=(act, act, P("dp"), deep, rows, cols, cols, cols, rows, deep, deep),
        out_specs=(act, act, deep, deep),
        check_vma=False,
    )
```
